512 devices in a mesh: ctx: 64 (over z, x), head: 8 (over y, core).
Axes of the slice: x: 4, y: 4, z: 16, core: 2. Of those that a mesh axis runs over, the one named last changes fastest.
Arguments:
- tokens: bfloat16 [32768, 2048], P('ctx', 'head'), may hold values from -400 to 400
- gain: float32 [2048], replicated, may hold values from 0.1 to 1.9
- w_feat: bfloat16 [2048, 256], P(None, 'head'), may hold values from -0.125 to 0.125
- w_value: bfloat16 [2048, 2048], P(None, 'head'), may hold values from -0.125 to 0.125
- w_window: bfloat16 [2048, 2048], P(None, 'head'), may hold values from -0.6960582 to 0.6960582
- w_out: bfloat16 [2048, 2048], P('head'), may hold values from -0.1875 to 0.1875
Outputs:
- layer_out: bfloat16 [32768, 2048], P('ctx', 'head')
The draws below stay inside these ranges and needn't reach their ends.
All inputs are finite; a program needn't handle non-finite values.
Results may differ from the reference program's by a relative error of at most 0.02.
Values may be sent and summed in bfloat16 or wider, within the bound.
No kernel may reach another device: no remote copies, remote signals or barrier semaphores. Data moves between devices by JAX's collectives and lax.ppermute only.
A program may use at most 64 MiB of HBM per device.

```python
import math
import jax
import jax.numpy as jnp
from jax import lax

D = 2048
HD = 128
FEAT = 16
WINDOW = 512
TOK_DEV = 512
PHI = 273
HEADS = 16
TOKENS = 32768
N_CTX = 64
N_HEAD = 8


def draw_tokens(key, part):
    first = jax.random.fold_in(key, 0)
    normal_part = jnp.clip(jax.random.normal(first, (TOKENS, D), jnp.float32), -4.0, 4.0)
    return normal_part.astype(jnp.bfloat16)


def draw_w_window(key, part):
    head_count = HEADS // 2
    first, second = jax.random.split(jax.random.fold_in(key, 11), 2)
    query_part = jnp.clip(jax.random.normal(first, (D, head_count, HD), jnp.float32), -5.0, 5.0)
    key_part = jnp.clip(jax.random.normal(second, (D, head_count, HD), jnp.float32), -5.0, 5.0)
    queries = 1.4 * query_part / math.sqrt(D)
    keys_made = 1.4 * key_part / math.sqrt(D)
    return jnp.stack([queries, keys_made], axis=2).reshape(D, head_count * 2 * HD).astype(jnp.bfloat16)


def raised(drawn, rng, source, target, parts, factor):
    def block_of(dim):
        return (jnp.arange(drawn.shape[dim]) // (drawn.shape[dim] // parts)).reshape((-1,) + (1,) * (drawn.ndim - 1 - dim))

    first = jax.random.permutation(rng, parts)[block_of(target)]
    second = (block_of(target) + parts // 2) % parts
    return jnp.where((block_of(source) == first) | (block_of(source) == second), factor * drawn, drawn)


def levels(key, dims, pieces, low, top_value):
    factor_of = 1.0
    for dim, parts in pieces:
        heights = jax.random.uniform(jax.random.fold_in(jax.random.fold_in(key, 6), dim), (parts,), jnp.float32, low / len(pieces), top_value / len(pieces))
        factor_of = factor_of * jnp.repeat(jnp.exp(heights), dims[dim] // parts).reshape((-1,) + (1,) * (len(dims) - 1 - dim))
    return factor_of


def bell_draw(own_key, dims, scale, most, pieces=(), kind=jnp.bfloat16):
    array = scale * jax.random.normal(own_key, dims, jnp.float32)
    if pieces:
        array = array * levels(own_key, dims, pieces, -0.22, 0.18)
    return jnp.clip(array, -most, most).astype(kind)


def noise_with(stream_key, extent, width, most, shards, heavy, kind=jnp.bfloat16):
    array = width * jax.random.normal(stream_key, extent, jnp.float32)
    if shards:
        array = array * levels(stream_key, extent, shards, -0.22, 0.18)
    return jnp.clip(raised(array, jax.random.fold_in(stream_key, 3), *heavy), -most, most).astype(kind)


def setup_inputs(seed: int = 0) -> dict:
    key_list = jax.random.split(jax.random.key(seed), 7)
    tokens = draw_tokens(jax.random.fold_in(key_list[6], 71), 0)
    gain = jnp.clip(1.0 + 0.18 * jax.random.normal(key_list[1], (D,), jnp.float32), 0.1, 1.9)
    w_feat = bell_draw(key_list[2], (D, N_HEAD * 2 * FEAT), D ** -0.5, 0.125, ((1, 8),))
    w_value = bell_draw(key_list[3], (D, N_HEAD * 2 * HD), D ** -0.5, 0.125, ((1, 8),))
    w_window = draw_w_window(jax.random.fold_in(key_list[6], 71), 0)
    w_out = noise_with(key_list[5], (N_HEAD * 2 * HD, D), (N_HEAD * 2 * HD) ** -0.5, 0.1875, ((0, 8),), (0, 1, 8, 2.0))
    return dict(tokens=tokens, gain=gain, w_feat=w_feat, w_value=w_value, w_window=w_window, w_out=w_out)


epsilon = 1e-05

def taylor(rows_in):
    widened = rows_in.astype(jnp.float32)
    count = widened.shape[0]
    width_in = widened.shape[1]
    outer = (widened[:, :, None] * widened[:, None, :]).reshape(count, width_in * width_in) / (4.0 * math.sqrt(2.0))
    return jnp.concatenate([jnp.ones((count, 1), jnp.float32), widened / 2.0, outer], axis=1).astype(jnp.bfloat16)

def state_of(k_lin, v_lin):
    return jnp.dot(taylor(k_lin).T, v_lin, preferred_element_type=jnp.float32)

def linear_part(q_lin, k_lin, v_lin, prefix):
    count = q_lin.shape[0]
    inner = jnp.dot(q_lin, k_lin.T, preferred_element_type=jnp.float32)
    series = 1.0 + inner / 4.0 + inner * inner / 32.0
    rows_at = jnp.arange(count, dtype=jnp.int32)
    causal = rows_at[:, None] >= rows_at[None, :]
    weights = jnp.where(causal, series, 0.0).astype(jnp.bfloat16)
    numerator = jnp.dot(weights, v_lin, preferred_element_type=jnp.float32)
    numerator = numerator + jnp.dot(taylor(q_lin), prefix.astype(jnp.bfloat16), preferred_element_type=jnp.float32)
    scale = lax.rsqrt(lax.optimization_barrier(jnp.mean(numerator * numerator, axis=1, keepdims=True)) + epsilon)
    return (numerator * scale).astype(jnp.bfloat16)

def window_part(q_win, k_win, v_win, prev_keys, prev_values, offset):
    count = q_win.shape[0]
    span = prev_keys.shape[0]
    key_rows = jnp.concatenate([prev_keys, k_win], axis=0)
    value_rows = jnp.concatenate([prev_values, v_win], axis=0)
    query_pos = offset + jnp.arange(count, dtype=jnp.int32)
    key_pos = offset - span + jnp.arange(span + count, dtype=jnp.int32)
    distance = query_pos[:, None] - key_pos[None, :]
    allowed = (key_pos[None, :] >= 0) & (distance >= 0) & (distance < span)
    scores = jnp.dot(q_win, key_rows.T, preferred_element_type=jnp.float32) / math.sqrt(q_win.shape[1])
    scores = jnp.where(allowed, scores, -1e+30)
    highest = lax.optimization_barrier(jnp.max(scores, axis=1, keepdims=True))
    lifted = jnp.exp(scores - highest)
    probs = (lifted / lax.optimization_barrier(jnp.sum(lifted, axis=1, keepdims=True))).astype(jnp.bfloat16)
    return jnp.dot(probs, value_rows, preferred_element_type=jnp.float32).astype(jnp.bfloat16)

def reference(tokens, gain, w_feat, w_value, w_window, w_out):
    widened = tokens.astype(jnp.float32)
    normed = (widened * lax.rsqrt(lax.optimization_barrier(jnp.mean(widened * widened, axis=1, keepdims=True)) + epsilon) * gain).astype(jnp.bfloat16)
    head_count = HEADS // 2
    features = jnp.dot(normed, w_feat, preferred_element_type=jnp.float32).astype(jnp.bfloat16)
    features = features.reshape(N_CTX, TOK_DEV, head_count, 2, FEAT).transpose(0, 2, 3, 1, 4)
    values = jnp.dot(normed, w_value, preferred_element_type=jnp.float32).astype(jnp.bfloat16)
    values = values.reshape(N_CTX, TOK_DEV, head_count, 2, HD).transpose(0, 2, 3, 1, 4)
    windowed = jnp.dot(normed, w_window, preferred_element_type=jnp.float32).astype(jnp.bfloat16)
    windowed = windowed.reshape(N_CTX, TOK_DEV, head_count, 2, HD).transpose(0, 2, 3, 1, 4)

    def advance(carry, inputs):
        prefix, prev_keys, prev_values = carry
        feat_block, value_block, window_block, block_index = inputs
        offset = block_index * TOK_DEV
        own_state = jax.vmap(state_of)(feat_block[:, 1], value_block[:, 0])
        lin_out = jax.vmap(linear_part)(feat_block[:, 0], feat_block[:, 1], value_block[:, 0], prefix)
        win_out = jax.vmap(window_part, in_axes=(0, 0, 0, 0, 0, None))(window_block[:, 0], window_block[:, 1], value_block[:, 1], prev_keys, prev_values, offset)
        mixture = jnp.concatenate([lin_out, win_out], axis=2)
        next_carry = (prefix + own_state, window_block[:, 1, TOK_DEV - WINDOW:], value_block[:, 1, TOK_DEV - WINDOW:])
        return (next_carry, mixture)
    start_carry = (jnp.zeros((head_count, PHI, HD), jnp.float32), jnp.zeros((head_count, WINDOW, HD), jnp.bfloat16), jnp.zeros((head_count, WINDOW, HD), jnp.bfloat16))
    final_carry, mixed = lax.scan(advance, start_carry, (features, values, windowed, jnp.arange(N_CTX, dtype=jnp.int32)))
    mixed = mixed.transpose(0, 2, 1, 3).reshape(TOKENS, head_count * 2 * HD)
    return jnp.dot(mixed, w_out, preferred_element_type=jnp.float32).astype(jnp.bfloat16)
```

```python
import functools
import math

import jax
import jax.numpy as jnp
from jax import lax
from jax.experimental import pallas as pl
from jax.experimental.pallas import tpu as pltpu
from jax.sharding import PartitionSpec as P

EPS = 1e-05
FEAT = 16
ROWS = 160
BF = jnp.bfloat16
F32 = jnp.float32
VMEM = 56 * 1024 * 1024


def call(kernel, outs, scratch=()):
    return pl.pallas_call(
        kernel,
        out_shape=outs,
        scratch_shapes=scratch,
        compiler_params=pltpu.CompilerParams(vmem_limit_bytes=VMEM),
    )


def call_with_scalar(kernel, outs, count):
    return pl.pallas_call(
        kernel,
        out_shape=outs,
        in_specs=[pl.BlockSpec(memory_space=pltpu.SMEM)]
        + [pl.BlockSpec(memory_space=pltpu.VMEM)] * count,
        compiler_params=pltpu.CompilerParams(vmem_limit_bytes=VMEM),
    )


def pick(shape, axis):
    r = lax.broadcasted_iota(jnp.int32, shape, axis)
    u = lax.broadcasted_iota(jnp.int32, shape, 1 - axis)
    first = (r >= 1) & (r <= FEAT) & (u == r - 1)
    second = jnp.zeros(shape, jnp.bool_)
    base = 1 + FEAT
    for i in range(FEAT):
        width = FEAT - i
        inside = (r >= base) & (r < base + width)
        first = first | (inside & (u == i))
        second = second | (inside & (u == i + r - base))
        base += width
    return first.astype(F32).astype(BF), second.astype(F32).astype(BF)


def weights_of(shape, axis, twice):
    r = lax.broadcasted_iota(jnp.int32, shape, axis)
    scale = jnp.where(r == 0, 1.0, jnp.where(r <= FEAT, 0.5, 1.0 / (4.0 * math.sqrt(2.0))))
    if twice:
        base = 1 + FEAT
        square = jnp.zeros(shape, jnp.bool_)
        for i in range(FEAT):
            square = square | (r == base)
            base += FEAT - i
        scale = jnp.where((r > FEAT) & ~square, 2.0 * scale, scale)
    one_first = jnp.where(r == 0, 1.0, 0.0)
    one_second = jnp.where(r <= FEAT, 1.0, 0.0)
    return scale, one_first, one_second


NT = (((1,), (1,)), ((), ()))
NN = (((1,), (0,)), ((), ()))


def dot(a, b, dims=NN):
    return lax.dot_general(a, b, dims, preferred_element_type=F32)


def project_kernel(x_ref, gain_ref, wf_ref, wv_ref, ww_ref, feat_ref, vlin_ref, qwin_ref, rim_ref, state_ref, normed):
    count = x_ref.shape[2]
    step = 128
    for r in range(0, count, step):
        total = jnp.zeros((step, 1), F32)
        for c in range(2):
            for y in range(4):
                x = x_ref[c, y, r : r + step, :].astype(F32)
                total = total + jnp.sum(x * x, axis=1, keepdims=True)
        scale = lax.rsqrt(total * (1.0 / 2048.0) + EPS)
        for c in range(2):
            for y in range(4):
                at = (2 * y + c) * 256
                x = x_ref[c, y, r : r + step, :].astype(F32)
                normed[r : r + step, at : at + 256] = (
                    x * scale * gain_ref[0:1, at : at + 256]
                ).astype(BF)
    n = normed[...]
    feats = dot(n, wf_ref[...]).astype(BF)
    values = dot(n, wv_ref[...]).astype(BF)
    feat_ref[...] = feats
    vlin = values[:, :128]
    vlin_ref[...] = vlin
    first, second = pick((ROWS, FEAT), 0)
    scale, add_first, add_second = weights_of((ROWS, 1), 0, False)
    k = feats[:, FEAT:]
    phi = (dot(first, k, NT) + add_first) * (dot(second, k, NT) + add_second) * scale
    state = dot(phi.astype(BF), vlin).astype(BF)
    for i in range(4):
        state_ref[i, :, :] = state
    windowed = dot(n, ww_ref[...]).astype(BF)
    qwin_ref[...] = windowed[:, :128]
    rim_ref[:, :128] = windowed[:, 128:]
    rim_ref[:, 128:] = values[:, 128:]


def attend_kernel(first_ref, q_ref, own_ref, prev_ref, feat_ref, vlin_ref, win_ref, num_ref):
    count = q_ref.shape[0]
    tile = 256
    no_prev = first_ref[0] == 0
    for t in range(count // tile):
        q = q_ref[t * tile : (t + 1) * tile, :]
        old = prev_ref[t * tile :, :]
        new = own_ref[: (t + 1) * tile, :]
        keys = jnp.concatenate([old[:, :128], new[:, :128]], axis=0)
        vals = jnp.concatenate([old[:, 128:], new[:, 128:]], axis=0)
        width = keys.shape[0]
        scores = dot(q, keys, NT) * (1.0 / math.sqrt(128.0))
        at = lax.broadcasted_iota(jnp.int32, (tile, width), 0) + count
        key = lax.broadcasted_iota(jnp.int32, (tile, width), 1)
        least = jnp.where(no_prev, count - t * tile, 0)
        allowed = (key <= at) & (key > at - count) & (key >= least)
        scores = jnp.where(allowed, scores, -1e30)
        lifted = jnp.exp(scores - jnp.max(scores, axis=1, keepdims=True))
        probs = (lifted / jnp.sum(lifted, axis=1, keepdims=True)).astype(BF)
        win_ref[t * tile : (t + 1) * tile, :] = dot(probs, vals).astype(BF)
        ql = feat_ref[t * tile : (t + 1) * tile, :FEAT]
        kl = feat_ref[: (t + 1) * tile, FEAT:]
        inner = dot(ql, kl, NT)
        width = kl.shape[0]
        row = lax.broadcasted_iota(jnp.int32, (tile, width), 0) + t * tile
        col = lax.broadcasted_iota(jnp.int32, (tile, width), 1)
        series = 1.0 + inner * 0.25 + inner * inner * (1.0 / 32.0)
        weight = jnp.where(row >= col, series, 0.0).astype(BF)
        num_ref[t * tile : (t + 1) * tile, :] = dot(weight, vlin_ref[: (t + 1) * tile, :])


def mix_kernel(core_ref, feat_ref, num_ref, prefix_ref, win_ref, w_ref, mix_ref, other_ref):
    first, second = pick((FEAT, ROWS), 1)
    scale, add_first, add_second = weights_of((1, ROWS), 1, True)
    q = feat_ref[:, :FEAT]
    phi = (dot(q, first) + add_first) * (dot(q, second) + add_second) * scale
    numerator = num_ref[...] + dot(phi.astype(BF), prefix_ref[...])
    mean = jnp.mean(numerator * numerator, axis=1, keepdims=True)
    mix_ref[:, :128] = (numerator * lax.rsqrt(mean + EPS)).astype(BF)
    mix_ref[:, 128:] = win_ref[...]
    mix = mix_ref[...]
    other = 1 - core_ref[0]
    for y in range(4):
        at = pl.multiple_of((2 * y + other) * 256, 256)
        other_ref[y, :, :] = dot(mix, w_ref[:, pl.ds(at, 256)]).astype(BF)


def join_kernel(core_ref, mix_ref, w_ref, got_ref, sum_ref):
    mix = mix_ref[...]
    for y in range(4):
        at = pl.multiple_of((2 * y + core_ref[0]) * 256, 256)
        mine = dot(mix, w_ref[:, pl.ds(at, 256)])
        sum_ref[y, :, :] = (mine + got_ref[y, :, :].astype(F32)).astype(BF)


def level(states, groups, place):
    got = lax.all_to_all(states, "ctx", 0, 0, tiled=True, axis_index_groups=groups)
    wide = got.astype(F32)
    order = lax.broadcasted_iota(jnp.int32, (4, 1, 1), 0)
    before = jnp.sum(jnp.where(order < place, wide, 0.0), axis=0)
    total = jnp.sum(wide, axis=0).astype(BF)
    return before, jnp.broadcast_to(total[None], states.shape)


def shards(tokens, gain, w_feat, w_value, w_window, w_out):
    count = tokens.shape[0]
    head = lax.axis_index("head")
    ctx = lax.axis_index("ctx")
    core = (head % 2).astype(jnp.int32).reshape(1)
    along_y = [[2 * y + c for y in range(4)] for c in range(2)]
    cores = [[2 * y, 2 * y + 1] for y in range(4)]
    spread = lax.all_to_all(
        jnp.broadcast_to(tokens[None], (4,) + tokens.shape), "head", 0, 0, tiled=True, axis_index_groups=along_y
    )
    gathered = lax.all_gather(spread, "head", axis_index_groups=cores)

    def shape(dims, kind=BF):
        return jax.ShapeDtypeStruct(dims, kind)

    feats, v_lin, q_win, rim, states = call(
        project_kernel,
        [shape((count, 32)), shape((count, 128)), shape((count, 128)), shape((count, 256)), shape((4, ROWS, 128))],
        [pltpu.VMEM((count, 2048), BF)],
    )(gathered, gain.reshape(1, -1), w_feat, w_value, w_window)
    prev = lax.ppermute(rim, "ctx", [(b, b + 1) for b in range(63)])
    in_x = [[4 * z + x for x in range(4)] for z in range(16)]
    in_low = [[16 * h + 4 * l + x for l in range(4)] for h in range(4) for x in range(4)]
    in_high = [[16 * h + 4 * l + x for h in range(4)] for l in range(4) for x in range(4)]
    before_x, states = level(states, in_x, ctx % 4)
    before_low, states = level(states, in_low, (ctx // 4) % 4)
    before_high, _ = level(states, in_high, ctx // 16)
    prefix = (before_x + before_low + before_high).astype(BF)
    win_out, numerator = call_with_scalar(attend_kernel, [shape((count, 128)), shape((count, 128), F32)], 5)(
        ctx.astype(jnp.int32).reshape(1), q_win, rim, prev, feats, v_lin
    )
    mix, other = call_with_scalar(mix_kernel, [shape((count, 256)), shape((4, count, 256))], 5)(
        core, feats, numerator, prefix, win_out, w_out
    )
    got = lax.ppermute(other, "head", [(h, h ^ 1) for h in range(8)])
    summed = call_with_scalar(join_kernel, shape((4, count, 256)), 3)(core, mix, w_out, got)
    parts = lax.all_to_all(summed, "head", 0, 0, tiled=True, axis_index_groups=along_y)
    return jnp.sum(parts.astype(F32), axis=0).astype(BF)


def solution(mesh):
    placed = (P("ctx", "head"), P(), P(None, "head"), P(None, "head"), P(None, "head"), P("head", None))
    return jax.shard_map(shards, mesh=mesh, in_specs=placed, out_specs=P("ctx", "head"), check_vma=False)
```

```python
import functools
import math

import jax
import jax.numpy as jnp
from jax import lax
from jax.experimental import pallas as pl
from jax.experimental.pallas import tpu as pltpu
from jax.sharding import PartitionSpec as P

EPS = 1e-05
FEAT = 16
ROWS = 160
BF = jnp.bfloat16
F32 = jnp.float32
VMEM = 24 * 1024 * 1024


def call(kernel, outs, scratch=()):
    return pl.pallas_call(
        kernel,
        out_shape=outs,
        scratch_shapes=scratch,
        compiler_params=pltpu.CompilerParams(vmem_limit_bytes=VMEM),
    )


def call_with_scalar(kernel, outs, count, scratch=()):
    return pl.pallas_call(
        kernel,
        out_shape=outs,
        in_specs=[pl.BlockSpec(memory_space=pltpu.SMEM)]
        + [pl.BlockSpec(memory_space=pltpu.VMEM)] * count,
        scratch_shapes=scratch,
        compiler_params=pltpu.CompilerParams(vmem_limit_bytes=VMEM),
    )


def pick(shape, axis):
    r = lax.broadcasted_iota(jnp.int32, shape, axis)
    u = lax.broadcasted_iota(jnp.int32, shape, 1 - axis)
    first = (r >= 1) & (r <= FEAT) & (u == r - 1)
    second = jnp.zeros(shape, jnp.bool_)
    base = 1 + FEAT
    for i in range(FEAT):
        width = FEAT - i
        inside = (r >= base) & (r < base + width)
        first = first | (inside & (u == i))
        second = second | (inside & (u == i + r - base))
        base += width
    return first.astype(F32).astype(BF), second.astype(F32).astype(BF)


def weights_of(shape, axis, twice):
    r = lax.broadcasted_iota(jnp.int32, shape, axis)
    scale = jnp.where(r == 0, 1.0, jnp.where(r <= FEAT, 0.5, 1.0 / (4.0 * math.sqrt(2.0))))
    if twice:
        base = 1 + FEAT
        square = jnp.zeros(shape, jnp.bool_)
        for i in range(FEAT):
            square = square | (r == base)
            base += FEAT - i
        scale = jnp.where((r > FEAT) & ~square, 2.0 * scale, scale)
    one_first = jnp.where(r == 0, 1.0, 0.0)
    one_second = jnp.where(r <= FEAT, 1.0, 0.0)
    return scale, one_first, one_second


NT = (((1,), (1,)), ((), ()))
NN = (((1,), (0,)), ((), ()))


def dot(a, b, dims=NN):
    return lax.dot_general(a, b, dims, preferred_element_type=F32)


def project_kernel(
    core_ref, mine_ref, other_ref, gain_ref, wf_ref, wv_ref, ww_ref, feat_ref, vlin_ref, qwin_ref, rim_ref, state_ref, normed
):
    count = mine_ref.shape[1]
    step = 128
    core = core_ref[0]
    for r in range(0, count, step):
        total = jnp.zeros((step, 256), F32)
        for source in (mine_ref, other_ref):
            for y in range(4):
                x = source[y, r : r + step, :].astype(F32)
                total = total + x * x
        scale = lax.rsqrt(jnp.sum(total, axis=1, keepdims=True) * (1.0 / 2048.0) + EPS)
        for flip, source in enumerate((mine_ref, other_ref)):
            for y in range(4):
                at = pl.multiple_of((2 * y + (core + flip) % 2) * 256, 256)
                x = source[y, r : r + step, :].astype(F32)
                normed[r : r + step, pl.ds(at, 256)] = (x * scale * gain_ref[0:1, pl.ds(at, 256)]).astype(BF)
    n = normed[...]
    feats = dot(n, wf_ref[...], NT).astype(BF)
    values = dot(n, wv_ref[...]).astype(BF)
    feat_ref[...] = feats
    vlin = values[:, :128]
    vlin_ref[...] = vlin
    first, second = pick((ROWS, FEAT), 0)
    scale, add_first, add_second = weights_of((ROWS, 1), 0, False)
    k = feats[:, FEAT:]
    phi = (dot(first, k, NT) + add_first) * (dot(second, k, NT) + add_second) * scale
    state = dot(phi.astype(BF), vlin).astype(BF)
    for i in range(4):
        state_ref[i, :, :] = state
    windowed = dot(n, ww_ref[...]).astype(BF)
    qwin_ref[...] = windowed[:, :128]
    rim_ref[:, :128] = windowed[:, 128:]
    rim_ref[:, 128:] = values[:, 128:]


def inner_kernel(feat_ref, vlin_ref, num_ref):
    count = feat_ref.shape[0]
    tile = 256
    for t in range(count // tile):
        ql = feat_ref[t * tile : (t + 1) * tile, :FEAT]
        kl = feat_ref[: (t + 1) * tile, FEAT:]
        inner = dot(ql, kl, NT)
        width = kl.shape[0]
        row = lax.broadcasted_iota(jnp.int32, (tile, width), 0) + t * tile
        col = lax.broadcasted_iota(jnp.int32, (tile, width), 1)
        series = 1.0 + inner * 0.25 + inner * inner * (1.0 / 32.0)
        weight = jnp.where(row >= col, series, 0.0).astype(BF)
        num_ref[t * tile : (t + 1) * tile, :] = dot(weight, vlin_ref[: (t + 1) * tile, :])


def attend_kernel(first_ref, q_ref, own_ref, prev_ref, win_ref):
    count = q_ref.shape[0]
    tile = 256
    no_prev = first_ref[0] == 0
    for t in range(count // tile):
        q = q_ref[t * tile : (t + 1) * tile, :]
        old = prev_ref[t * tile :, :]
        new = own_ref[: (t + 1) * tile, :]
        keys = jnp.concatenate([old[:, :128], new[:, :128]], axis=0)
        vals = jnp.concatenate([old[:, 128:], new[:, 128:]], axis=0)
        width = keys.shape[0]
        scores = dot(q, keys, NT) * (1.0 / math.sqrt(128.0))
        at = lax.broadcasted_iota(jnp.int32, (tile, width), 0) + count
        key = lax.broadcasted_iota(jnp.int32, (tile, width), 1)
        least = jnp.where(no_prev, count - t * tile, 0)
        allowed = (key <= at) & (key > at - count) & (key >= least)
        scores = jnp.where(allowed, scores, -1e30)
        lifted = jnp.exp(scores - jnp.max(scores, axis=1, keepdims=True))
        probs = (lifted / jnp.sum(lifted, axis=1, keepdims=True)).astype(BF)
        win_ref[t * tile : (t + 1) * tile, :] = dot(probs, vals).astype(BF)


def linear_kernel(feat_ref, num_ref, prefix_ref, lin_ref):
    first, second = pick((FEAT, ROWS), 1)
    scale, add_first, add_second = weights_of((1, ROWS), 1, True)
    q = feat_ref[:, :FEAT]
    phi = (dot(q, first) + add_first) * (dot(q, second) + add_second) * scale
    numerator = num_ref[...] + dot(phi.astype(BF), prefix_ref[...])
    mean = jnp.mean(numerator * numerator, axis=1, keepdims=True)
    lin_ref[...] = (numerator * lax.rsqrt(mean + EPS)).astype(BF)


def output_kernel(core_ref, lin_ref, win_ref, w_ref, lin2_ref, win2_ref, w2_ref, sum_ref):
    mine = jnp.concatenate([lin_ref[...], win_ref[...]], axis=1)
    other = jnp.concatenate([lin2_ref[...], win2_ref[...]], axis=1)
    for y in range(4):
        at = pl.multiple_of((2 * y + core_ref[0]) * 256, 256)
        total = dot(mine, w_ref[:, pl.ds(at, 256)]) + dot(other, w2_ref[:, pl.ds(at, 256)])
        sum_ref[y, :, :] = total.astype(BF)


def level(states, groups, place):
    got = lax.all_to_all(states, "ctx", 0, 0, tiled=True, axis_index_groups=groups)
    wide = got.astype(F32)
    order = lax.broadcasted_iota(jnp.int32, (4, 1, 1), 0)
    before = jnp.sum(jnp.where(order < place, wide, 0.0), axis=0)
    total = jnp.sum(wide, axis=0).astype(BF)
    return before, jnp.broadcast_to(total[None], states.shape)


def shards(tokens, gain, w_feat, w_value, w_window, w_out):
    count = tokens.shape[0]
    head = lax.axis_index("head")
    ctx = lax.axis_index("ctx")
    core = (head % 2).astype(jnp.int32).reshape(1)
    along_y = [[2 * y + c for y in range(4)] for c in range(2)]

    def across(value):
        return lax.ppermute(value, "head", [(h, h ^ 1) for h in range(8)])

    def shape(dims, kind=BF):
        return jax.ShapeDtypeStruct(dims, kind)

    spread = lax.all_to_all(
        jnp.broadcast_to(tokens[None], (4,) + tokens.shape), "head", 0, 0, tiled=True, axis_index_groups=along_y
    )
    feats, v_lin, q_win, rim, states = call_with_scalar(
        project_kernel,
        [shape((count, 32)), shape((count, 128)), shape((count, 128)), shape((count, 256)), shape((4, ROWS, 128))],
        6,
        [pltpu.VMEM((count, 2048), BF)],
    )(core, spread, across(spread), gain.reshape(1, -1), w_feat.T, w_value, w_window)
    prev = lax.ppermute(rim, "ctx", [(b, b + 1) for b in range(63)])
    in_x = [[4 * z + x for x in range(4)] for z in range(16)]
    in_low = [[16 * h + 4 * l + x for l in range(4)] for h in range(4) for x in range(4)]
    in_high = [[16 * h + 4 * l + x for h in range(4)] for l in range(4) for x in range(4)]
    before_x, states = level(states, in_x, ctx % 4)
    numerator = call(inner_kernel, shape((count, 128), F32))(feats, v_lin)
    states, numerator = lax.optimization_barrier((states, numerator))
    before_low, states = level(states, in_low, (ctx // 4) % 4)
    win_out = call_with_scalar(attend_kernel, shape((count, 128)), 3)(ctx.astype(jnp.int32).reshape(1), q_win, rim, prev)
    states, win_out, w_later = lax.optimization_barrier((states, win_out, w_out))
    win_other = across(win_out)
    w_other = across(w_later)
    before_high, _ = level(states, in_high, ctx // 16)
    prefix = (before_x + before_low + before_high).astype(BF)
    lin_out = call(linear_kernel, shape((count, 128)))(feats, numerator, prefix)
    lin_other = across(lin_out)
    summed = call_with_scalar(output_kernel, shape((4, count, 256)), 6)(
        core, lin_out, win_out, w_out, lin_other, win_other, w_other
    )
    parts = lax.all_to_all(summed, "head", 0, 0, tiled=True, axis_index_groups=along_y)
    return jnp.sum(parts.astype(F32), axis=0).astype(BF)


def solution(mesh):
    placed = (P("ctx", "head"), P(), P(None, "head"), P(None, "head"), P(None, "head"), P("head", None))
    return jax.shard_map(shards, mesh=mesh, in_specs=placed, out_specs=P("ctx", "head"), check_vma=False)
```

```python
import functools
import math

import jax
import jax.numpy as jnp
from jax import lax
from jax.experimental import pallas as pl
from jax.experimental.pallas import tpu as pltpu
from jax.sharding import PartitionSpec as P

EPS = 1e-05
FEAT = 16
PARTS = 64
DEEP = 3
ROWS = PARTS * DEEP
BF = jnp.bfloat16
F32 = jnp.float32
VMEM = 24 * 1024 * 1024


def call(kernel, outs, scratch=()):
    return pl.pallas_call(
        kernel,
        out_shape=outs,
        scratch_shapes=scratch,
        compiler_params=pltpu.CompilerParams(vmem_limit_bytes=VMEM),
    )


def call_with_scalar(kernel, outs, count, scratch=()):
    return pl.pallas_call(
        kernel,
        out_shape=outs,
        in_specs=[pl.BlockSpec(memory_space=pltpu.SMEM)]
        + [pl.BlockSpec(memory_space=pltpu.VMEM)] * count,
        scratch_shapes=scratch,
        compiler_params=pltpu.CompilerParams(vmem_limit_bytes=VMEM),
    )


def pick(shape, axis):
    r = lax.broadcasted_iota(jnp.int32, shape, axis)
    u = lax.broadcasted_iota(jnp.int32, shape, 1 - axis)
    first = (r >= 1) & (r <= FEAT) & (u == r - 1)
    second = jnp.zeros(shape, jnp.bool_)
    base = 1 + FEAT
    for i in range(FEAT):
        width = FEAT - i
        inside = (r >= base) & (r < base + width)
        first = first | (inside & (u == i))
        second = second | (inside & (u == i + r - base))
        base += width
    return first.astype(F32).astype(BF), second.astype(F32).astype(BF)


def weights_of(shape, axis, twice):
    r = lax.broadcasted_iota(jnp.int32, shape, axis)
    scale = jnp.where(r == 0, 1.0, jnp.where(r <= FEAT, 0.5, 1.0 / (4.0 * math.sqrt(2.0))))
    if twice:
        base = 1 + FEAT
        square = jnp.zeros(shape, jnp.bool_)
        for i in range(FEAT):
            square = square | (r == base)
            base += FEAT - i
        scale = jnp.where((r > FEAT) & ~square, 2.0 * scale, scale)
    one_first = jnp.where(r == 0, 1.0, 0.0)
    one_second = jnp.where(r <= FEAT, 1.0, 0.0)
    return scale, one_first, one_second


NT = (((1,), (1,)), ((), ()))
NN = (((1,), (0,)), ((), ()))


def dot(a, b, dims=NN):
    return lax.dot_general(a, b, dims, preferred_element_type=F32)


def project_kernel(
    core_ref, mine_ref, other_ref, gain_ref, wf_ref, wv_ref, ww_ref, feat_ref, vlin_ref, qwin_ref, rim_ref, state_ref, normed
):
    count = mine_ref.shape[1]
    step = 128
    core = core_ref[0]
    for r in range(0, count, step):
        total = jnp.zeros((step, 256), F32)
        for source in (mine_ref, other_ref):
            for y in range(4):
                x = source[y, r : r + step, :].astype(F32)
                total = total + x * x
        scale = lax.rsqrt(jnp.sum(total, axis=1, keepdims=True) * (1.0 / 2048.0) + EPS)
        for flip, source in enumerate((mine_ref, other_ref)):
            for y in range(4):
                at = pl.multiple_of((2 * y + (core + flip) % 2) * 256, 256)
                x = source[y, r : r + step, :].astype(F32)
                normed[r : r + step, pl.ds(at, 256)] = (x * scale * gain_ref[0:1, pl.ds(at, 256)]).astype(BF)
    n = normed[...]
    feats = dot(n, wf_ref[...], NT).astype(BF)
    values = dot(n, wv_ref[...]).astype(BF)
    feat_ref[...] = feats
    vlin = values[:, :128]
    vlin_ref[...] = vlin
    first, second = pick((ROWS, FEAT), 0)
    scale, add_first, add_second = weights_of((ROWS, 1), 0, False)
    k = feats[:, FEAT:]
    phi = (dot(first, k, NT) + add_first) * (dot(second, k, NT) + add_second) * scale
    state = dot(phi.astype(BF), vlin).astype(BF)
    for i in range(DEEP):
        state_ref[:, i, :] = state[PARTS * i : PARTS * (i + 1), :]
    windowed = dot(n, ww_ref[...]).astype(BF)
    qwin_ref[...] = windowed[:, :128]
    rim_ref[:, :128] = windowed[:, 128:]
    rim_ref[:, 128:] = values[:, 128:]


def inner_kernel(feat_ref, vlin_ref, num_ref):
    count = feat_ref.shape[0]
    tile = 256
    for t in range(count // tile):
        ql = feat_ref[t * tile : (t + 1) * tile, :FEAT]
        kl = feat_ref[: (t + 1) * tile, FEAT:]
        inner = dot(ql, kl, NT)
        width = kl.shape[0]
        row = lax.broadcasted_iota(jnp.int32, (tile, width), 0) + t * tile
        col = lax.broadcasted_iota(jnp.int32, (tile, width), 1)
        series = 1.0 + inner * 0.25 + inner * inner * (1.0 / 32.0)
        weight = jnp.where(row >= col, series, 0.0).astype(BF)
        num_ref[t * tile : (t + 1) * tile, :] = dot(weight, vlin_ref[: (t + 1) * tile, :])


def attend_kernel(first_ref, q_ref, own_ref, prev_ref, win_ref):
    count = q_ref.shape[0]
    tile = 256
    no_prev = first_ref[0] == 0
    for t in range(count // tile):
        q = q_ref[t * tile : (t + 1) * tile, :]
        old = prev_ref[t * tile :, :]
        new = own_ref[: (t + 1) * tile, :]
        keys = jnp.concatenate([old[:, :128], new[:, :128]], axis=0)
        vals = jnp.concatenate([old[:, 128:], new[:, 128:]], axis=0)
        width = keys.shape[0]
        scores = dot(q, keys, NT) * (1.0 / math.sqrt(128.0))
        at = lax.broadcasted_iota(jnp.int32, (tile, width), 0) + count
        key = lax.broadcasted_iota(jnp.int32, (tile, width), 1)
        least = jnp.where(no_prev, count - t * tile, 0)
        allowed = (key <= at) & (key > at - count) & (key >= least)
        scores = jnp.where(allowed, scores, -1e30)
        lifted = jnp.exp(scores - jnp.max(scores, axis=1, keepdims=True))
        probs = (lifted / jnp.sum(lifted, axis=1, keepdims=True)).astype(BF)
        win_ref[t * tile : (t + 1) * tile, :] = dot(probs, vals).astype(BF)


def linear_kernel(feat_ref, num_ref, prefix_ref, lin_ref):
    first, second = pick((FEAT, ROWS), 1)
    scale, add_first, add_second = weights_of((1, ROWS), 1, True)
    q = feat_ref[:, :FEAT]
    phi = (dot(q, first) + add_first) * (dot(q, second) + add_second) * scale
    prefix = jnp.concatenate([prefix_ref[:, i, :] for i in range(DEEP)], axis=0)
    numerator = num_ref[...] + dot(phi.astype(BF), prefix)
    mean = jnp.mean(numerator * numerator, axis=1, keepdims=True)
    lin_ref[...] = (numerator * lax.rsqrt(mean + EPS)).astype(BF)


def output_kernel(core_ref, lin_ref, win_ref, w_ref, lin2_ref, win2_ref, w2_ref, sum_ref):
    mine = jnp.concatenate([lin_ref[...], win_ref[...]], axis=1)
    other = jnp.concatenate([lin2_ref[...], win2_ref[...]], axis=1)
    for y in range(4):
        at = pl.multiple_of((2 * y + core_ref[0]) * 256, 256)
        total = dot(mine, w_ref[:, pl.ds(at, 256)]) + dot(other, w2_ref[:, pl.ds(at, 256)])
        sum_ref[y, :, :] = total.astype(BF)


def prefix_kernel(got_ref, out_ref):
    earlier = lax.broadcasted_iota(jnp.int32, (PARTS, PARTS), 1) < lax.broadcasted_iota(jnp.int32, (PARTS, PARTS), 0)
    earlier = earlier.astype(F32).astype(BF)
    for i in range(DEEP):
        out_ref[:, i, :] = dot(earlier, got_ref[:, i, :]).astype(BF)


def shards(tokens, gain, w_feat, w_value, w_window, w_out):
    count = tokens.shape[0]
    head = lax.axis_index("head")
    ctx = lax.axis_index("ctx")
    core = (head % 2).astype(jnp.int32).reshape(1)
    along_y = [[2 * y + c for y in range(4)] for c in range(2)]

    def across(value):
        return lax.ppermute(value, "head", [(h, h ^ 1) for h in range(8)])

    def shape(dims, kind=BF):
        return jax.ShapeDtypeStruct(dims, kind)

    spread = lax.all_to_all(
        jnp.broadcast_to(tokens[None], (4,) + tokens.shape), "head", 0, 0, tiled=True, axis_index_groups=along_y
    )
    feats, v_lin, q_win, rim, states = call_with_scalar(
        project_kernel,
        [shape((count, 32)), shape((count, 128)), shape((count, 128)), shape((count, 256)), shape((PARTS, DEEP, 128))],
        6,
        [pltpu.VMEM((count, 2048), BF)],
    )(core, spread, across(spread), gain.reshape(1, -1), w_feat.T, w_value, w_window)
    numerator = call(inner_kernel, shape((count, 128), F32))(feats, v_lin)
    rim, numerator = lax.optimization_barrier((rim, numerator))
    prev = lax.ppermute(rim, "ctx", [(b, b + 1) for b in range(PARTS - 1)])
    pieces = lax.all_to_all(states, "ctx", 0, 0, tiled=True)
    sums = call(prefix_kernel, shape((PARTS, DEEP, 128)))(pieces)
    sums, prev = lax.optimization_barrier((sums, prev))
    prefix = lax.all_to_all(sums, "ctx", 0, 0, tiled=True)
    win_out = call_with_scalar(attend_kernel, shape((count, 128)), 3)(ctx.astype(jnp.int32).reshape(1), q_win, rim, prev)
    w_later, win_out = lax.optimization_barrier((w_out, win_out))
    w_other = across(w_later)
    win_other = across(win_out)
    lin_out = call(linear_kernel, shape((count, 128)))(feats, numerator, prefix)
    lin_other = across(lin_out)
    summed = call_with_scalar(output_kernel, shape((4, count, 256)), 6)(
        core, lin_out, win_out, w_out, lin_other, win_other, w_other
    )
    parts = lax.all_to_all(summed, "head", 0, 0, tiled=True, axis_index_groups=along_y)
    return jnp.sum(parts.astype(F32), axis=0).astype(BF)


def solution(mesh):
    placed = (P("ctx", "head"), P(), P(None, "head"), P(None, "head"), P(None, "head"), P("head", None))
    return jax.shard_map(shards, mesh=mesh, in_specs=placed, out_specs=P("ctx", "head"), check_vma=False)
```

```python
import functools
import math

import jax
import jax.numpy as jnp
from jax import lax
from jax.experimental import pallas as pl
from jax.experimental.pallas import tpu as pltpu
from jax.sharding import PartitionSpec as P

EPS = 1e-05
FEAT = 16
QUARTER = 40
ROWS = 4 * QUARTER
BF = jnp.bfloat16
F32 = jnp.float32
VMEM = 12 * 1024 * 1024


def call(kernel, outs, scratch=()):
    return pl.pallas_call(
        kernel,
        out_shape=outs,
        scratch_shapes=scratch,
        compiler_params=pltpu.CompilerParams(vmem_limit_bytes=VMEM),
    )


def call_with_scalar(kernel, outs, count, scratch=(), in_place=None):
    return pl.pallas_call(
        kernel,
        out_shape=outs,
        in_specs=[pl.BlockSpec(memory_space=pltpu.SMEM)]
        + [pl.BlockSpec(memory_space=pltpu.HBM if i + 1 == in_place else pltpu.VMEM) for i in range(count)],
        scratch_shapes=scratch,
        compiler_params=pltpu.CompilerParams(vmem_limit_bytes=VMEM),
    )


def pick(shape, axis):
    r = lax.broadcasted_iota(jnp.int32, shape, axis)
    u = lax.broadcasted_iota(jnp.int32, shape, 1 - axis)
    first = (r >= 1) & (r <= FEAT) & (u == r - 1)
    second = jnp.zeros(shape, jnp.bool_)
    base = 1 + FEAT
    for i in range(FEAT):
        width = FEAT - i
        inside = (r >= base) & (r < base + width)
        first = first | (inside & (u == i))
        second = second | (inside & (u == i + r - base))
        base += width
    return first.astype(F32).astype(BF), second.astype(F32).astype(BF)


def weights_of(shape, axis, twice):
    r = lax.broadcasted_iota(jnp.int32, shape, axis)
    scale = jnp.where(r == 0, 1.0, jnp.where(r <= FEAT, 0.5, 1.0 / (4.0 * math.sqrt(2.0))))
    if twice:
        base = 1 + FEAT
        square = jnp.zeros(shape, jnp.bool_)
        for i in range(FEAT):
            square = square | (r == base)
            base += FEAT - i
        scale = jnp.where((r > FEAT) & ~square, 2.0 * scale, scale)
    one_first = jnp.where(r == 0, 1.0, 0.0)
    one_second = jnp.where(r <= FEAT, 1.0, 0.0)
    return scale, one_first, one_second


NT = (((1,), (1,)), ((), ()))
NN = (((1,), (0,)), ((), ()))


def dot(a, b, dims=NN):
    return lax.dot_general(a, b, dims, preferred_element_type=F32)


def project_kernel(
    core_ref, mine_ref, other_ref, gain_ref, wf_hbm, wv_ref, ww_ref, pack_ref, rim_ref, state_ref, normed, wf_ref, wf_sem
):
    load = pltpu.make_async_copy(wf_hbm, wf_ref, wf_sem)
    load.start()
    count = mine_ref.shape[1]
    step = 128
    core = core_ref[0]
    for r in range(0, count, step):
        total = jnp.zeros((step, 256), F32)
        for source in (mine_ref, other_ref):
            for y in range(4):
                x = source[y, r : r + step, :].astype(F32)
                total = total + x * x
        scale = lax.rsqrt(jnp.sum(total, axis=1, keepdims=True) * (1.0 / 2048.0) + EPS)
        for flip, source in enumerate((mine_ref, other_ref)):
            for y in range(4):
                at = pl.multiple_of((2 * y + (core + flip) % 2) * 256, 256)
                x = source[y, r : r + step, :].astype(F32)
                normed[r : r + step, pl.ds(at, 256)] = (x * scale * gain_ref[0:1, pl.ds(at, 256)]).astype(BF)
    n = normed[...]
    load.wait()
    feats = dot(n, wf_ref[...], NT).astype(BF)
    values = dot(n, wv_ref[...]).astype(BF)
    pack_ref[:, 256:288] = feats
    pack_ref[:, 288:] = jnp.zeros((count, 96), BF)
    vlin = values[:, :128]
    pack_ref[:, 128:256] = vlin
    first, second = pick((ROWS, FEAT), 0)
    scale, add_first, add_second = weights_of((ROWS, 1), 0, False)
    k = feats[:, FEAT:]
    phi = (dot(first, k, NT) + add_first) * (dot(second, k, NT) + add_second) * scale
    state = dot(phi.astype(BF), vlin)
    for i in range(4):
        state_ref[i, :, :] = state[QUARTER * i : QUARTER * (i + 1), :].astype(BF)
    windowed = dot(n, ww_ref[...]).astype(BF)
    pack_ref[:, :128] = windowed[:, :128]
    rim_ref[:, :128] = windowed[:, 128:]
    rim_ref[:, 128:] = values[:, 128:]


def inner_kernel(pack_ref, num_ref):
    count = pack_ref.shape[0]
    tile = 256
    for t in range(count // tile):
        ql = pack_ref[t * tile : (t + 1) * tile, 256 : 256 + FEAT]
        kl = pack_ref[: (t + 1) * tile, 256 + FEAT : 256 + 2 * FEAT]
        inner = dot(ql, kl, NT)
        width = kl.shape[0]
        row = lax.broadcasted_iota(jnp.int32, (tile, width), 0) + t * tile
        col = lax.broadcasted_iota(jnp.int32, (tile, width), 1)
        series = 1.0 + inner * 0.25 + inner * inner * (1.0 / 32.0)
        weight = jnp.where(row >= col, series, 0.0).astype(BF)
        num_ref[t * tile : (t + 1) * tile, :] = dot(weight, pack_ref[: (t + 1) * tile, 128:256])


def attend_kernel(first_ref, pack_ref, own_ref, prev_ref, win_ref):
    count = pack_ref.shape[0]
    tile = 256
    no_prev = first_ref[0] == 0
    for t in range(count // tile):
        q = pack_ref[t * tile : (t + 1) * tile, :128]
        old = prev_ref[t * tile :, :]
        new = own_ref[: (t + 1) * tile, :]
        keys = jnp.concatenate([old[:, :128], new[:, :128]], axis=0)
        vals = jnp.concatenate([old[:, 128:], new[:, 128:]], axis=0)
        width = keys.shape[0]
        scores = dot(q, keys, NT) * (1.0 / math.sqrt(128.0))
        at = lax.broadcasted_iota(jnp.int32, (tile, width), 0) + count
        key = lax.broadcasted_iota(jnp.int32, (tile, width), 1)
        least = jnp.where(no_prev, count - t * tile, 0)
        allowed = (key <= at) & (key > at - count) & (key >= least)
        scores = jnp.where(allowed, scores, -1e30)
        lifted = jnp.exp(scores - jnp.max(scores, axis=1, keepdims=True))
        probs = (lifted / jnp.sum(lifted, axis=1, keepdims=True)).astype(BF)
        win_ref[t * tile : (t + 1) * tile, :] = dot(probs, vals).astype(BF)


def linear_kernel(pack_ref, num_ref, prefix_ref, win_ref, mix_ref):
    first, second = pick((FEAT, ROWS), 1)
    scale, add_first, add_second = weights_of((1, ROWS), 1, True)
    q = pack_ref[:, 256 : 256 + FEAT]
    phi = (dot(q, first) + add_first) * (dot(q, second) + add_second) * scale
    prefix = jnp.concatenate([prefix_ref[i, :, :].astype(F32) for i in range(4)], axis=0).astype(BF)
    numerator = num_ref[...] + dot(phi.astype(BF), prefix)
    mean = jnp.mean(numerator * numerator, axis=1, keepdims=True)
    mix_ref[:, :128] = (numerator * lax.rsqrt(mean + EPS)).astype(BF)
    mix_ref[:, 128:] = win_ref[...]


def output_kernel(core_ref, mix_ref, w_ref, mix2_ref, w2_ref, sum_ref):
    for y in range(4):
        at = pl.multiple_of((2 * y + core_ref[0]) * 256, 256)
        total = dot(mix_ref[...], w_ref[:, pl.ds(at, 256)]) + dot(mix2_ref[...], w2_ref[:, pl.ds(at, 256)])
        sum_ref[y, :, :] = total.astype(BF)


def total_kernel(got_ref, out_ref):
    total = got_ref[0, :, :].astype(F32)
    for i in range(1, 4):
        total = total + got_ref[i, :, :].astype(F32)
    total = total.astype(BF)
    for z in range(16):
        out_ref[z, :, :] = total


def prefix_kernel(place_ref, got_ref, totals_ref, out_ref):
    state = jnp.zeros((QUARTER, 128), F32)
    for z in range(15):
        state = state + jnp.where(z < place_ref[0], totals_ref[z, :, :].astype(F32), 0.0)
    for i in range(4):
        out_ref[i, :, :] = state.astype(BF)
        state = state + got_ref[i, :, :].astype(F32)


def shards(tokens, gain, w_feat, w_value, w_window, w_out):
    count = tokens.shape[0]
    head = lax.axis_index("head")
    ctx = lax.axis_index("ctx")
    core = (head % 2).astype(jnp.int32).reshape(1)
    along_y = [[2 * y + c for y in range(4)] for c in range(2)]

    def across(value):
        return lax.ppermute(value, "head", [(h, h ^ 1) for h in range(8)])

    def shape(dims, kind=BF):
        return jax.ShapeDtypeStruct(dims, kind)

    spread = lax.all_to_all(
        jnp.broadcast_to(tokens[None], (4,) + tokens.shape), "head", 0, 0, tiled=True, axis_index_groups=along_y
    )
    spread, w_later = lax.optimization_barrier((spread, w_out))
    other = across(spread)
    w_other = across(w_later)
    pack, rim, states = call_with_scalar(
        project_kernel,
        [shape((count, 384)), shape((count, 256)), shape((4, QUARTER, 128))],
        6,
        [pltpu.VMEM((count, 2048), BF), pltpu.VMEM((32, 2048), BF), pltpu.SemaphoreType.DMA],
        4,
    )(core, spread, other, gain.reshape(1, -1), w_feat.T, w_value, w_window)
    in_x = [[4 * z + x for x in range(4)] for z in range(16)]
    in_z = [[4 * z + x for z in range(16)] for x in range(4)]
    quarters = lax.all_to_all(states, "ctx", 0, 0, tiled=True, axis_index_groups=in_x)
    rim, quarters = lax.optimization_barrier((rim, quarters))
    totals = lax.all_to_all(
        call(total_kernel, shape((16, QUARTER, 128)))(quarters), "ctx", 0, 0, tiled=True, axis_index_groups=in_z
    )
    prev = lax.ppermute(rim, "ctx", [(b, b + 1) for b in range(63)])
    numerator = call(inner_kernel, shape((count, 128), F32))(pack)
    win_out = call_with_scalar(attend_kernel, shape((count, 128)), 3)(ctx.astype(jnp.int32).reshape(1), pack, rim, prev)
    sums = call_with_scalar(prefix_kernel, shape((4, QUARTER, 128)), 2)(
        (ctx // 4).astype(jnp.int32).reshape(1), quarters, totals
    )
    sums, numerator, win_out = lax.optimization_barrier((sums, numerator, win_out))
    prefix = lax.all_to_all(sums, "ctx", 0, 0, tiled=True, axis_index_groups=in_x)
    mix = call(linear_kernel, shape((count, 256)))(pack, numerator, prefix, win_out)
    summed = call_with_scalar(output_kernel, shape((4, count, 256)), 4)(core, mix, w_out, across(mix), w_other)
    parts = lax.all_to_all(summed, "head", 0, 0, tiled=True, axis_index_groups=along_y)
    return jnp.sum(parts.astype(F32), axis=0).astype(BF)


def solution(mesh):
    placed = (P("ctx", "head"), P(), P(None, "head"), P(None, "head"), P(None, "head"), P("head", None))
    return jax.shard_map(shards, mesh=mesh, in_specs=placed, out_specs=P("ctx", "head"), check_vma=False)
```

```python
import functools
import math

import jax
import jax.numpy as jnp
from jax import lax
from jax.experimental import pallas as pl
from jax.experimental.pallas import tpu as pltpu
from jax.sharding import PartitionSpec as P

EPS = 1e-05
FEAT = 16
QUARTER = 40
ROWS = 4 * QUARTER
BF = jnp.bfloat16
F32 = jnp.float32
VMEM = 12 * 1024 * 1024


def call(kernel, outs, scratch=()):
    return pl.pallas_call(
        kernel,
        out_shape=outs,
        scratch_shapes=scratch,
        compiler_params=pltpu.CompilerParams(vmem_limit_bytes=VMEM),
    )


def call_with_scalar(kernel, outs, count):
    return pl.pallas_call(
        kernel,
        out_shape=outs,
        in_specs=[pl.BlockSpec(memory_space=pltpu.SMEM)]
        + [pl.BlockSpec(memory_space=pltpu.VMEM)] * count,
        compiler_params=pltpu.CompilerParams(vmem_limit_bytes=VMEM),
    )


def pick(shape, axis):
    r = lax.broadcasted_iota(jnp.int32, shape, axis)
    u = lax.broadcasted_iota(jnp.int32, shape, 1 - axis)
    first = (r >= 1) & (r <= FEAT) & (u == r - 1)
    second = jnp.zeros(shape, jnp.bool_)
    base = 1 + FEAT
    for i in range(FEAT):
        width = FEAT - i
        inside = (r >= base) & (r < base + width)
        first = first | (inside & (u == i))
        second = second | (inside & (u == i + r - base))
        base += width
    return first.astype(F32).astype(BF), second.astype(F32).astype(BF)


def weights_of(shape, axis, twice):
    r = lax.broadcasted_iota(jnp.int32, shape, axis)
    scale = jnp.where(r == 0, 1.0, jnp.where(r <= FEAT, 0.5, 1.0 / (4.0 * math.sqrt(2.0))))
    if twice:
        base = 1 + FEAT
        square = jnp.zeros(shape, jnp.bool_)
        for i in range(FEAT):
            square = square | (r == base)
            base += FEAT - i
        scale = jnp.where((r > FEAT) & ~square, 2.0 * scale, scale)
    one_first = jnp.where(r == 0, 1.0, 0.0)
    one_second = jnp.where(r <= FEAT, 1.0, 0.0)
    return scale, one_first, one_second


NT = (((1,), (1,)), ((), ()))
NN = (((1,), (0,)), ((), ()))


def dot(a, b, dims=NN):
    return lax.dot_general(a, b, dims, preferred_element_type=F32)


def project_kernel(
    core_ref, mine_ref, other_ref, gain_ref, wf_hbm, wv_ref, ww_ref, *rest
):
    *before, pack_hbm, rim_hbm, state_ref, flag_ref, normed, wf_ref, pack_ref, rim_ref, sems = rest
    load = pltpu.make_async_copy(wf_hbm, wf_ref, sems.at[0])
    load.start()
    count = mine_ref.shape[1]
    step = 128
    core = core_ref[0]
    for r in range(0, count, step):
        total = jnp.zeros((step, 256), F32)
        for source in (mine_ref, other_ref):
            for y in range(4):
                x = source[y, r : r + step, :].astype(F32)
                total = total + x * x
        scale = lax.rsqrt(jnp.sum(total, axis=1, keepdims=True) * (1.0 / 2048.0) + EPS)
        for flip, source in enumerate((mine_ref, other_ref)):
            for y in range(4):
                at = pl.multiple_of((2 * y + (core + flip) % 2) * 256, 256)
                x = source[y, r : r + step, :].astype(F32)
                normed[r : r + step, pl.ds(at, 256)] = (x * scale * gain_ref[0:1, pl.ds(at, 256)]).astype(BF)
    low = count if before else 0
    n = normed[...]
    windowed = dot(n, ww_ref[...]).astype(BF)
    values = dot(n, wv_ref[...]).astype(BF)
    rim_ref[:, :128] = windowed[:, 128:]
    rim_ref[:, 128:] = values[:, 128:]
    store_rim = pltpu.make_async_copy(rim_ref, rim_hbm.at[low : low + count, :], sems.at[1])
    store_rim.start()
    load.wait()
    feats = dot(n, wf_ref[...], NT).astype(BF)
    vlin = values[:, :128]
    pack_ref[:, :128] = windowed[:, :128]
    pack_ref[:, 128:256] = vlin
    pack_ref[:, 256:288] = feats
    pack_ref[:, 288:] = jnp.zeros((count, 96), BF)
    store_pack = pltpu.make_async_copy(pack_ref, pack_hbm.at[low : low + count, :], sems.at[2])
    store_pack.start()
    first, second = pick((ROWS, FEAT), 0)
    scale, add_first, add_second = weights_of((ROWS, 1), 0, False)
    k = feats[:, FEAT:]
    phi = (dot(first, k, NT) + add_first) * (dot(second, k, NT) + add_second) * scale
    state = dot(phi.astype(BF), vlin)
    if not before:
        state_ref[...] = state
        flag_ref[...] = jnp.zeros(flag_ref.shape, F32)
    else:
        state = state + before[2][...]
        flag_ref[...] = before[3][...]
        for i in range(4):
            state_ref[i, :, :] = state[QUARTER * i : QUARTER * (i + 1), :].astype(BF)
    store_rim.wait()
    store_pack.wait()


def inner_kernel(pack_ref, num_ref):
    count = pack_ref.shape[0]
    tile = 256
    for t in range(count // tile):
        ql = pack_ref[t * tile : (t + 1) * tile, 256 : 256 + FEAT]
        kl = pack_ref[: (t + 1) * tile, 256 + FEAT : 256 + 2 * FEAT]
        inner = dot(ql, kl, NT)
        width = kl.shape[0]
        row = lax.broadcasted_iota(jnp.int32, (tile, width), 0) + t * tile
        col = lax.broadcasted_iota(jnp.int32, (tile, width), 1)
        series = 1.0 + inner * 0.25 + inner * inner * (1.0 / 32.0)
        weight = jnp.where(row >= col, series, 0.0).astype(BF)
        num_ref[t * tile : (t + 1) * tile, :] = dot(weight, pack_ref[: (t + 1) * tile, 128:256])


def attend_kernel(first_ref, pack_ref, own_ref, prev_ref, win_ref):
    count = pack_ref.shape[0]
    tile = 256
    no_prev = first_ref[0] == 0
    for t in range(count // tile):
        q = pack_ref[t * tile : (t + 1) * tile, :128]
        old = prev_ref[t * tile :, :]
        new = own_ref[: (t + 1) * tile, :]
        keys = jnp.concatenate([old[:, :128], new[:, :128]], axis=0)
        vals = jnp.concatenate([old[:, 128:], new[:, 128:]], axis=0)
        width = keys.shape[0]
        scores = dot(q, keys, NT) * (1.0 / math.sqrt(128.0))
        at = lax.broadcasted_iota(jnp.int32, (tile, width), 0) + count
        key = lax.broadcasted_iota(jnp.int32, (tile, width), 1)
        least = jnp.where(no_prev, count - t * tile, 0)
        allowed = (key <= at) & (key > at - count) & (key >= least)
        scores = jnp.where(allowed, scores, -1e30)
        lifted = jnp.exp(scores - jnp.max(scores, axis=1, keepdims=True))
        probs = (lifted / jnp.sum(lifted, axis=1, keepdims=True)).astype(BF)
        win_ref[t * tile : (t + 1) * tile, :] = dot(probs, vals).astype(BF)


def linear_kernel(pack_ref, num_ref, prefix_ref, win_ref, mix_ref):
    first, second = pick((FEAT, ROWS), 1)
    scale, add_first, add_second = weights_of((1, ROWS), 1, True)
    q = pack_ref[:, 256 : 256 + FEAT]
    phi = (dot(q, first) + add_first) * (dot(q, second) + add_second) * scale
    prefix = jnp.concatenate([prefix_ref[i, :, :].astype(F32) for i in range(4)], axis=0).astype(BF)
    numerator = num_ref[...] + dot(phi.astype(BF), prefix)
    mean = jnp.mean(numerator * numerator, axis=1, keepdims=True)
    mix_ref[:, :128] = (numerator * lax.rsqrt(mean + EPS)).astype(BF)
    mix_ref[:, 128:] = win_ref[...]


def output_kernel(core_ref, mix_ref, w_ref, mix2_ref, w2_ref, sum_ref):
    for y in range(4):
        at = pl.multiple_of((2 * y + core_ref[0]) * 256, 256)
        total = dot(mix_ref[...], w_ref[:, pl.ds(at, 256)]) + dot(mix2_ref[...], w2_ref[:, pl.ds(at, 256)])
        sum_ref[y, :, :] = total.astype(BF)


def total_kernel(got_ref, out_ref):
    total = got_ref[0, :, :].astype(F32)
    for i in range(1, 4):
        total = total + got_ref[i, :, :].astype(F32)
    total = total.astype(BF)
    for z in range(16):
        out_ref[z, :, :] = total


def prefix_kernel(place_ref, got_ref, totals_ref, out_ref):
    state = jnp.zeros((QUARTER, 128), F32)
    for z in range(15):
        state = state + jnp.where(z < place_ref[0], totals_ref[z, :, :].astype(F32), 0.0)
    for i in range(4):
        out_ref[i, :, :] = state.astype(BF)
        state = state + got_ref[i, :, :].astype(F32)


def shards(tokens, gain, w_feat, w_value, w_window, w_out):
    count = tokens.shape[0]
    head = lax.axis_index("head")
    ctx = lax.axis_index("ctx")
    core = (head % 2).astype(jnp.int32).reshape(1)
    along_y = [[2 * y + c for y in range(4)] for c in range(2)]

    def across(value):
        return lax.ppermute(value, "head", [(h, h ^ 1) for h in range(8)])

    def shape(dims, kind=BF):
        return jax.ShapeDtypeStruct(dims, kind)

    half = count // 2
    vmem, hbm = pl.BlockSpec(memory_space=pltpu.VMEM), pl.BlockSpec(memory_space=pltpu.HBM)
    done = []
    for part in range(2):
        rows = tokens[half * part : half * (part + 1)]
        spread = lax.all_to_all(
            jnp.broadcast_to(rows[None], (4,) + rows.shape), "head", 0, 0, tiled=True, axis_index_groups=along_y
        )
        if part == 1:
            w_later, done[3] = lax.optimization_barrier((w_out, done[3]))
            w_other = across(w_later)
            spread, done[3] = lax.optimization_barrier((spread, done[3]))
        other = across(spread)
        done = list(pl.pallas_call(
            project_kernel,
            out_shape=[
                shape((count, 384)),
                shape((count, 256)),
                shape((4, QUARTER, 128)) if part else shape((ROWS, 128), F32),
                shape((8, 128), F32),
            ],
            in_specs=[pl.BlockSpec(memory_space=pltpu.SMEM), vmem, vmem, vmem, hbm, vmem, vmem]
            + ([hbm, hbm, vmem, vmem] if part else []),
            out_specs=[hbm, hbm, vmem, vmem],
            input_output_aliases={7: 0, 8: 1} if part else {},
            scratch_shapes=[
                pltpu.VMEM((half, 2048), BF),
                pltpu.VMEM((32, 2048), BF),
                pltpu.VMEM((half, 384), BF),
                pltpu.VMEM((half, 256), BF),
                pltpu.SemaphoreType.DMA((3,)),
            ],
            compiler_params=pltpu.CompilerParams(vmem_limit_bytes=VMEM),
        )(core, spread, other, gain.reshape(1, -1), w_feat.T, w_value, w_window, *done))
    pack, rim, states, _ = done
    in_x = [[4 * z + x for x in range(4)] for z in range(16)]
    in_z = [[4 * z + x for z in range(16)] for x in range(4)]
    quarters = lax.all_to_all(states, "ctx", 0, 0, tiled=True, axis_index_groups=in_x)
    rim, quarters = lax.optimization_barrier((rim, quarters))
    totals = lax.all_to_all(
        call(total_kernel, shape((16, QUARTER, 128)))(quarters), "ctx", 0, 0, tiled=True, axis_index_groups=in_z
    )
    prev = lax.ppermute(rim, "ctx", [(b, b + 1) for b in range(63)])
    numerator = call(inner_kernel, shape((count, 128), F32))(pack)
    win_out = call_with_scalar(attend_kernel, shape((count, 128)), 3)(ctx.astype(jnp.int32).reshape(1), pack, rim, prev)
    sums = call_with_scalar(prefix_kernel, shape((4, QUARTER, 128)), 2)(
        (ctx // 4).astype(jnp.int32).reshape(1), quarters, totals
    )
    sums, numerator, win_out = lax.optimization_barrier((sums, numerator, win_out))
    prefix = lax.all_to_all(sums, "ctx", 0, 0, tiled=True, axis_index_groups=in_x)
    mix = call(linear_kernel, shape((count, 256)))(pack, numerator, prefix, win_out)
    summed = call_with_scalar(output_kernel, shape((4, count, 256)), 4)(core, mix, w_out, across(mix), w_other)
    parts = lax.all_to_all(summed, "head", 0, 0, tiled=True, axis_index_groups=along_y)
    return jnp.sum(parts.astype(F32), axis=0).astype(BF)


def solution(mesh):
    placed = (P("ctx", "head"), P(), P(None, "head"), P(None, "head"), P(None, "head"), P("head", None))
    return jax.shard_map(shards, mesh=mesh, in_specs=placed, out_specs=P("ctx", "head"), check_vma=False)
```

```python
import functools
import math

import jax
import jax.numpy as jnp
from jax import lax
from jax.experimental import pallas as pl
from jax.experimental.pallas import tpu as pltpu
from jax.sharding import PartitionSpec as P

EPS = 1e-05
FEAT = 16
QUARTER = 40
ROWS = 4 * QUARTER
BF = jnp.bfloat16
F32 = jnp.float32
VMEM = 12 * 1024 * 1024


def call(kernel, outs, scratch=()):
    return pl.pallas_call(
        kernel,
        out_shape=outs,
        scratch_shapes=scratch,
        compiler_params=pltpu.CompilerParams(vmem_limit_bytes=VMEM),
    )


def call_with_scalar(kernel, outs, count):
    return pl.pallas_call(
        kernel,
        out_shape=outs,
        in_specs=[pl.BlockSpec(memory_space=pltpu.SMEM)] + [pl.BlockSpec(memory_space=pltpu.VMEM)] * count,
        compiler_params=pltpu.CompilerParams(vmem_limit_bytes=VMEM),
    )


def pick(shape, axis):
    r = lax.broadcasted_iota(jnp.int32, shape, axis)
    u = lax.broadcasted_iota(jnp.int32, shape, 1 - axis)
    first = (r >= 1) & (r <= FEAT) & (u == r - 1)
    second = jnp.zeros(shape, jnp.bool_)
    base = 1 + FEAT
    for i in range(FEAT):
        width = FEAT - i
        inside = (r >= base) & (r < base + width)
        first = first | (inside & (u == i))
        second = second | (inside & (u == i + r - base))
        base += width
    return first.astype(F32).astype(BF), second.astype(F32).astype(BF)


def weights_of(shape, axis, twice):
    r = lax.broadcasted_iota(jnp.int32, shape, axis)
    scale = jnp.where(r == 0, 1.0, jnp.where(r <= FEAT, 0.5, 1.0 / (4.0 * math.sqrt(2.0))))
    if twice:
        base = 1 + FEAT
        square = jnp.zeros(shape, jnp.bool_)
        for i in range(FEAT):
            square = square | (r == base)
            base += FEAT - i
        scale = jnp.where((r > FEAT) & ~square, 2.0 * scale, scale)
    one_first = jnp.where(r == 0, 1.0, 0.0)
    one_second = jnp.where(r <= FEAT, 1.0, 0.0)
    return scale, one_first, one_second


NT = (((1,), (1,)), ((), ()))
NN = (((1,), (0,)), ((), ()))


def dot(a, b, dims=NN):
    return lax.dot_general(a, b, dims, preferred_element_type=F32)


def gather_products(flip, core_ref, x_ref, gain_ref, wf_ref, wv_ref, ww_ref):
    squares = feats = values = windowed = 0.0
    for y in range(4):
        at = pl.multiple_of((2 * y + (core_ref[0] + flip) % 2) * 256, 256)
        x = x_ref[y, :, :].astype(F32)
        squares = squares + x * x
        scaled = (x * gain_ref[0:1, pl.ds(at, 256)]).astype(BF)
        feats = feats + dot(scaled, wf_ref[:, pl.ds(at, 256)], NT)
        values = values + dot(scaled, wv_ref[pl.ds(at, 256), :])
        windowed = windowed + dot(scaled, ww_ref[pl.ds(at, 256), :])
    return jnp.sum(squares, axis=1, keepdims=True), feats, values, windowed


def begin_kernel(core_ref, x_ref, gain_ref, wf_ref, wv_ref, ww_ref, held_ref):
    squares, feats, values, windowed = gather_products(0, core_ref, x_ref, gain_ref, wf_ref, wv_ref, ww_ref)
    held_ref[:, :256] = values
    held_ref[:, 256:512] = windowed
    held_ref[:, 512:544] = feats
    held_ref[:, 544:] = jnp.broadcast_to(squares, (squares.shape[0], 96))


def project_kernel(core_ref, x_ref, gain_ref, wf_ref, wv_ref, ww_ref, held_ref, pack_ref, rim_ref, state_ref):
    count = x_ref.shape[1]
    squares, feats, values, windowed = gather_products(1, core_ref, x_ref, gain_ref, wf_ref, wv_ref, ww_ref)
    scale = lax.rsqrt((squares + held_ref[:, 544:545]) * (1.0 / 2048.0) + EPS)
    values = ((values + held_ref[:, :256]) * scale).astype(BF)
    windowed = ((windowed + held_ref[:, 256:512]) * scale).astype(BF)
    feats = ((feats + held_ref[:, 512:544]) * scale).astype(BF)
    rim_ref[:, :128] = windowed[:, 128:]
    rim_ref[:, 128:] = values[:, 128:]
    vlin = values[:, :128]
    pack_ref[:, :128] = windowed[:, :128]
    pack_ref[:, 128:256] = vlin
    pack_ref[:, 256:288] = feats
    pack_ref[:, 288:] = jnp.zeros((count, 96), BF)
    first, second = pick((ROWS, FEAT), 0)
    scale, add_first, add_second = weights_of((ROWS, 1), 0, False)
    k = feats[:, FEAT:]
    phi = (dot(first, k, NT) + add_first) * (dot(second, k, NT) + add_second) * scale
    state = dot(phi.astype(BF), vlin)
    for i in range(4):
        state_ref[i, :, :] = state[QUARTER * i : QUARTER * (i + 1), :].astype(BF)


def inner_kernel(pack_ref, after_ref, num_ref):
    count = pack_ref.shape[0]
    tile = 256
    for t in range(count // tile):
        ql = pack_ref[t * tile : (t + 1) * tile, 256 : 256 + FEAT]
        kl = pack_ref[: (t + 1) * tile, 256 + FEAT : 256 + 2 * FEAT]
        inner = dot(ql, kl, NT)
        width = kl.shape[0]
        row = lax.broadcasted_iota(jnp.int32, (tile, width), 0) + t * tile
        col = lax.broadcasted_iota(jnp.int32, (tile, width), 1)
        series = 1.0 + inner * 0.25 + inner * inner * (1.0 / 32.0)
        weight = jnp.where(row >= col, series, 0.0).astype(BF)
        num_ref[t * tile : (t + 1) * tile, :] = dot(weight, pack_ref[: (t + 1) * tile, 128:256])


def attend_kernel(first_ref, pack_ref, own_ref, prev_ref, win_ref):
    count = pack_ref.shape[0]
    tile = 256
    no_prev = first_ref[0] == 0
    for t in range(count // tile):
        q = pack_ref[t * tile : (t + 1) * tile, :128]
        old = prev_ref[t * tile :, :]
        new = own_ref[: (t + 1) * tile, :]
        keys = jnp.concatenate([old[:, :128], new[:, :128]], axis=0)
        vals = jnp.concatenate([old[:, 128:], new[:, 128:]], axis=0)
        width = keys.shape[0]
        scores = dot(q, keys, NT) * (1.0 / math.sqrt(128.0))
        at = lax.broadcasted_iota(jnp.int32, (tile, width), 0) + count
        key = lax.broadcasted_iota(jnp.int32, (tile, width), 1)
        least = jnp.where(no_prev, count - t * tile, 0)
        allowed = (key <= at) & (key > at - count) & (key >= least)
        scores = jnp.where(allowed, scores, -1e30)
        lifted = jnp.exp(scores - jnp.max(scores, axis=1, keepdims=True))
        probs = (lifted / jnp.sum(lifted, axis=1, keepdims=True)).astype(BF)
        win_ref[t * tile : (t + 1) * tile, :] = dot(probs, vals).astype(BF)


def linear_kernel(pack_ref, num_ref, prefix_ref, win_ref, mix_ref):
    first, second = pick((FEAT, ROWS), 1)
    scale, add_first, add_second = weights_of((1, ROWS), 1, True)
    q = pack_ref[:, 256 : 256 + FEAT]
    phi = (dot(q, first) + add_first) * (dot(q, second) + add_second) * scale
    prefix = jnp.concatenate([prefix_ref[i, :, :].astype(F32) for i in range(4)], axis=0).astype(BF)
    numerator = num_ref[...] + dot(phi.astype(BF), prefix)
    mean = jnp.mean(numerator * numerator, axis=1, keepdims=True)
    mix_ref[:, :128] = (numerator * lax.rsqrt(mean + EPS)).astype(BF)
    mix_ref[:, 128:] = win_ref[...]


def own_kernel(core_ref, mix_ref, w_ref, sum_ref):
    for y in range(4):
        at = pl.multiple_of((2 * y + core_ref[0]) * 256, 256)
        sum_ref[y, :, :] = dot(mix_ref[...], w_ref[:, pl.ds(at, 256)])


def output_kernel(core_ref, mix_ref, w_ref, own_ref, sum_ref):
    for y in range(4):
        at = pl.multiple_of((2 * y + core_ref[0]) * 256, 256)
        sum_ref[y, :, :] = (own_ref[y, :, :] + dot(mix_ref[...], w_ref[:, pl.ds(at, 256)])).astype(BF)


def total_kernel(got_ref, out_ref):
    total = got_ref[0, :, :].astype(F32)
    for i in range(1, 4):
        total = total + got_ref[i, :, :].astype(F32)
    total = total.astype(BF)
    for z in range(16):
        out_ref[z, :, :] = total


def prefix_kernel(place_ref, got_ref, totals_ref, out_ref):
    state = jnp.zeros((QUARTER, 128), F32)
    for z in range(15):
        state = state + jnp.where(z < place_ref[0], totals_ref[z, :, :].astype(F32), 0.0)
    for i in range(4):
        out_ref[i, :, :] = state.astype(BF)
        state = state + got_ref[i, :, :].astype(F32)


def shards(tokens, gain, w_feat, w_value, w_window, w_out):
    count = tokens.shape[0]
    head = lax.axis_index("head")
    ctx = lax.axis_index("ctx")
    core = (head % 2).astype(jnp.int32).reshape(1)
    along_y = [[2 * y + c for y in range(4)] for c in range(2)]

    def across(value):
        return lax.ppermute(value, "head", [(h, h ^ 1) for h in range(8)])

    def shape(dims, kind=BF):
        return jax.ShapeDtypeStruct(dims, kind)

    spread = lax.all_to_all(
        jnp.broadcast_to(tokens[None], (4,) + tokens.shape), "head", 0, 0, tiled=True, axis_index_groups=along_y
    )
    other = across(spread)
    weights = (gain.reshape(1, -1), w_feat.T, w_value, w_window)
    held = call_with_scalar(begin_kernel, shape((count, 640), F32), 5)(core, spread, *weights)
    pack, rim, states = call_with_scalar(
        project_kernel, [shape((count, 384)), shape((count, 256)), shape((4, QUARTER, 128))], 6
    )(core, other, *weights, held)
    in_x = [[4 * z + x for x in range(4)] for z in range(16)]
    in_z = [[4 * z + x for z in range(16)] for x in range(4)]
    quarters = lax.all_to_all(states, "ctx", 0, 0, tiled=True, axis_index_groups=in_x)
    rim, quarters = lax.optimization_barrier((rim, quarters))
    totals = lax.all_to_all(
        call(total_kernel, shape((16, QUARTER, 128)))(quarters), "ctx", 0, 0, tiled=True, axis_index_groups=in_z
    )
    prev = lax.ppermute(rim, "ctx", [(b, b + 1) for b in range(63)])
    numerator = call(inner_kernel, shape((count, 128), F32))(pack, quarters)
    w_later, prev = lax.optimization_barrier((w_out, prev))
    w_other = across(w_later)
    win_out = call_with_scalar(attend_kernel, shape((count, 128)), 3)(ctx.astype(jnp.int32).reshape(1), pack, rim, prev)
    sums = call_with_scalar(prefix_kernel, shape((4, QUARTER, 128)), 2)(
        (ctx // 4).astype(jnp.int32).reshape(1), quarters, totals
    )
    sums, numerator, win_out = lax.optimization_barrier((sums, numerator, win_out))
    prefix = lax.all_to_all(sums, "ctx", 0, 0, tiled=True, axis_index_groups=in_x)
    mix = call(linear_kernel, shape((count, 256)))(pack, numerator, prefix, win_out)
    own = call_with_scalar(own_kernel, shape((4, count, 256), F32), 2)(core, mix, w_out)
    summed = call_with_scalar(output_kernel, shape((4, count, 256)), 3)(core, across(mix), w_other, own)
    parts = lax.all_to_all(summed, "head", 0, 0, tiled=True, axis_index_groups=along_y)
    return jnp.sum(parts.astype(F32), axis=0).astype(BF)


def solution(mesh):
    placed = (P("ctx", "head"), P(), P(None, "head"), P(None, "head"), P(None, "head"), P("head", None))
    return jax.shard_map(shards, mesh=mesh, in_specs=placed, out_specs=P("ctx", "head"), check_vma=False)
```

```python
import functools
import math

import jax
import jax.numpy as jnp
from jax import lax
from jax.experimental import pallas as pl
from jax.experimental.pallas import tpu as pltpu
from jax.sharding import PartitionSpec as P

EPS = 1e-05
FEAT = 16
QUARTER = 40
ROWS = 4 * QUARTER
BF = jnp.bfloat16
F32 = jnp.float32
VMEM = 12 * 1024 * 1024


def call(kernel, outs, scratch=()):
    return pl.pallas_call(
        kernel,
        out_shape=outs,
        scratch_shapes=scratch,
        compiler_params=pltpu.CompilerParams(vmem_limit_bytes=VMEM),
    )


def call_with_scalar(kernel, outs, count):
    return pl.pallas_call(
        kernel,
        out_shape=outs,
        in_specs=[pl.BlockSpec(memory_space=pltpu.SMEM)] + [pl.BlockSpec(memory_space=pltpu.VMEM)] * count,
        compiler_params=pltpu.CompilerParams(vmem_limit_bytes=VMEM),
    )


def pick(shape, axis):
    r = lax.broadcasted_iota(jnp.int32, shape, axis)
    u = lax.broadcasted_iota(jnp.int32, shape, 1 - axis)
    first = (r >= 1) & (r <= FEAT) & (u == r - 1)
    second = jnp.zeros(shape, jnp.bool_)
    base = 1 + FEAT
    for i in range(FEAT):
        width = FEAT - i
        inside = (r >= base) & (r < base + width)
        first = first | (inside & (u == i))
        second = second | (inside & (u == i + r - base))
        base += width
    return first.astype(F32).astype(BF), second.astype(F32).astype(BF)


def weights_of(shape, axis, twice):
    r = lax.broadcasted_iota(jnp.int32, shape, axis)
    scale = jnp.where(r == 0, 1.0, jnp.where(r <= FEAT, 0.5, 1.0 / (4.0 * math.sqrt(2.0))))
    if twice:
        base = 1 + FEAT
        square = jnp.zeros(shape, jnp.bool_)
        for i in range(FEAT):
            square = square | (r == base)
            base += FEAT - i
        scale = jnp.where((r > FEAT) & ~square, 2.0 * scale, scale)
    one_first = jnp.where(r == 0, 1.0, 0.0)
    one_second = jnp.where(r <= FEAT, 1.0, 0.0)
    return scale, one_first, one_second


NT = (((1,), (1,)), ((), ()))
NN = (((1,), (0,)), ((), ()))


def dot(a, b, dims=NN):
    return lax.dot_general(a, b, dims, preferred_element_type=F32)


def gather_products(flip, core_ref, x_ref, gain_ref, wf_ref, wv_ref, ww_ref):
    squares = feats = values = windowed = 0.0
    for y in range(4):
        at = pl.multiple_of((2 * y + (core_ref[0] + flip) % 2) * 256, 256)
        x = x_ref[y, :, :].astype(F32)
        squares = squares + x * x
        scaled = (x * gain_ref[0:1, pl.ds(at, 256)]).astype(BF)
        feats = feats + dot(scaled, wf_ref[:, pl.ds(at, 256)], NT)
        values = values + dot(scaled, wv_ref[pl.ds(at, 256), :])
        windowed = windowed + dot(scaled, ww_ref[pl.ds(at, 256), :])
    return jnp.sum(squares, axis=1, keepdims=True), feats, values, windowed


def begin_kernel(core_ref, x_ref, gain_ref, wf_ref, wv_ref, ww_ref, held_ref):
    squares, feats, values, windowed = gather_products(0, core_ref, x_ref, gain_ref, wf_ref, wv_ref, ww_ref)
    held_ref[:, :256] = values
    held_ref[:, 256:512] = windowed
    held_ref[:, 512:544] = feats
    held_ref[:, 544:] = jnp.broadcast_to(squares, (squares.shape[0], 96))


def project_kernel(core_ref, x_ref, gain_ref, wf_ref, wv_ref, ww_ref, held_ref, pack_ref, rim_ref, state_ref):
    count = x_ref.shape[1]
    squares, feats, values, windowed = gather_products(1, core_ref, x_ref, gain_ref, wf_ref, wv_ref, ww_ref)
    scale = lax.rsqrt((squares + held_ref[:, 544:545]) * (1.0 / 2048.0) + EPS)
    values = ((values + held_ref[:, :256]) * scale).astype(BF)
    windowed = ((windowed + held_ref[:, 256:512]) * scale).astype(BF)
    feats = ((feats + held_ref[:, 512:544]) * scale).astype(BF)
    rim_ref[:, :128] = windowed[:, 128:]
    rim_ref[:, 128:] = values[:, 128:]
    vlin = values[:, :128]
    pack_ref[:, :128] = windowed[:, :128]
    pack_ref[:, 128:256] = vlin
    pack_ref[:, 256:288] = feats
    pack_ref[:, 288:] = jnp.zeros((count, 96), BF)
    first, second = pick((ROWS, FEAT), 0)
    scale, add_first, add_second = weights_of((ROWS, 1), 0, False)
    k = feats[:, FEAT:]
    phi = (dot(first, k, NT) + add_first) * (dot(second, k, NT) + add_second) * scale
    state = dot(phi.astype(BF), vlin)
    for i in range(4):
        state_ref[i, :, :] = state[QUARTER * i : QUARTER * (i + 1), :].astype(BF)


def inner_kernel(pack_ref, after_ref, num_ref):
    count = pack_ref.shape[0]
    tile = 256
    for t in range(count // tile):
        ql = pack_ref[t * tile : (t + 1) * tile, 256 : 256 + FEAT]
        kl = pack_ref[: (t + 1) * tile, 256 + FEAT : 256 + 2 * FEAT]
        inner = dot(ql, kl, NT)
        width = kl.shape[0]
        row = lax.broadcasted_iota(jnp.int32, (tile, width), 0) + t * tile
        col = lax.broadcasted_iota(jnp.int32, (tile, width), 1)
        series = 1.0 + inner * 0.25 + inner * inner * (1.0 / 32.0)
        weight = jnp.where(row >= col, series, 0.0).astype(BF)
        num_ref[t * tile : (t + 1) * tile, :] = dot(weight, pack_ref[: (t + 1) * tile, 128:256])


def attend_kernel(first_ref, pack_ref, own_ref, prev_ref, win_ref):
    count = pack_ref.shape[0]
    tile = 256
    no_prev = first_ref[0] == 0
    for t in range(count // tile):
        q = pack_ref[t * tile : (t + 1) * tile, :128]
        old = prev_ref[t * tile :, :]
        new = own_ref[: (t + 1) * tile, :]
        keys = jnp.concatenate([old[:, :128], new[:, :128]], axis=0)
        vals = jnp.concatenate([old[:, 128:], new[:, 128:]], axis=0)
        width = keys.shape[0]
        scores = dot(q, keys, NT) * (1.0 / math.sqrt(128.0))
        at = lax.broadcasted_iota(jnp.int32, (tile, width), 0) + count
        key = lax.broadcasted_iota(jnp.int32, (tile, width), 1)
        least = jnp.where(no_prev, count - t * tile, 0)
        allowed = (key <= at) & (key > at - count) & (key >= least)
        scores = jnp.where(allowed, scores, -1e30)
        lifted = jnp.exp(scores - jnp.max(scores, axis=1, keepdims=True))
        probs = (lifted / jnp.sum(lifted, axis=1, keepdims=True)).astype(BF)
        win_ref[t * tile : (t + 1) * tile, :] = dot(probs, vals).astype(BF)


def linear_kernel(pack_ref, num_ref, prefix_ref, win_ref, mix_ref):
    first, second = pick((FEAT, ROWS), 1)
    scale, add_first, add_second = weights_of((1, ROWS), 1, True)
    q = pack_ref[:, 256 : 256 + FEAT]
    phi = (dot(q, first) + add_first) * (dot(q, second) + add_second) * scale
    prefix = jnp.concatenate([prefix_ref[i, :, :].astype(F32) for i in range(4)], axis=0).astype(BF)
    numerator = num_ref[...] + dot(phi.astype(BF), prefix)
    mean = jnp.mean(numerator * numerator, axis=1, keepdims=True)
    mix_ref[:, :128] = (numerator * lax.rsqrt(mean + EPS)).astype(BF)
    mix_ref[:, 128:] = win_ref[...]


def own_kernel(core_ref, mix_ref, w_ref, sum_ref):
    for y in range(4):
        at = pl.multiple_of((2 * y + core_ref[0]) * 256, 256)
        sum_ref[y, :, :] = dot(mix_ref[...], w_ref[:, pl.ds(at, 256)])


def output_kernel(core_ref, mix_ref, w_ref, own_ref, sum_ref):
    for y in range(4):
        at = pl.multiple_of((2 * y + core_ref[0]) * 256, 256)
        sum_ref[y, :, :] = (own_ref[y, :, :] + dot(mix_ref[...], w_ref[:, pl.ds(at, 256)])).astype(BF)


def total_kernel(got_ref, out_ref):
    total = got_ref[0, :, :].astype(F32)
    for i in range(1, 4):
        total = total + got_ref[i, :, :].astype(F32)
    total = total.astype(BF)
    for z in range(16):
        out_ref[z, :, :] = total


def prefix_kernel(place_ref, got_ref, totals_ref, out_ref):
    state = jnp.zeros((QUARTER, 128), F32)
    for z in range(15):
        state = state + jnp.where(z < place_ref[0], totals_ref[z, :, :].astype(F32), 0.0)
    for i in range(4):
        out_ref[i, :, :] = state.astype(BF)
        state = state + got_ref[i, :, :].astype(F32)


def shards(tokens, gain, w_feat, w_value, w_window, w_out):
    count = tokens.shape[0]
    head = lax.axis_index("head")
    ctx = lax.axis_index("ctx")
    core = (head % 2).astype(jnp.int32).reshape(1)
    along_y = [[2 * y + c for y in range(4)] for c in range(2)]

    def across(value):
        return lax.ppermute(value, "head", [(h, h ^ 1) for h in range(8)])

    def shape(dims, kind=BF):
        return jax.ShapeDtypeStruct(dims, kind)

    spread = lax.all_to_all(
        jnp.broadcast_to(tokens[None], (4,) + tokens.shape), "head", 0, 0, tiled=True, axis_index_groups=along_y
    )
    spread, w_later = lax.optimization_barrier((spread, w_out))
    other = across(spread)
    w_other = across(w_later)
    weights = (gain.reshape(1, -1), w_feat.T, w_value, w_window)
    held = call_with_scalar(begin_kernel, shape((count, 640), F32), 5)(core, spread, *weights)
    pack, rim, states = call_with_scalar(
        project_kernel, [shape((count, 384)), shape((count, 256)), shape((4, QUARTER, 128))], 6
    )(core, other, *weights, held)
    in_x = [[4 * z + x for x in range(4)] for z in range(16)]
    in_z = [[4 * z + x for z in range(16)] for x in range(4)]
    quarters = lax.all_to_all(states, "ctx", 0, 0, tiled=True, axis_index_groups=in_x)
    rim, quarters = lax.optimization_barrier((rim, quarters))
    totals = lax.all_to_all(
        call(total_kernel, shape((16, QUARTER, 128)))(quarters), "ctx", 0, 0, tiled=True, axis_index_groups=in_z
    )
    prev = lax.ppermute(rim, "ctx", [(b, b + 1) for b in range(63)])
    numerator = call(inner_kernel, shape((count, 128), F32))(pack, quarters)
    win_out = call_with_scalar(attend_kernel, shape((count, 128)), 3)(ctx.astype(jnp.int32).reshape(1), pack, rim, prev)
    sums = call_with_scalar(prefix_kernel, shape((4, QUARTER, 128)), 2)(
        (ctx // 4).astype(jnp.int32).reshape(1), quarters, totals
    )
    sums, numerator, win_out = lax.optimization_barrier((sums, numerator, win_out))
    prefix = lax.all_to_all(sums, "ctx", 0, 0, tiled=True, axis_index_groups=in_x)
    mix = call(linear_kernel, shape((count, 256)))(pack, numerator, prefix, win_out)
    own = call_with_scalar(own_kernel, shape((4, count, 256), F32), 2)(core, mix, w_out)
    summed = call_with_scalar(output_kernel, shape((4, count, 256)), 3)(core, across(mix), w_other, own)
    parts = lax.all_to_all(summed, "head", 0, 0, tiled=True, axis_index_groups=along_y)
    return jnp.sum(parts.astype(F32), axis=0).astype(BF)


def solution(mesh):
    placed = (P("ctx", "head"), P(), P(None, "head"), P(None, "head"), P(None, "head"), P("head", None))
    return jax.shard_map(shards, mesh=mesh, in_specs=placed, out_specs=P("ctx", "head"), check_vma=False)
```

```python
import functools
import math

import jax
import jax.numpy as jnp
from jax import lax
from jax.experimental import pallas as pl
from jax.experimental.pallas import tpu as pltpu
from jax.sharding import PartitionSpec as P

EPS = 1e-05
FEAT = 16
QUARTER = 40
ROWS = 4 * QUARTER
BF = jnp.bfloat16
F32 = jnp.float32
VMEM = 12 * 1024 * 1024


def call(kernel, outs, scratch=()):
    return pl.pallas_call(
        kernel,
        out_shape=outs,
        scratch_shapes=scratch,
        compiler_params=pltpu.CompilerParams(vmem_limit_bytes=VMEM),
    )


def call_with_scalar(kernel, outs, count):
    return pl.pallas_call(
        kernel,
        out_shape=outs,
        in_specs=[pl.BlockSpec(memory_space=pltpu.SMEM)] + [pl.BlockSpec(memory_space=pltpu.VMEM)] * count,
        compiler_params=pltpu.CompilerParams(vmem_limit_bytes=VMEM),
    )


def pick(shape, axis):
    r = lax.broadcasted_iota(jnp.int32, shape, axis)
    u = lax.broadcasted_iota(jnp.int32, shape, 1 - axis)
    first = (r >= 1) & (r <= FEAT) & (u == r - 1)
    second = jnp.zeros(shape, jnp.bool_)
    base = 1 + FEAT
    for i in range(FEAT):
        width = FEAT - i
        inside = (r >= base) & (r < base + width)
        first = first | (inside & (u == i))
        second = second | (inside & (u == i + r - base))
        base += width
    return first.astype(F32).astype(BF), second.astype(F32).astype(BF)


def weights_of(shape, axis, twice):
    r = lax.broadcasted_iota(jnp.int32, shape, axis)
    scale = jnp.where(r == 0, 1.0, jnp.where(r <= FEAT, 0.5, 1.0 / (4.0 * math.sqrt(2.0))))
    if twice:
        base = 1 + FEAT
        square = jnp.zeros(shape, jnp.bool_)
        for i in range(FEAT):
            square = square | (r == base)
            base += FEAT - i
        scale = jnp.where((r > FEAT) & ~square, 2.0 * scale, scale)
    one_first = jnp.where(r == 0, 1.0, 0.0)
    one_second = jnp.where(r <= FEAT, 1.0, 0.0)
    return scale, one_first, one_second


NT = (((1,), (1,)), ((), ()))
NN = (((1,), (0,)), ((), ()))


def dot(a, b, dims=NN):
    return lax.dot_general(a, b, dims, preferred_element_type=F32)


def gather_products(flip, core_ref, x_ref, gain_ref, wf_ref, wv_ref, ww_ref):
    squares = feats = values = windowed = 0.0
    for y in range(4):
        at = pl.multiple_of((2 * y + (core_ref[0] + flip) % 2) * 256, 256)
        x = x_ref[y, :, :].astype(F32)
        squares = squares + x * x
        scaled = (x * gain_ref[0:1, pl.ds(at, 256)]).astype(BF)
        feats = feats + dot(scaled, wf_ref[:, pl.ds(at, 256)], NT)
        values = values + dot(scaled, wv_ref[pl.ds(at, 256), :])
        windowed = windowed + dot(scaled, ww_ref[pl.ds(at, 256), :])
    return jnp.sum(squares, axis=1, keepdims=True), feats, values, windowed


def begin_kernel(core_ref, x_ref, gain_ref, wf_ref, wv_ref, ww_ref, held_ref):
    squares, feats, values, windowed = gather_products(0, core_ref, x_ref, gain_ref, wf_ref, wv_ref, ww_ref)
    held_ref[:, :256] = values
    held_ref[:, 256:512] = windowed
    held_ref[:, 512:544] = feats
    held_ref[:, 544:] = jnp.broadcast_to(squares, (squares.shape[0], 96))


def project_kernel(core_ref, x_ref, gain_ref, wf_ref, wv_ref, ww_ref, held_ref, pack_ref, rim_ref, state_ref):
    count = x_ref.shape[1]
    squares, feats, values, windowed = gather_products(1, core_ref, x_ref, gain_ref, wf_ref, wv_ref, ww_ref)
    scale = lax.rsqrt((squares + held_ref[:, 544:545]) * (1.0 / 2048.0) + EPS)
    values = ((values + held_ref[:, :256]) * scale).astype(BF)
    windowed = ((windowed + held_ref[:, 256:512]) * scale).astype(BF)
    feats = ((feats + held_ref[:, 512:544]) * scale).astype(BF)
    rim_ref[:, :128] = windowed[:, 128:]
    rim_ref[:, 128:] = values[:, 128:]
    vlin = values[:, :128]
    pack_ref[:, :128] = windowed[:, :128]
    pack_ref[:, 128:256] = vlin
    pack_ref[:, 256:288] = feats
    pack_ref[:, 288:] = jnp.zeros((count, 96), BF)
    first, second = pick((ROWS, FEAT), 0)
    scale, add_first, add_second = weights_of((ROWS, 1), 0, False)
    k = feats[:, FEAT:]
    phi = (dot(first, k, NT) + add_first) * (dot(second, k, NT) + add_second) * scale
    state = dot(phi.astype(BF), vlin)
    for i in range(4):
        state_ref[i, :, :] = state[QUARTER * i : QUARTER * (i + 1), :].astype(BF)


def inner_kernel(pack_ref, after_ref, num_ref):
    count = pack_ref.shape[0]
    tile = 256
    for t in range(count // tile):
        ql = pack_ref[t * tile : (t + 1) * tile, 256 : 256 + FEAT]
        kl = pack_ref[: (t + 1) * tile, 256 + FEAT : 256 + 2 * FEAT]
        inner = dot(ql, kl, NT)
        width = kl.shape[0]
        row = lax.broadcasted_iota(jnp.int32, (tile, width), 0) + t * tile
        col = lax.broadcasted_iota(jnp.int32, (tile, width), 1)
        series = 1.0 + inner * 0.25 + inner * inner * (1.0 / 32.0)
        weight = jnp.where(row >= col, series, 0.0).astype(BF)
        num_ref[t * tile : (t + 1) * tile, :] = dot(weight, pack_ref[: (t + 1) * tile, 128:256])


def attend_kernel(first_ref, pack_ref, own_ref, prev_ref, win_ref):
    count = pack_ref.shape[0]
    tile = 256
    no_prev = first_ref[0] == 0
    for t in range(count // tile):
        q = pack_ref[t * tile : (t + 1) * tile, :128]
        old = prev_ref[t * tile :, :]
        new = own_ref[: (t + 1) * tile, :]
        keys = jnp.concatenate([old[:, :128], new[:, :128]], axis=0)
        vals = jnp.concatenate([old[:, 128:], new[:, 128:]], axis=0)
        width = keys.shape[0]
        scores = dot(q, keys, NT) * (1.0 / math.sqrt(128.0))
        at = lax.broadcasted_iota(jnp.int32, (tile, width), 0) + count
        key = lax.broadcasted_iota(jnp.int32, (tile, width), 1)
        least = jnp.where(no_prev, count - t * tile, 0)
        allowed = (key <= at) & (key > at - count) & (key >= least)
        scores = jnp.where(allowed, scores, -1e30)
        lifted = jnp.exp(scores - jnp.max(scores, axis=1, keepdims=True))
        probs = (lifted / jnp.sum(lifted, axis=1, keepdims=True)).astype(BF)
        win_ref[t * tile : (t + 1) * tile, :] = dot(probs, vals).astype(BF)


def linear_kernel(pack_ref, num_ref, prefix_ref, win_ref, mix_ref):
    first, second = pick((FEAT, ROWS), 1)
    scale, add_first, add_second = weights_of((1, ROWS), 1, True)
    q = pack_ref[:, 256 : 256 + FEAT]
    phi = (dot(q, first) + add_first) * (dot(q, second) + add_second) * scale
    prefix = jnp.concatenate([prefix_ref[i, :, :].astype(F32) for i in range(4)], axis=0).astype(BF)
    numerator = num_ref[...] + dot(phi.astype(BF), prefix)
    mean = jnp.mean(numerator * numerator, axis=1, keepdims=True)
    mix_ref[:, :128] = (numerator * lax.rsqrt(mean + EPS)).astype(BF)
    mix_ref[:, 128:] = win_ref[...]


def pick_kernel(core_ref, w_ref, after_ref, out_ref):
    for y in range(4):
        at = pl.multiple_of((2 * y + 1 - core_ref[0]) * 256, 256)
        out_ref[y, :, :] = w_ref[:, pl.ds(at, 256)]


def own_kernel(core_ref, mix_ref, w_ref, sum_ref):
    for y in range(4):
        at = pl.multiple_of((2 * y + core_ref[0]) * 256, 256)
        sum_ref[y, :, :] = dot(mix_ref[...], w_ref[:, pl.ds(at, 256)])


def output_kernel(mix_ref, w_ref, own_ref, sum_ref):
    for y in range(4):
        sum_ref[y, :, :] = (own_ref[y, :, :] + dot(mix_ref[...], w_ref[y, :, :])).astype(BF)


def total_kernel(got_ref, out_ref):
    total = got_ref[0, :, :].astype(F32)
    for i in range(1, 4):
        total = total + got_ref[i, :, :].astype(F32)
    total = total.astype(BF)
    for z in range(16):
        out_ref[z, :, :] = total


def prefix_kernel(place_ref, got_ref, totals_ref, out_ref):
    state = jnp.zeros((QUARTER, 128), F32)
    for z in range(15):
        state = state + jnp.where(z < place_ref[0], totals_ref[z, :, :].astype(F32), 0.0)
    for i in range(4):
        out_ref[i, :, :] = state.astype(BF)
        state = state + got_ref[i, :, :].astype(F32)


def shards(tokens, gain, w_feat, w_value, w_window, w_out):
    count = tokens.shape[0]
    head = lax.axis_index("head")
    ctx = lax.axis_index("ctx")
    core = (head % 2).astype(jnp.int32).reshape(1)
    along_y = [[2 * y + c for y in range(4)] for c in range(2)]

    def across(value):
        return lax.ppermute(value, "head", [(h, h ^ 1) for h in range(8)])

    def shape(dims, kind=BF):
        return jax.ShapeDtypeStruct(dims, kind)

    spread = lax.all_to_all(
        jnp.broadcast_to(tokens[None], (4,) + tokens.shape), "head", 0, 0, tiled=True, axis_index_groups=along_y
    )
    other = across(spread)
    weights = (gain.reshape(1, -1), w_feat.T, w_value, w_window)
    held = call_with_scalar(begin_kernel, shape((count, 640), F32), 5)(core, spread, *weights)
    pack, rim, states = call_with_scalar(
        project_kernel, [shape((count, 384)), shape((count, 256)), shape((4, QUARTER, 128))], 6
    )(core, other, *weights, held)
    in_x = [[4 * z + x for x in range(4)] for z in range(16)]
    in_z = [[4 * z + x for z in range(16)] for x in range(4)]
    quarters = lax.all_to_all(states, "ctx", 0, 0, tiled=True, axis_index_groups=in_x)
    rim, quarters = lax.optimization_barrier((rim, quarters))
    totals = lax.all_to_all(
        call(total_kernel, shape((16, QUARTER, 128)))(quarters), "ctx", 0, 0, tiled=True, axis_index_groups=in_z
    )
    prev = lax.ppermute(rim, "ctx", [(b, b + 1) for b in range(63)])
    numerator = call(inner_kernel, shape((count, 128), F32))(pack, quarters)
    w_other = across(call_with_scalar(pick_kernel, shape((4, 256, 256)), 2)(core, w_out, quarters))
    win_out = call_with_scalar(attend_kernel, shape((count, 128)), 3)(ctx.astype(jnp.int32).reshape(1), pack, rim, prev)
    sums = call_with_scalar(prefix_kernel, shape((4, QUARTER, 128)), 2)(
        (ctx // 4).astype(jnp.int32).reshape(1), quarters, totals
    )
    sums, numerator, win_out = lax.optimization_barrier((sums, numerator, win_out))
    prefix = lax.all_to_all(sums, "ctx", 0, 0, tiled=True, axis_index_groups=in_x)
    mix = call(linear_kernel, shape((count, 256)))(pack, numerator, prefix, win_out)
    own = call_with_scalar(own_kernel, shape((4, count, 256), F32), 2)(core, mix, w_out)
    summed = call(output_kernel, shape((4, count, 256)))(across(mix), w_other, own)
    parts = lax.all_to_all(summed, "head", 0, 0, tiled=True, axis_index_groups=along_y)
    return jnp.sum(parts.astype(F32), axis=0).astype(BF)


def solution(mesh):
    placed = (P("ctx", "head"), P(), P(None, "head"), P(None, "head"), P(None, "head"), P("head", None))
    return jax.shard_map(shards, mesh=mesh, in_specs=placed, out_specs=P("ctx", "head"), check_vma=False)
```

```python
import functools
import math

import jax
import jax.numpy as jnp
from jax import lax
from jax.experimental import pallas as pl
from jax.experimental.pallas import tpu as pltpu
from jax.sharding import PartitionSpec as P

EPS = 1e-05
FEAT = 16
QUARTER = 40
ROWS = 4 * QUARTER
BF = jnp.bfloat16
F32 = jnp.float32
VMEM = 12 * 1024 * 1024


def call(kernel, outs, scratch=()):
    return pl.pallas_call(
        kernel,
        out_shape=outs,
        scratch_shapes=scratch,
        compiler_params=pltpu.CompilerParams(vmem_limit_bytes=VMEM),
    )


def call_with_scalar(kernel, outs, count):
    return pl.pallas_call(
        kernel,
        out_shape=outs,
        in_specs=[pl.BlockSpec(memory_space=pltpu.SMEM)] + [pl.BlockSpec(memory_space=pltpu.VMEM)] * count,
        compiler_params=pltpu.CompilerParams(vmem_limit_bytes=VMEM),
    )


def pick(shape, axis):
    r = lax.broadcasted_iota(jnp.int32, shape, axis)
    u = lax.broadcasted_iota(jnp.int32, shape, 1 - axis)
    first = (r >= 1) & (r <= FEAT) & (u == r - 1)
    second = jnp.zeros(shape, jnp.bool_)
    base = 1 + FEAT
    for i in range(FEAT):
        width = FEAT - i
        inside = (r >= base) & (r < base + width)
        first = first | (inside & (u == i))
        second = second | (inside & (u == i + r - base))
        base += width
    return first.astype(F32).astype(BF), second.astype(F32).astype(BF)


def weights_of(shape, axis, twice):
    r = lax.broadcasted_iota(jnp.int32, shape, axis)
    scale = jnp.where(r == 0, 1.0, jnp.where(r <= FEAT, 0.5, 1.0 / (4.0 * math.sqrt(2.0))))
    if twice:
        base = 1 + FEAT
        square = jnp.zeros(shape, jnp.bool_)
        for i in range(FEAT):
            square = square | (r == base)
            base += FEAT - i
        scale = jnp.where((r > FEAT) & ~square, 2.0 * scale, scale)
    one_first = jnp.where(r == 0, 1.0, 0.0)
    one_second = jnp.where(r <= FEAT, 1.0, 0.0)
    return scale, one_first, one_second


NT = (((1,), (1,)), ((), ()))
NN = (((1,), (0,)), ((), ()))


def dot(a, b, dims=NN):
    return lax.dot_general(a, b, dims, preferred_element_type=F32)


def gather_products(flip, core_ref, x_ref, gain_ref, wf_ref, wv_ref, ww_ref):
    squares = feats = values = windowed = 0.0
    for y in range(4):
        at = pl.multiple_of((2 * y + (core_ref[0] + flip) % 2) * 256, 256)
        x = x_ref[y, :, :].astype(F32)
        squares = squares + x * x
        scaled = (x * gain_ref[0:1, pl.ds(at, 256)]).astype(BF)
        feats = feats + dot(scaled, wf_ref[:, pl.ds(at, 256)], NT)
        values = values + dot(scaled, wv_ref[pl.ds(at, 256), :])
        windowed = windowed + dot(scaled, ww_ref[pl.ds(at, 256), :])
    return jnp.sum(squares, axis=1, keepdims=True), feats, values, windowed


def begin_kernel(core_ref, x_ref, gain_ref, wf_ref, wv_ref, ww_ref, held_ref):
    squares, feats, values, windowed = gather_products(0, core_ref, x_ref, gain_ref, wf_ref, wv_ref, ww_ref)
    held_ref[:, :256] = values
    held_ref[:, 256:512] = windowed
    held_ref[:, 512:544] = feats
    held_ref[:, 544:] = jnp.broadcast_to(squares, (squares.shape[0], 96))


def project_kernel(core_ref, x_ref, gain_ref, wf_ref, wv_ref, ww_ref, held_ref, pack_ref, rim_ref, state_ref):
    count = x_ref.shape[1]
    squares, feats, values, windowed = gather_products(1, core_ref, x_ref, gain_ref, wf_ref, wv_ref, ww_ref)
    scale = lax.rsqrt((squares + held_ref[:, 544:545]) * (1.0 / 2048.0) + EPS)
    values = ((values + held_ref[:, :256]) * scale).astype(BF)
    windowed = ((windowed + held_ref[:, 256:512]) * scale).astype(BF)
    feats = ((feats + held_ref[:, 512:544]) * scale).astype(BF)
    rim_ref[:, :128] = windowed[:, 128:]
    rim_ref[:, 128:] = values[:, 128:]
    vlin = values[:, :128]
    pack_ref[:, :128] = windowed[:, :128]
    pack_ref[:, 128:256] = vlin
    pack_ref[:, 256:288] = feats
    pack_ref[:, 288:] = jnp.zeros((count, 96), BF)
    first, second = pick((ROWS, FEAT), 0)
    scale, add_first, add_second = weights_of((ROWS, 1), 0, False)
    k = feats[:, FEAT:]
    phi = (dot(first, k, NT) + add_first) * (dot(second, k, NT) + add_second) * scale
    state = dot(phi.astype(BF), vlin)
    for i in range(4):
        state_ref[i, :, :] = state[QUARTER * i : QUARTER * (i + 1), :].astype(BF)


def inner_kernel(pack_ref, after_ref, num_ref):
    count = pack_ref.shape[0]
    tile = 256
    for t in range(count // tile):
        ql = pack_ref[t * tile : (t + 1) * tile, 256 : 256 + FEAT]
        kl = pack_ref[: (t + 1) * tile, 256 + FEAT : 256 + 2 * FEAT]
        inner = dot(ql, kl, NT)
        width = kl.shape[0]
        row = lax.broadcasted_iota(jnp.int32, (tile, width), 0) + t * tile
        col = lax.broadcasted_iota(jnp.int32, (tile, width), 1)
        series = 1.0 + inner * 0.25 + inner * inner * (1.0 / 32.0)
        weight = jnp.where(row >= col, series, 0.0).astype(BF)
        num_ref[t * tile : (t + 1) * tile, :] = dot(weight, pack_ref[: (t + 1) * tile, 128:256])


def attend_kernel(first_ref, pack_ref, own_ref, prev_ref, win_ref):
    count = pack_ref.shape[0]
    tile = 256
    no_prev = first_ref[0] == 0
    for t in range(count // tile):
        q = pack_ref[t * tile : (t + 1) * tile, :128]
        old = prev_ref[t * tile :, :]
        new = own_ref[: (t + 1) * tile, :]
        keys = jnp.concatenate([old[:, :128], new[:, :128]], axis=0)
        vals = jnp.concatenate([old[:, 128:], new[:, 128:]], axis=0)
        width = keys.shape[0]
        scores = dot(q, keys, NT) * (1.0 / math.sqrt(128.0))
        at = lax.broadcasted_iota(jnp.int32, (tile, width), 0) + count
        key = lax.broadcasted_iota(jnp.int32, (tile, width), 1)
        least = jnp.where(no_prev, count - t * tile, 0)
        allowed = (key <= at) & (key > at - count) & (key >= least)
        scores = jnp.where(allowed, scores, -1e30)
        lifted = jnp.exp(scores - jnp.max(scores, axis=1, keepdims=True))
        probs = (lifted / jnp.sum(lifted, axis=1, keepdims=True)).astype(BF)
        win_ref[t * tile : (t + 1) * tile, :] = dot(probs, vals).astype(BF)


def linear_kernel(pack_ref, num_ref, prefix_ref, win_ref, mix_ref):
    first, second = pick((FEAT, ROWS), 1)
    scale, add_first, add_second = weights_of((1, ROWS), 1, True)
    q = pack_ref[:, 256 : 256 + FEAT]
    phi = (dot(q, first) + add_first) * (dot(q, second) + add_second) * scale
    prefix = jnp.concatenate([prefix_ref[i, :, :].astype(F32) for i in range(4)], axis=0).astype(BF)
    numerator = num_ref[...] + dot(phi.astype(BF), prefix)
    mean = jnp.mean(numerator * numerator, axis=1, keepdims=True)
    mix_ref[:, :128] = (numerator * lax.rsqrt(mean + EPS)).astype(BF)
    mix_ref[:, 128:] = win_ref[...]


def pick_kernel(core_ref, w_ref, after_ref, out_ref):
    for y in range(4):
        at = pl.multiple_of((2 * y + 1 - core_ref[0]) * 256, 256)
        out_ref[y, :, :] = w_ref[:, pl.ds(at, 256)]


def own_kernel(core_ref, mix_ref, w_ref, sum_ref):
    for y in range(4):
        at = pl.multiple_of((2 * y + core_ref[0]) * 256, 256)
        sum_ref[y, :, :] = dot(mix_ref[...], w_ref[:, pl.ds(at, 256)])


def output_kernel(mix_ref, w_ref, own_ref, sum_ref):
    for y in range(4):
        sum_ref[y, :, :] = (own_ref[y, :, :] + dot(mix_ref[...], w_ref[y, :, :])).astype(BF)


def total_kernel(got_ref, out_ref):
    total = got_ref[0, :, :].astype(F32)
    for i in range(1, 4):
        total = total + got_ref[i, :, :].astype(F32)
    total = total.astype(BF)
    for z in range(16):
        out_ref[z, :, :] = total


def prefix_kernel(place_ref, got_ref, totals_ref, out_ref):
    state = jnp.zeros((QUARTER, 128), F32)
    for z in range(15):
        state = state + jnp.where(z < place_ref[0], totals_ref[z, :, :].astype(F32), 0.0)
    for i in range(4):
        out_ref[i, :, :] = state.astype(BF)
        state = state + got_ref[i, :, :].astype(F32)


def shards(tokens, gain, w_feat, w_value, w_window, w_out):
    count = tokens.shape[0]
    head = lax.axis_index("head")
    ctx = lax.axis_index("ctx")
    core = (head % 2).astype(jnp.int32).reshape(1)
    along_y = [[2 * y + c for y in range(4)] for c in range(2)]

    def across(value):
        return lax.ppermute(value, "head", [(h, h ^ 1) for h in range(8)])

    def shape(dims, kind=BF):
        return jax.ShapeDtypeStruct(dims, kind)

    spread = lax.all_to_all(
        jnp.broadcast_to(tokens[None], (4,) + tokens.shape), "head", 0, 0, tiled=True, axis_index_groups=along_y
    )
    other = across(spread)
    weights = (gain.reshape(1, -1), w_feat.T, w_value, w_window)
    held = call_with_scalar(begin_kernel, shape((count, 640), F32), 5)(core, spread, *weights)
    pack, rim, states = call_with_scalar(
        project_kernel, [shape((count, 384)), shape((count, 256)), shape((4, QUARTER, 128))], 6
    )(core, other, *weights, held)
    in_x = [[4 * z + x for x in range(4)] for z in range(16)]
    in_z = [[4 * z + x for z in range(16)] for x in range(4)]
    quarters = lax.all_to_all(states, "ctx", 0, 0, tiled=True, axis_index_groups=in_x)
    rim, quarters = lax.optimization_barrier((rim, quarters))
    totals = lax.all_to_all(
        call(total_kernel, shape((16, QUARTER, 128)))(quarters), "ctx", 0, 0, tiled=True, axis_index_groups=in_z
    )
    prev = lax.ppermute(rim, "ctx", [(b, b + 1) for b in range(63)])
    numerator = call(inner_kernel, shape((count, 128), F32))(pack, quarters)
    w_other = across(call_with_scalar(pick_kernel, shape((4, 256, 256)), 2)(core, w_out, quarters))
    win_out = call_with_scalar(attend_kernel, shape((count, 128)), 3)(ctx.astype(jnp.int32).reshape(1), pack, rim, prev)
    sums = call_with_scalar(prefix_kernel, shape((4, QUARTER, 128)), 2)(
        (ctx // 4).astype(jnp.int32).reshape(1), quarters, totals
    )
    sums, numerator = lax.optimization_barrier((sums, numerator))
    prefix = lax.all_to_all(sums, "ctx", 0, 0, tiled=True, axis_index_groups=in_x)
    mix = call(linear_kernel, shape((count, 256)))(pack, numerator, prefix, win_out)
    own = call_with_scalar(own_kernel, shape((4, count, 256), F32), 2)(core, mix, w_out)
    summed = call(output_kernel, shape((4, count, 256)))(across(mix), w_other, own)
    parts = lax.all_to_all(summed, "head", 0, 0, tiled=True, axis_index_groups=along_y)
    return jnp.sum(parts.astype(F32), axis=0).astype(BF)


def solution(mesh):
    placed = (P("ctx", "head"), P(), P(None, "head"), P(None, "head"), P(None, "head"), P("head", None))
    return jax.shard_map(shards, mesh=mesh, in_specs=placed, out_specs=P("ctx", "head"), check_vma=False)
```

```python
import functools
import math

import jax
import jax.numpy as jnp
from jax import lax
from jax.experimental import pallas as pl
from jax.experimental.pallas import tpu as pltpu
from jax.sharding import PartitionSpec as P

EPS = 1e-05
FEAT = 16
QUARTER = 40
ROWS = 4 * QUARTER
BF = jnp.bfloat16
F32 = jnp.float32
VMEM = 12 * 1024 * 1024


def call(kernel, outs, scratch=()):
    return pl.pallas_call(
        kernel,
        out_shape=outs,
        scratch_shapes=scratch,
        compiler_params=pltpu.CompilerParams(vmem_limit_bytes=VMEM),
    )


def call_with_scalar(kernel, outs, count):
    return pl.pallas_call(
        kernel,
        out_shape=outs,
        in_specs=[pl.BlockSpec(memory_space=pltpu.SMEM)] + [pl.BlockSpec(memory_space=pltpu.VMEM)] * count,
        compiler_params=pltpu.CompilerParams(vmem_limit_bytes=VMEM),
    )


def pick(shape, axis):
    r = lax.broadcasted_iota(jnp.int32, shape, axis)
    u = lax.broadcasted_iota(jnp.int32, shape, 1 - axis)
    first = (r >= 1) & (r <= FEAT) & (u == r - 1)
    second = jnp.zeros(shape, jnp.bool_)
    base = 1 + FEAT
    for i in range(FEAT):
        width = FEAT - i
        inside = (r >= base) & (r < base + width)
        first = first | (inside & (u == i))
        second = second | (inside & (u == i + r - base))
        base += width
    return first.astype(F32).astype(BF), second.astype(F32).astype(BF)


def weights_of(shape, axis, twice):
    r = lax.broadcasted_iota(jnp.int32, shape, axis)
    scale = jnp.where(r == 0, 1.0, jnp.where(r <= FEAT, 0.5, 1.0 / (4.0 * math.sqrt(2.0))))
    if twice:
        base = 1 + FEAT
        square = jnp.zeros(shape, jnp.bool_)
        for i in range(FEAT):
            square = square | (r == base)
            base += FEAT - i
        scale = jnp.where((r > FEAT) & ~square, 2.0 * scale, scale)
    one_first = jnp.where(r == 0, 1.0, 0.0)
    one_second = jnp.where(r <= FEAT, 1.0, 0.0)
    return scale, one_first, one_second


NT = (((1,), (1,)), ((), ()))
NN = (((1,), (0,)), ((), ()))


def dot(a, b, dims=NN):
    return lax.dot_general(a, b, dims, preferred_element_type=F32)


def gather_products(flip, core_ref, x_ref, gain_ref, wf_ref, wv_ref, ww_ref):
    squares = feats = values = windowed = 0.0
    for y in range(4):
        at = pl.multiple_of((2 * y + (core_ref[0] + flip) % 2) * 256, 256)
        x = x_ref[y, :, :].astype(F32)
        squares = squares + x * x
        scaled = (x * gain_ref[0:1, pl.ds(at, 256)]).astype(BF)
        feats = feats + dot(scaled, wf_ref[:, pl.ds(at, 256)], NT)
        values = values + dot(scaled, wv_ref[pl.ds(at, 256), :])
        windowed = windowed + dot(scaled, ww_ref[pl.ds(at, 256), :])
    return jnp.sum(squares, axis=1, keepdims=True), feats, values, windowed


def begin_kernel(core_ref, x_ref, gain_ref, wf_ref, wv_ref, ww_ref, held_ref):
    squares, feats, values, windowed = gather_products(0, core_ref, x_ref, gain_ref, wf_ref, wv_ref, ww_ref)
    held_ref[:, :256] = values
    held_ref[:, 256:512] = windowed
    held_ref[:, 512:544] = feats
    held_ref[:, 544:] = jnp.broadcast_to(squares, (squares.shape[0], 96))


def project_kernel(core_ref, x_ref, gain_ref, wf_ref, wv_ref, ww_ref, held_ref, pack_ref, rim_ref, state_ref):
    count = x_ref.shape[1]
    squares, feats, values, windowed = gather_products(1, core_ref, x_ref, gain_ref, wf_ref, wv_ref, ww_ref)
    scale = lax.rsqrt((squares + held_ref[:, 544:545]) * (1.0 / 2048.0) + EPS)
    values = ((values + held_ref[:, :256]) * scale).astype(BF)
    windowed = ((windowed + held_ref[:, 256:512]) * scale).astype(BF)
    feats = ((feats + held_ref[:, 512:544]) * scale).astype(BF)
    rim_ref[:, :128] = windowed[:, 128:]
    rim_ref[:, 128:] = values[:, 128:]
    vlin = values[:, :128]
    pack_ref[:, :128] = windowed[:, :128]
    pack_ref[:, 128:256] = vlin
    pack_ref[:, 256:288] = feats
    pack_ref[:, 288:] = jnp.zeros((count, 96), BF)
    first, second = pick((ROWS, FEAT), 0)
    scale, add_first, add_second = weights_of((ROWS, 1), 0, False)
    k = feats[:, FEAT:]
    phi = (dot(first, k, NT) + add_first) * (dot(second, k, NT) + add_second) * scale
    state = dot(phi.astype(BF), vlin)
    for i in range(4):
        state_ref[i, :, :] = state[QUARTER * i : QUARTER * (i + 1), :].astype(BF)


def inner_kernel(pack_ref, after_ref, num_ref):
    count = pack_ref.shape[0]
    tile = 256
    for t in range(count // tile):
        ql = pack_ref[t * tile : (t + 1) * tile, 256 : 256 + FEAT]
        kl = pack_ref[: (t + 1) * tile, 256 + FEAT : 256 + 2 * FEAT]
        inner = dot(ql, kl, NT)
        width = kl.shape[0]
        row = lax.broadcasted_iota(jnp.int32, (tile, width), 0) + t * tile
        col = lax.broadcasted_iota(jnp.int32, (tile, width), 1)
        series = 1.0 + inner * 0.25 + inner * inner * (1.0 / 32.0)
        weight = jnp.where(row >= col, series, 0.0).astype(BF)
        num_ref[t * tile : (t + 1) * tile, :] = dot(weight, pack_ref[: (t + 1) * tile, 128:256])


def attend_kernel(first_ref, pack_ref, own_ref, prev_ref, win_ref):
    count = pack_ref.shape[0]
    tile = 256
    no_prev = first_ref[0] == 0
    for t in range(count // tile):
        q = pack_ref[t * tile : (t + 1) * tile, :128]
        old = prev_ref[t * tile :, :]
        new = own_ref[: (t + 1) * tile, :]
        keys = jnp.concatenate([old[:, :128], new[:, :128]], axis=0)
        vals = jnp.concatenate([old[:, 128:], new[:, 128:]], axis=0)
        width = keys.shape[0]
        scores = dot(q, keys, NT) * (1.0 / math.sqrt(128.0))
        at = lax.broadcasted_iota(jnp.int32, (tile, width), 0) + count
        key = lax.broadcasted_iota(jnp.int32, (tile, width), 1)
        least = jnp.where(no_prev, count - t * tile, 0)
        allowed = (key <= at) & (key > at - count) & (key >= least)
        scores = jnp.where(allowed, scores, -1e30)
        lifted = jnp.exp(scores - jnp.max(scores, axis=1, keepdims=True))
        probs = (lifted / jnp.sum(lifted, axis=1, keepdims=True)).astype(BF)
        win_ref[t * tile : (t + 1) * tile, :] = dot(probs, vals).astype(BF)


def linear_kernel(pack_ref, num_ref, prefix_ref, win_ref, mix_ref):
    first, second = pick((FEAT, ROWS), 1)
    scale, add_first, add_second = weights_of((1, ROWS), 1, True)
    q = pack_ref[:, 256 : 256 + FEAT]
    phi = (dot(q, first) + add_first) * (dot(q, second) + add_second) * scale
    prefix = jnp.concatenate([prefix_ref[i, :, :].astype(F32) for i in range(4)], axis=0).astype(BF)
    numerator = num_ref[...] + dot(phi.astype(BF), prefix)
    mean = jnp.mean(numerator * numerator, axis=1, keepdims=True)
    mix_ref[:, :128] = (numerator * lax.rsqrt(mean + EPS)).astype(BF)
    mix_ref[:, 128:] = win_ref[...]


def pick_kernel(core_ref, w_ref, after_ref, out_ref):
    for y in range(4):
        at = pl.multiple_of((2 * y + 1 - core_ref[0]) * 256, 256)
        out_ref[y, :, :] = w_ref[:, pl.ds(at, 256)]


def own_kernel(core_ref, mix_ref, w_ref, sum_ref):
    for y in range(4):
        at = pl.multiple_of((2 * y + core_ref[0]) * 256, 256)
        sum_ref[y, :, :] = dot(mix_ref[...], w_ref[:, pl.ds(at, 256)])


def output_kernel(mix_ref, w_ref, own_ref, sum_ref):
    for y in range(4):
        sum_ref[y, :, :] = (own_ref[y, :, :] + dot(mix_ref[...], w_ref[y, :, :])).astype(BF)


def total_kernel(got_ref, out_ref):
    total = got_ref[0, :, :].astype(F32)
    for i in range(1, 4):
        total = total + got_ref[i, :, :].astype(F32)
    total = total.astype(BF)
    for z in range(16):
        out_ref[z, :, :] = total


def prefix_kernel(place_ref, got_ref, totals_ref, out_ref):
    state = jnp.zeros((QUARTER, 128), F32)
    for z in range(15):
        state = state + jnp.where(z < place_ref[0], totals_ref[z, :, :].astype(F32), 0.0)
    for i in range(4):
        out_ref[i, :, :] = state.astype(BF)
        state = state + got_ref[i, :, :].astype(F32)


def shards(tokens, gain, w_feat, w_value, w_window, w_out):
    count = tokens.shape[0]
    head = lax.axis_index("head")
    ctx = lax.axis_index("ctx")
    core = (head % 2).astype(jnp.int32).reshape(1)
    along_y = [[2 * y + c for y in range(4)] for c in range(2)]

    def across(value):
        return lax.ppermute(value, "head", [(h, h ^ 1) for h in range(8)])

    def shape(dims, kind=BF):
        return jax.ShapeDtypeStruct(dims, kind)

    spread = lax.all_to_all(
        jnp.broadcast_to(tokens[None], (4,) + tokens.shape), "head", 0, 0, tiled=True, axis_index_groups=along_y
    )
    other = across(spread)
    weights = (gain.reshape(1, -1), w_feat.T, w_value, w_window)
    held = call_with_scalar(begin_kernel, shape((count, 640), F32), 5)(core, spread, *weights)
    pack, rim, states = call_with_scalar(
        project_kernel, [shape((count, 384)), shape((count, 256)), shape((4, QUARTER, 128))], 6
    )(core, other, *weights, held)
    in_x = [[4 * z + x for x in range(4)] for z in range(16)]
    in_z = [[4 * z + x for z in range(16)] for x in range(4)]
    quarters = lax.all_to_all(states, "ctx", 0, 0, tiled=True, axis_index_groups=in_x)
    totals = lax.all_to_all(
        call(total_kernel, shape((16, QUARTER, 128)))(quarters), "ctx", 0, 0, tiled=True, axis_index_groups=in_z
    )
    picked = call_with_scalar(pick_kernel, shape((4, 256, 256)), 2)(core, w_out, quarters)
    w_other = across(picked)
    numerator = call(inner_kernel, shape((count, 128), F32))(pack, picked)
    rim, numerator = lax.optimization_barrier((rim, numerator))
    prev = lax.ppermute(rim, "ctx", [(b, b + 1) for b in range(63)])
    win_out = call_with_scalar(attend_kernel, shape((count, 128)), 3)(ctx.astype(jnp.int32).reshape(1), pack, rim, prev)
    sums = call_with_scalar(prefix_kernel, shape((4, QUARTER, 128)), 2)(
        (ctx // 4).astype(jnp.int32).reshape(1), quarters, totals
    )
    sums, numerator = lax.optimization_barrier((sums, numerator))
    prefix = lax.all_to_all(sums, "ctx", 0, 0, tiled=True, axis_index_groups=in_x)
    mix = call(linear_kernel, shape((count, 256)))(pack, numerator, prefix, win_out)
    own = call_with_scalar(own_kernel, shape((4, count, 256), F32), 2)(core, mix, w_out)
    summed = call(output_kernel, shape((4, count, 256)))(across(mix), w_other, own)
    parts = lax.all_to_all(summed, "head", 0, 0, tiled=True, axis_index_groups=along_y)
    return jnp.sum(parts.astype(F32), axis=0).astype(BF)


def solution(mesh):
    placed = (P("ctx", "head"), P(), P(None, "head"), P(None, "head"), P(None, "head"), P("head", None))
    return jax.shard_map(shards, mesh=mesh, in_specs=placed, out_specs=P("ctx", "head"), check_vma=False)
```

```python
import functools
import math

import jax
import jax.numpy as jnp
from jax import lax
from jax.experimental import pallas as pl
from jax.experimental.pallas import tpu as pltpu
from jax.sharding import PartitionSpec as P

EPS = 1e-05
FEAT = 16
QUARTER = 40
ROWS = 4 * QUARTER
BF = jnp.bfloat16
F32 = jnp.float32
VMEM = 12 * 1024 * 1024


def call(kernel, outs, scratch=()):
    return pl.pallas_call(
        kernel,
        out_shape=outs,
        scratch_shapes=scratch,
        compiler_params=pltpu.CompilerParams(vmem_limit_bytes=VMEM),
    )


def call_with_scalar(kernel, outs, count, scalars=1):
    return pl.pallas_call(
        kernel,
        out_shape=outs,
        in_specs=[pl.BlockSpec(memory_space=pltpu.SMEM)] * scalars + [pl.BlockSpec(memory_space=pltpu.VMEM)] * count,
        compiler_params=pltpu.CompilerParams(vmem_limit_bytes=VMEM),
    )


def pick(shape, axis):
    r = lax.broadcasted_iota(jnp.int32, shape, axis)
    u = lax.broadcasted_iota(jnp.int32, shape, 1 - axis)
    first = (r >= 1) & (r <= FEAT) & (u == r - 1)
    second = jnp.zeros(shape, jnp.bool_)
    base = 1 + FEAT
    for i in range(FEAT):
        width = FEAT - i
        inside = (r >= base) & (r < base + width)
        first = first | (inside & (u == i))
        second = second | (inside & (u == i + r - base))
        base += width
    return first.astype(F32).astype(BF), second.astype(F32).astype(BF)


def weights_of(shape, axis, twice):
    r = lax.broadcasted_iota(jnp.int32, shape, axis)
    scale = jnp.where(r == 0, 1.0, jnp.where(r <= FEAT, 0.5, 1.0 / (4.0 * math.sqrt(2.0))))
    if twice:
        base = 1 + FEAT
        square = jnp.zeros(shape, jnp.bool_)
        for i in range(FEAT):
            square = square | (r == base)
            base += FEAT - i
        scale = jnp.where((r > FEAT) & ~square, 2.0 * scale, scale)
    one_first = jnp.where(r == 0, 1.0, 0.0)
    one_second = jnp.where(r <= FEAT, 1.0, 0.0)
    return scale, one_first, one_second


NT = (((1,), (1,)), ((), ()))
NN = (((1,), (0,)), ((), ()))


def dot(a, b, dims=NN):
    return lax.dot_general(a, b, dims, preferred_element_type=F32)


def gather_products(flip, core_ref, y_ref, blocks, gain_ref, wf_ref, wv_ref, ww_ref):
    squares = feats = values = windowed = 0.0
    for back, x_ref in enumerate(blocks):
        at = pl.multiple_of((2 * ((y_ref[0] + 4 - back) % 4) + (core_ref[0] + flip) % 2) * 256, 256)
        x = x_ref[...].astype(F32)
        squares = squares + x * x
        scaled = (x * gain_ref[0:1, pl.ds(at, 256)]).astype(BF)
        feats = feats + dot(scaled, wf_ref[:, pl.ds(at, 256)], NT)
        values = values + dot(scaled, wv_ref[pl.ds(at, 256), :])
        windowed = windowed + dot(scaled, ww_ref[pl.ds(at, 256), :])
    return jnp.sum(squares, axis=1, keepdims=True), feats, values, windowed


def hold_kernel(core_ref, y_ref, gain_ref, wf_ref, wv_ref, ww_ref, gain_out, wf_out, wv_out, ww_out):
    gain_out[...] = gain_ref[...]
    wf_out[...] = wf_ref[...]
    wv_out[...] = wv_ref[...]
    ww_out[...] = ww_ref[...]


def begin_kernel(core_ref, y_ref, b0, b1, b2, b3, gain_ref, wf_ref, wv_ref, ww_ref, held_ref):
    squares, feats, values, windowed = gather_products(0, core_ref, y_ref, (b0, b1, b2, b3), gain_ref, wf_ref, wv_ref, ww_ref)
    held_ref[:, :256] = values
    held_ref[:, 256:512] = windowed
    held_ref[:, 512:544] = feats
    held_ref[:, 544:] = jnp.broadcast_to(squares, (squares.shape[0], 96))


def project_kernel(
    core_ref, y_ref, b0, b1, b2, b3, gain_ref, wf_ref, wv_ref, ww_ref, held_ref, pack_ref, rim_ref, state_ref
):
    count = b0.shape[0]
    squares, feats, values, windowed = gather_products(1, core_ref, y_ref, (b0, b1, b2, b3), gain_ref, wf_ref, wv_ref, ww_ref)
    scale = lax.rsqrt((squares + held_ref[:, 544:545]) * (1.0 / 2048.0) + EPS)
    values = ((values + held_ref[:, :256]) * scale).astype(BF)
    windowed = ((windowed + held_ref[:, 256:512]) * scale).astype(BF)
    feats = ((feats + held_ref[:, 512:544]) * scale).astype(BF)
    rim_ref[:, :128] = windowed[:, 128:]
    rim_ref[:, 128:] = values[:, 128:]
    vlin = values[:, :128]
    pack_ref[:, :128] = windowed[:, :128]
    pack_ref[:, 128:256] = vlin
    pack_ref[:, 256:288] = feats
    pack_ref[:, 288:] = jnp.zeros((count, 96), BF)
    first, second = pick((ROWS, FEAT), 0)
    scale, add_first, add_second = weights_of((ROWS, 1), 0, False)
    k = feats[:, FEAT:]
    phi = (dot(first, k, NT) + add_first) * (dot(second, k, NT) + add_second) * scale
    state = dot(phi.astype(BF), vlin)
    for i in range(4):
        state_ref[i, :, :] = state[QUARTER * i : QUARTER * (i + 1), :].astype(BF)


def inner_kernel(pack_ref, after_ref, num_ref):
    count = pack_ref.shape[0]
    tile = 256
    for t in range(count // tile):
        ql = pack_ref[t * tile : (t + 1) * tile, 256 : 256 + FEAT]
        kl = pack_ref[: (t + 1) * tile, 256 + FEAT : 256 + 2 * FEAT]
        inner = dot(ql, kl, NT)
        width = kl.shape[0]
        row = lax.broadcasted_iota(jnp.int32, (tile, width), 0) + t * tile
        col = lax.broadcasted_iota(jnp.int32, (tile, width), 1)
        series = 1.0 + inner * 0.25 + inner * inner * (1.0 / 32.0)
        weight = jnp.where(row >= col, series, 0.0).astype(BF)
        num_ref[t * tile : (t + 1) * tile, :] = dot(weight, pack_ref[: (t + 1) * tile, 128:256])


def attend_kernel(first_ref, pack_ref, own_ref, prev_ref, win_ref):
    count = pack_ref.shape[0]
    tile = 256
    no_prev = first_ref[0] == 0
    for t in range(count // tile):
        q = pack_ref[t * tile : (t + 1) * tile, :128]
        old = prev_ref[t * tile :, :]
        new = own_ref[: (t + 1) * tile, :]
        keys = jnp.concatenate([old[:, :128], new[:, :128]], axis=0)
        vals = jnp.concatenate([old[:, 128:], new[:, 128:]], axis=0)
        width = keys.shape[0]
        scores = dot(q, keys, NT) * (1.0 / math.sqrt(128.0))
        at = lax.broadcasted_iota(jnp.int32, (tile, width), 0) + count
        key = lax.broadcasted_iota(jnp.int32, (tile, width), 1)
        least = jnp.where(no_prev, count - t * tile, 0)
        allowed = (key <= at) & (key > at - count) & (key >= least)
        scores = jnp.where(allowed, scores, -1e30)
        lifted = jnp.exp(scores - jnp.max(scores, axis=1, keepdims=True))
        probs = (lifted / jnp.sum(lifted, axis=1, keepdims=True)).astype(BF)
        win_ref[t * tile : (t + 1) * tile, :] = dot(probs, vals).astype(BF)


def linear_kernel(pack_ref, num_ref, prefix_ref, win_ref, mix_ref):
    first, second = pick((FEAT, ROWS), 1)
    scale, add_first, add_second = weights_of((1, ROWS), 1, True)
    q = pack_ref[:, 256 : 256 + FEAT]
    phi = (dot(q, first) + add_first) * (dot(q, second) + add_second) * scale
    prefix = jnp.concatenate([prefix_ref[i, :, :].astype(F32) for i in range(4)], axis=0).astype(BF)
    numerator = num_ref[...] + dot(phi.astype(BF), prefix)
    mean = jnp.mean(numerator * numerator, axis=1, keepdims=True)
    mix_ref[:, :128] = (numerator * lax.rsqrt(mean + EPS)).astype(BF)
    mix_ref[:, 128:] = win_ref[...]


def pick_kernel(core_ref, w_ref, after_ref, out_ref):
    for y in range(4):
        at = pl.multiple_of((2 * y + 1 - core_ref[0]) * 256, 256)
        out_ref[y, :, :] = w_ref[:, pl.ds(at, 256)]


def own_kernel(core_ref, mix_ref, w_ref, sum_ref):
    for y in range(4):
        at = pl.multiple_of((2 * y + core_ref[0]) * 256, 256)
        sum_ref[y, :, :] = dot(mix_ref[...], w_ref[:, pl.ds(at, 256)])


def output_kernel(mix_ref, w_ref, own_ref, sum_ref):
    for y in range(4):
        sum_ref[y, :, :] = (own_ref[y, :, :] + dot(mix_ref[...], w_ref[y, :, :])).astype(BF)


def total_kernel(got_ref, out_ref):
    total = got_ref[0, :, :].astype(F32)
    for i in range(1, 4):
        total = total + got_ref[i, :, :].astype(F32)
    total = total.astype(BF)
    for z in range(16):
        out_ref[z, :, :] = total


def prefix_kernel(place_ref, got_ref, totals_ref, out_ref):
    state = jnp.zeros((QUARTER, 128), F32)
    for z in range(15):
        state = state + jnp.where(z < place_ref[0], totals_ref[z, :, :].astype(F32), 0.0)
    for i in range(4):
        out_ref[i, :, :] = state.astype(BF)
        state = state + got_ref[i, :, :].astype(F32)


def shards(tokens, gain, w_feat, w_value, w_window, w_out):
    count = tokens.shape[0]
    head = lax.axis_index("head")
    ctx = lax.axis_index("ctx")
    core = (head % 2).astype(jnp.int32).reshape(1)
    along_y = [[2 * y + c for y in range(4)] for c in range(2)]

    def across(value):
        return lax.ppermute(value, "head", [(h, h ^ 1) for h in range(8)])

    def shape(dims, kind=BF):
        return jax.ShapeDtypeStruct(dims, kind)

    near = [tokens] + [
        lax.ppermute(tokens, "head", [(h, (h + 2 * k) % 8) for h in range(8)]) for k in (1, 2, 3)
    ]
    far = [across(near[0]), across(near[1]), None, across(near[3])]
    row = (head // 2).astype(jnp.int32).reshape(1)
    weights = call_with_scalar(
        hold_kernel,
        [shape((1, 2048), F32), shape(w_feat.shape[::-1]), shape(w_value.shape), shape(w_window.shape)],
        4,
        2,
    )(core, row, gain.reshape(1, -1), w_feat.T, w_value, w_window)
    near[2], far[1], far[3], *weights = lax.optimization_barrier((near[2], far[1], far[3], *weights))
    far[2] = across(near[2])
    held = call_with_scalar(begin_kernel, shape((count, 640), F32), 8, 2)(core, row, *near, *weights)
    pack, rim, states = call_with_scalar(
        project_kernel, [shape((count, 384)), shape((count, 256)), shape((4, QUARTER, 128))], 9, 2
    )(core, row, *far, *weights, held)
    in_x = [[4 * z + x for x in range(4)] for z in range(16)]
    in_z = [[4 * z + x for z in range(16)] for x in range(4)]
    quarters = lax.all_to_all(states, "ctx", 0, 0, tiled=True, axis_index_groups=in_x)
    rim, quarters = lax.optimization_barrier((rim, quarters))
    totals = lax.all_to_all(
        call(total_kernel, shape((16, QUARTER, 128)))(quarters), "ctx", 0, 0, tiled=True, axis_index_groups=in_z
    )
    prev = lax.ppermute(rim, "ctx", [(b, b + 1) for b in range(63)])
    numerator = call(inner_kernel, shape((count, 128), F32))(pack, quarters)
    w_other = across(call_with_scalar(pick_kernel, shape((4, 256, 256)), 2)(core, w_out, quarters))
    win_out = call_with_scalar(attend_kernel, shape((count, 128)), 3)(ctx.astype(jnp.int32).reshape(1), pack, rim, prev)
    sums = call_with_scalar(prefix_kernel, shape((4, QUARTER, 128)), 2)(
        (ctx // 4).astype(jnp.int32).reshape(1), quarters, totals
    )
    sums, numerator = lax.optimization_barrier((sums, numerator))
    prefix = lax.all_to_all(sums, "ctx", 0, 0, tiled=True, axis_index_groups=in_x)
    mix = call(linear_kernel, shape((count, 256)))(pack, numerator, prefix, win_out)
    own = call_with_scalar(own_kernel, shape((4, count, 256), F32), 2)(core, mix, w_out)
    summed = call(output_kernel, shape((4, count, 256)))(across(mix), w_other, own)
    parts = lax.all_to_all(summed, "head", 0, 0, tiled=True, axis_index_groups=along_y)
    return jnp.sum(parts.astype(F32), axis=0).astype(BF)


def solution(mesh):
    placed = (P("ctx", "head"), P(), P(None, "head"), P(None, "head"), P(None, "head"), P("head", None))
    return jax.shard_map(shards, mesh=mesh, in_specs=placed, out_specs=P("ctx", "head"), check_vma=False)
```

```python
import functools
import math

import jax
import jax.numpy as jnp
from jax import lax
from jax.experimental import pallas as pl
from jax.experimental.pallas import tpu as pltpu
from jax.sharding import PartitionSpec as P

EPS = 1e-05
FEAT = 16
QUARTER = 40
ROWS = 4 * QUARTER
BF = jnp.bfloat16
F32 = jnp.float32
VMEM = 12 * 1024 * 1024


def call(kernel, outs, scratch=()):
    return pl.pallas_call(
        kernel,
        out_shape=outs,
        scratch_shapes=scratch,
        compiler_params=pltpu.CompilerParams(vmem_limit_bytes=VMEM),
    )


def call_with_scalar(kernel, outs, count, scalars=1):
    return pl.pallas_call(
        kernel,
        out_shape=outs,
        in_specs=[pl.BlockSpec(memory_space=pltpu.SMEM)] * scalars + [pl.BlockSpec(memory_space=pltpu.VMEM)] * count,
        compiler_params=pltpu.CompilerParams(vmem_limit_bytes=VMEM),
    )


def pick(shape, axis):
    r = lax.broadcasted_iota(jnp.int32, shape, axis)
    u = lax.broadcasted_iota(jnp.int32, shape, 1 - axis)
    first = (r >= 1) & (r <= FEAT) & (u == r - 1)
    second = jnp.zeros(shape, jnp.bool_)
    base = 1 + FEAT
    for i in range(FEAT):
        width = FEAT - i
        inside = (r >= base) & (r < base + width)
        first = first | (inside & (u == i))
        second = second | (inside & (u == i + r - base))
        base += width
    return first.astype(F32).astype(BF), second.astype(F32).astype(BF)


def weights_of(shape, axis, twice):
    r = lax.broadcasted_iota(jnp.int32, shape, axis)
    scale = jnp.where(r == 0, 1.0, jnp.where(r <= FEAT, 0.5, 1.0 / (4.0 * math.sqrt(2.0))))
    if twice:
        base = 1 + FEAT
        square = jnp.zeros(shape, jnp.bool_)
        for i in range(FEAT):
            square = square | (r == base)
            base += FEAT - i
        scale = jnp.where((r > FEAT) & ~square, 2.0 * scale, scale)
    one_first = jnp.where(r == 0, 1.0, 0.0)
    one_second = jnp.where(r <= FEAT, 1.0, 0.0)
    return scale, one_first, one_second


NT = (((1,), (1,)), ((), ()))
NN = (((1,), (0,)), ((), ()))


def dot(a, b, dims=NN):
    return lax.dot_general(a, b, dims, preferred_element_type=F32)


def gather_products(flip, core_ref, x_ref, gain_ref, wf_ref, wv_ref, ww_ref):
    squares = feats = values = windowed = 0.0
    for y in range(4):
        at = pl.multiple_of((2 * y + (core_ref[0] + flip) % 2) * 256, 256)
        x = x_ref[y, :, :].astype(F32)
        squares = squares + x * x
        scaled = (x * gain_ref[0:1, pl.ds(at, 256)]).astype(BF)
        feats = feats + dot(scaled, wf_ref[:, pl.ds(at, 256)], NT)
        values = values + dot(scaled, wv_ref[pl.ds(at, 256), :])
        windowed = windowed + dot(scaled, ww_ref[pl.ds(at, 256), :])
    return jnp.sum(squares, axis=1, keepdims=True), feats, values, windowed


def copies_kernel(core_ref, ctx_ref, row_ref, x_ref, out_ref):
    for y in range(4):
        out_ref[y, :, :] = x_ref[...]


def begin_kernel(core_ref, x_ref, gain_ref, wf_ref, wv_ref, ww_ref, held_ref):
    squares, feats, values, windowed = gather_products(0, core_ref, x_ref, gain_ref, wf_ref, wv_ref, ww_ref)
    held_ref[:, :256] = values
    held_ref[:, 256:512] = windowed
    held_ref[:, 512:544] = feats
    held_ref[:, 544:] = jnp.broadcast_to(squares, (squares.shape[0], 96))


def project_kernel(core_ref, x_ref, gain_ref, wf_ref, wv_ref, ww_ref, held_ref, pack_ref, rim_ref, state_ref):
    count = x_ref.shape[1]
    squares, feats, values, windowed = gather_products(1, core_ref, x_ref, gain_ref, wf_ref, wv_ref, ww_ref)
    scale = lax.rsqrt((squares + held_ref[:, 544:545]) * (1.0 / 2048.0) + EPS)
    values = ((values + held_ref[:, :256]) * scale).astype(BF)
    windowed = ((windowed + held_ref[:, 256:512]) * scale).astype(BF)
    feats = ((feats + held_ref[:, 512:544]) * scale).astype(BF)
    rim_ref[:, :128] = windowed[:, 128:]
    rim_ref[:, 128:] = values[:, 128:]
    vlin = values[:, :128]
    pack_ref[:, :128] = windowed[:, :128]
    pack_ref[:, 128:256] = vlin
    pack_ref[:, 256:288] = feats
    pack_ref[:, 288:] = jnp.zeros((count, 96), BF)
    first, second = pick((ROWS, FEAT), 0)
    scale, add_first, add_second = weights_of((ROWS, 1), 0, False)
    k = feats[:, FEAT:]
    phi = (dot(first, k, NT) + add_first) * (dot(second, k, NT) + add_second) * scale
    state = dot(phi.astype(BF), vlin)
    for i in range(4):
        state_ref[i, :, :] = state[QUARTER * i : QUARTER * (i + 1), :].astype(BF)


def inner_kernel(pack_ref, after_ref, num_ref):
    count = pack_ref.shape[0]
    tile = 256
    for t in range(count // tile):
        ql = pack_ref[t * tile : (t + 1) * tile, 256 : 256 + FEAT]
        kl = pack_ref[: (t + 1) * tile, 256 + FEAT : 256 + 2 * FEAT]
        inner = dot(ql, kl, NT)
        width = kl.shape[0]
        row = lax.broadcasted_iota(jnp.int32, (tile, width), 0) + t * tile
        col = lax.broadcasted_iota(jnp.int32, (tile, width), 1)
        series = 1.0 + inner * 0.25 + inner * inner * (1.0 / 32.0)
        weight = jnp.where(row >= col, series, 0.0).astype(BF)
        num_ref[t * tile : (t + 1) * tile, :] = dot(weight, pack_ref[: (t + 1) * tile, 128:256])


def attend_kernel(first_ref, pack_ref, own_ref, prev_ref, win_ref):
    count = pack_ref.shape[0]
    tile = 256
    no_prev = first_ref[0] == 0
    for t in range(count // tile):
        q = pack_ref[t * tile : (t + 1) * tile, :128]
        old = prev_ref[t * tile :, :]
        new = own_ref[: (t + 1) * tile, :]
        keys = jnp.concatenate([old[:, :128], new[:, :128]], axis=0)
        vals = jnp.concatenate([old[:, 128:], new[:, 128:]], axis=0)
        width = keys.shape[0]
        scores = dot(q, keys, NT) * (1.0 / math.sqrt(128.0))
        at = lax.broadcasted_iota(jnp.int32, (tile, width), 0) + count
        key = lax.broadcasted_iota(jnp.int32, (tile, width), 1)
        least = jnp.where(no_prev, count - t * tile, 0)
        allowed = (key <= at) & (key > at - count) & (key >= least)
        scores = jnp.where(allowed, scores, -1e30)
        lifted = jnp.exp(scores - jnp.max(scores, axis=1, keepdims=True))
        probs = (lifted / jnp.sum(lifted, axis=1, keepdims=True)).astype(BF)
        win_ref[t * tile : (t + 1) * tile, :] = dot(probs, vals).astype(BF)


def linear_kernel(pack_ref, num_ref, prefix_ref, win_ref, mix_ref):
    first, second = pick((FEAT, ROWS), 1)
    scale, add_first, add_second = weights_of((1, ROWS), 1, True)
    q = pack_ref[:, 256 : 256 + FEAT]
    phi = (dot(q, first) + add_first) * (dot(q, second) + add_second) * scale
    prefix = jnp.concatenate([prefix_ref[i, :, :].astype(F32) for i in range(4)], axis=0).astype(BF)
    numerator = num_ref[...] + dot(phi.astype(BF), prefix)
    mean = jnp.mean(numerator * numerator, axis=1, keepdims=True)
    mix_ref[:, :128] = (numerator * lax.rsqrt(mean + EPS)).astype(BF)
    mix_ref[:, 128:] = win_ref[...]


def pick_kernel(core_ref, w_ref, after_ref, out_ref):
    for y in range(4):
        at = pl.multiple_of((2 * y + 1 - core_ref[0]) * 256, 256)
        out_ref[y, :, :] = w_ref[:, pl.ds(at, 256)]


def own_kernel(core_ref, mix_ref, w_ref, sum_ref):
    for y in range(4):
        at = pl.multiple_of((2 * y + core_ref[0]) * 256, 256)
        sum_ref[y, :, :] = dot(mix_ref[...], w_ref[:, pl.ds(at, 256)])


def output_kernel(mix_ref, w_ref, own_ref, sum_ref):
    for y in range(4):
        sum_ref[y, :, :] = (own_ref[y, :, :] + dot(mix_ref[...], w_ref[y, :, :])).astype(BF)


def total_kernel(got_ref, out_ref):
    total = got_ref[0, :, :].astype(F32)
    for i in range(1, 4):
        total = total + got_ref[i, :, :].astype(F32)
    total = total.astype(BF)
    for z in range(16):
        out_ref[z, :, :] = total


def prefix_kernel(place_ref, got_ref, totals_ref, out_ref):
    state = jnp.zeros((QUARTER, 128), F32)
    for z in range(15):
        state = state + jnp.where(z < place_ref[0], totals_ref[z, :, :].astype(F32), 0.0)
    for i in range(4):
        out_ref[i, :, :] = state.astype(BF)
        state = state + got_ref[i, :, :].astype(F32)


def shards(tokens, gain, w_feat, w_value, w_window, w_out):
    count = tokens.shape[0]
    head = lax.axis_index("head")
    ctx = lax.axis_index("ctx")
    core = (head % 2).astype(jnp.int32).reshape(1)
    along_y = [[2 * y + c for y in range(4)] for c in range(2)]

    def across(value):
        return lax.ppermute(value, "head", [(h, h ^ 1) for h in range(8)])

    def shape(dims, kind=BF):
        return jax.ShapeDtypeStruct(dims, kind)

    block = ctx.astype(jnp.int32).reshape(1)
    row = (ctx // 4).astype(jnp.int32).reshape(1)
    copies = call_with_scalar(copies_kernel, shape((4,) + tokens.shape), 1, 3)(core, block, row, tokens)
    spread = lax.all_to_all(copies, "head", 0, 0, tiled=True, axis_index_groups=along_y)
    other = across(spread)
    weights = (gain.reshape(1, -1), w_feat.T, w_value, w_window)
    held = call_with_scalar(begin_kernel, shape((count, 640), F32), 5)(core, spread, *weights)
    pack, rim, states = call_with_scalar(
        project_kernel, [shape((count, 384)), shape((count, 256)), shape((4, QUARTER, 128))], 6
    )(core, other, *weights, held)
    in_x = [[4 * z + x for x in range(4)] for z in range(16)]
    in_z = [[4 * z + x for z in range(16)] for x in range(4)]
    quarters = lax.all_to_all(states, "ctx", 0, 0, tiled=True, axis_index_groups=in_x)
    rim, quarters = lax.optimization_barrier((rim, quarters))
    totals = lax.all_to_all(
        call(total_kernel, shape((16, QUARTER, 128)))(quarters), "ctx", 0, 0, tiled=True, axis_index_groups=in_z
    )
    prev = lax.ppermute(rim, "ctx", [(b, b + 1) for b in range(63)])
    numerator = call(inner_kernel, shape((count, 128), F32))(pack, quarters)
    w_other = across(call_with_scalar(pick_kernel, shape((4, 256, 256)), 2)(core, w_out, quarters))
    win_out = call_with_scalar(attend_kernel, shape((count, 128)), 3)(block, pack, rim, prev)
    sums = call_with_scalar(prefix_kernel, shape((4, QUARTER, 128)), 2)(
        row, quarters, totals
    )
    sums, numerator = lax.optimization_barrier((sums, numerator))
    prefix = lax.all_to_all(sums, "ctx", 0, 0, tiled=True, axis_index_groups=in_x)
    mix = call(linear_kernel, shape((count, 256)))(pack, numerator, prefix, win_out)
    own = call_with_scalar(own_kernel, shape((4, count, 256), F32), 2)(core, mix, w_out)
    summed = call(output_kernel, shape((4, count, 256)))(across(mix), w_other, own)
    parts = lax.all_to_all(summed, "head", 0, 0, tiled=True, axis_index_groups=along_y)
    return jnp.sum(parts.astype(F32), axis=0).astype(BF)


def solution(mesh):
    placed = (P("ctx", "head"), P(), P(None, "head"), P(None, "head"), P(None, "head"), P("head", None))
    return jax.shard_map(shards, mesh=mesh, in_specs=placed, out_specs=P("ctx", "head"), check_vma=False)
```

```python
import functools
import math

import jax
import jax.numpy as jnp
from jax import lax
from jax.experimental import pallas as pl
from jax.experimental.pallas import tpu as pltpu
from jax.sharding import PartitionSpec as P

EPS = 1e-05
FEAT = 16
QUARTER = 40
ROWS = 4 * QUARTER
BF = jnp.bfloat16
F32 = jnp.float32
VMEM = 12 * 1024 * 1024


def call(kernel, outs, scratch=()):
    return pl.pallas_call(
        kernel,
        out_shape=outs,
        scratch_shapes=scratch,
        compiler_params=pltpu.CompilerParams(vmem_limit_bytes=VMEM),
    )


def call_with_scalar(kernel, outs, count, scalars=1):
    return pl.pallas_call(
        kernel,
        out_shape=outs,
        in_specs=[pl.BlockSpec(memory_space=pltpu.SMEM)] * scalars + [pl.BlockSpec(memory_space=pltpu.VMEM)] * count,
        compiler_params=pltpu.CompilerParams(vmem_limit_bytes=VMEM),
    )


def pick(shape, axis):
    r = lax.broadcasted_iota(jnp.int32, shape, axis)
    u = lax.broadcasted_iota(jnp.int32, shape, 1 - axis)
    first = (r >= 1) & (r <= FEAT) & (u == r - 1)
    second = jnp.zeros(shape, jnp.bool_)
    base = 1 + FEAT
    for i in range(FEAT):
        width = FEAT - i
        inside = (r >= base) & (r < base + width)
        first = first | (inside & (u == i))
        second = second | (inside & (u == i + r - base))
        base += width
    return first.astype(F32).astype(BF), second.astype(F32).astype(BF)


def weights_of(shape, axis, twice):
    r = lax.broadcasted_iota(jnp.int32, shape, axis)
    scale = jnp.where(r == 0, 1.0, jnp.where(r <= FEAT, 0.5, 1.0 / (4.0 * math.sqrt(2.0))))
    if twice:
        base = 1 + FEAT
        square = jnp.zeros(shape, jnp.bool_)
        for i in range(FEAT):
            square = square | (r == base)
            base += FEAT - i
        scale = jnp.where((r > FEAT) & ~square, 2.0 * scale, scale)
    one_first = jnp.where(r == 0, 1.0, 0.0)
    one_second = jnp.where(r <= FEAT, 1.0, 0.0)
    return scale, one_first, one_second


NT = (((1,), (1,)), ((), ()))
NN = (((1,), (0,)), ((), ()))


def dot(a, b, dims=NN):
    return lax.dot_general(a, b, dims, preferred_element_type=F32)


def gather_products(flip, core_ref, x_ref, gain_ref, wf_ref, wv_ref, ww_ref):
    squares = feats = values = windowed = 0.0
    for y in range(4):
        at = pl.multiple_of((2 * y + (core_ref[0] + flip) % 2) * 256, 256)
        x = x_ref[y, :, :].astype(F32)
        squares = squares + x * x
        scaled = (x * gain_ref[0:1, pl.ds(at, 256)]).astype(BF)
        feats = feats + dot(scaled, wf_ref[:, pl.ds(at, 256)], NT)
        values = values + dot(scaled, wv_ref[pl.ds(at, 256), :])
        windowed = windowed + dot(scaled, ww_ref[pl.ds(at, 256), :])
    return jnp.sum(squares, axis=1, keepdims=True), feats, values, windowed


def copies_kernel(core_ref, ctx_ref, row_ref, x_ref, out_ref):
    for y in range(4):
        out_ref[y, :, :] = x_ref[...]


def begin_kernel(core_ref, x_ref, gain_ref, wf_ref, wv_ref, ww_ref, held_ref):
    squares, feats, values, windowed = gather_products(0, core_ref, x_ref, gain_ref, wf_ref, wv_ref, ww_ref)
    held_ref[:, :256] = values
    held_ref[:, 256:512] = windowed
    held_ref[:, 512:544] = feats
    held_ref[:, 544:] = jnp.broadcast_to(squares, (squares.shape[0], 96))


def project_kernel(core_ref, x_ref, gain_ref, wf_ref, wv_ref, ww_ref, held_ref, pack_ref, rim_ref, state_ref):
    count = x_ref.shape[1]
    squares, feats, values, windowed = gather_products(1, core_ref, x_ref, gain_ref, wf_ref, wv_ref, ww_ref)
    scale = lax.rsqrt((squares + held_ref[:, 544:545]) * (1.0 / 2048.0) + EPS)
    values = ((values + held_ref[:, :256]) * scale).astype(BF)
    windowed = ((windowed + held_ref[:, 256:512]) * scale).astype(BF)
    feats = ((feats + held_ref[:, 512:544]) * scale).astype(BF)
    rim_ref[:, :128] = windowed[:, 128:]
    rim_ref[:, 128:] = values[:, 128:]
    vlin = values[:, :128]
    pack_ref[:, :128] = windowed[:, :128]
    pack_ref[:, 128:256] = vlin
    pack_ref[:, 256:288] = feats
    pack_ref[:, 288:384] = jnp.zeros((count, 96), BF)
    pack_ref[:, 384:512] = windowed[:, 128:]
    pack_ref[:, 512:] = values[:, 128:]
    first, second = pick((ROWS, FEAT), 0)
    scale, add_first, add_second = weights_of((ROWS, 1), 0, False)
    k = feats[:, FEAT:]
    phi = (dot(first, k, NT) + add_first) * (dot(second, k, NT) + add_second) * scale
    state = dot(phi.astype(BF), vlin)
    for i in range(4):
        state_ref[i, :, :] = state[QUARTER * i : QUARTER * (i + 1), :].astype(BF)


def inner_kernel(pack_ref, after_ref, num_ref):
    count = pack_ref.shape[0]
    tile = 256
    for t in range(count // tile):
        ql = pack_ref[t * tile : (t + 1) * tile, 256 : 256 + FEAT]
        kl = pack_ref[: (t + 1) * tile, 256 + FEAT : 256 + 2 * FEAT]
        inner = dot(ql, kl, NT)
        width = kl.shape[0]
        row = lax.broadcasted_iota(jnp.int32, (tile, width), 0) + t * tile
        col = lax.broadcasted_iota(jnp.int32, (tile, width), 1)
        series = 1.0 + inner * 0.25 + inner * inner * (1.0 / 32.0)
        weight = jnp.where(row >= col, series, 0.0).astype(BF)
        num_ref[t * tile : (t + 1) * tile, :] = dot(weight, pack_ref[: (t + 1) * tile, 128:256])


def attend_kernel(first_ref, pack_ref, prev_ref, win_ref):
    count = pack_ref.shape[0]
    tile = 256
    no_prev = first_ref[0] == 0
    for t in range(count // tile):
        q = pack_ref[t * tile : (t + 1) * tile, :128]
        old = prev_ref[t * tile :, :]
        new = pack_ref[: (t + 1) * tile, 384:]
        keys = jnp.concatenate([old[:, :128], new[:, :128]], axis=0)
        vals = jnp.concatenate([old[:, 128:], new[:, 128:]], axis=0)
        width = keys.shape[0]
        scores = dot(q, keys, NT) * (1.0 / math.sqrt(128.0))
        at = lax.broadcasted_iota(jnp.int32, (tile, width), 0) + count
        key = lax.broadcasted_iota(jnp.int32, (tile, width), 1)
        least = jnp.where(no_prev, count - t * tile, 0)
        allowed = (key <= at) & (key > at - count) & (key >= least)
        scores = jnp.where(allowed, scores, -1e30)
        lifted = jnp.exp(scores - jnp.max(scores, axis=1, keepdims=True))
        probs = (lifted / jnp.sum(lifted, axis=1, keepdims=True)).astype(BF)
        win_ref[t * tile : (t + 1) * tile, :] = dot(probs, vals).astype(BF)


def linear_kernel(pack_ref, num_ref, prefix_ref, win_ref, mix_ref):
    first, second = pick((FEAT, ROWS), 1)
    scale, add_first, add_second = weights_of((1, ROWS), 1, True)
    q = pack_ref[:, 256 : 256 + FEAT]
    phi = (dot(q, first) + add_first) * (dot(q, second) + add_second) * scale
    prefix = jnp.concatenate([prefix_ref[i, :, :].astype(F32) for i in range(4)], axis=0).astype(BF)
    numerator = num_ref[...] + dot(phi.astype(BF), prefix)
    mean = jnp.mean(numerator * numerator, axis=1, keepdims=True)
    mix_ref[:, :128] = (numerator * lax.rsqrt(mean + EPS)).astype(BF)
    mix_ref[:, 128:] = win_ref[...]


def pick_kernel(core_ref, w_ref, after_ref, out_ref):
    for y in range(4):
        at = pl.multiple_of((2 * y + 1 - core_ref[0]) * 256, 256)
        out_ref[y, :, :] = w_ref[:, pl.ds(at, 256)]


def own_kernel(core_ref, mix_ref, w_ref, sum_ref):
    for y in range(4):
        at = pl.multiple_of((2 * y + core_ref[0]) * 256, 256)
        sum_ref[y, :, :] = dot(mix_ref[...], w_ref[:, pl.ds(at, 256)])


def output_kernel(mix_ref, w_ref, own_ref, sum_ref):
    for y in range(4):
        sum_ref[y, :, :] = (own_ref[y, :, :] + dot(mix_ref[...], w_ref[y, :, :])).astype(BF)


def total_kernel(got_ref, out_ref):
    total = got_ref[0, :, :].astype(F32)
    for i in range(1, 4):
        total = total + got_ref[i, :, :].astype(F32)
    total = total.astype(BF)
    for z in range(16):
        out_ref[z, :, :] = total


def prefix_kernel(place_ref, got_ref, totals_ref, out_ref):
    state = jnp.zeros((QUARTER, 128), F32)
    for z in range(15):
        state = state + jnp.where(z < place_ref[0], totals_ref[z, :, :].astype(F32), 0.0)
    for i in range(4):
        out_ref[i, :, :] = state.astype(BF)
        state = state + got_ref[i, :, :].astype(F32)


def shards(tokens, gain, w_feat, w_value, w_window, w_out):
    count = tokens.shape[0]
    head = lax.axis_index("head")
    ctx = lax.axis_index("ctx")
    core = (head % 2).astype(jnp.int32).reshape(1)
    along_y = [[2 * y + c for y in range(4)] for c in range(2)]

    def across(value):
        return lax.ppermute(value, "head", [(h, h ^ 1) for h in range(8)])

    def shape(dims, kind=BF):
        return jax.ShapeDtypeStruct(dims, kind)

    block = ctx.astype(jnp.int32).reshape(1)
    row = (ctx // 4).astype(jnp.int32).reshape(1)
    copies = call_with_scalar(copies_kernel, shape((4,) + tokens.shape), 1, 3)(core, block, row, tokens)
    spread = lax.all_to_all(copies, "head", 0, 0, tiled=True, axis_index_groups=along_y)
    other = across(spread)
    weights = (gain.reshape(1, -1), w_feat.T, w_value, w_window)
    held = call_with_scalar(begin_kernel, shape((count, 640), F32), 5)(core, spread, *weights)
    pack, rim, states = call_with_scalar(
        project_kernel, [shape((count, 640)), shape((count, 256)), shape((4, QUARTER, 128))], 6
    )(core, other, *weights, held)
    in_x = [[4 * z + x for x in range(4)] for z in range(16)]
    in_z = [[4 * z + x for z in range(16)] for x in range(4)]
    quarters = lax.all_to_all(states, "ctx", 0, 0, tiled=True, axis_index_groups=in_x)
    rim, quarters = lax.optimization_barrier((rim, quarters))
    totals = lax.all_to_all(
        call(total_kernel, shape((16, QUARTER, 128)))(quarters), "ctx", 0, 0, tiled=True, axis_index_groups=in_z
    )
    prev = lax.ppermute(rim, "ctx", [(b, b + 1) for b in range(63)])
    numerator = call(inner_kernel, shape((count, 128), F32))(pack, quarters)
    w_other = across(call_with_scalar(pick_kernel, shape((4, 256, 256)), 2)(core, w_out, quarters))
    win_out = call_with_scalar(attend_kernel, shape((count, 128)), 2)(block, pack, prev)
    sums = call_with_scalar(prefix_kernel, shape((4, QUARTER, 128)), 2)(
        row, quarters, totals
    )
    sums, numerator = lax.optimization_barrier((sums, numerator))
    prefix = lax.all_to_all(sums, "ctx", 0, 0, tiled=True, axis_index_groups=in_x)
    mix = call(linear_kernel, shape((count, 256)))(pack, numerator, prefix, win_out)
    own = call_with_scalar(own_kernel, shape((4, count, 256), F32), 2)(core, mix, w_out)
    summed = call(output_kernel, shape((4, count, 256)))(across(mix), w_other, own)
    parts = lax.all_to_all(summed, "head", 0, 0, tiled=True, axis_index_groups=along_y)
    return jnp.sum(parts.astype(F32), axis=0).astype(BF)


def solution(mesh):
    placed = (P("ctx", "head"), P(), P(None, "head"), P(None, "head"), P(None, "head"), P("head", None))
    return jax.shard_map(shards, mesh=mesh, in_specs=placed, out_specs=P("ctx", "head"), check_vma=False)
```

```python
import functools
import math

import jax
import jax.numpy as jnp
from jax import lax
from jax.experimental import pallas as pl
from jax.experimental.pallas import tpu as pltpu
from jax.sharding import PartitionSpec as P

EPS = 1e-05
FEAT = 16
NEAR = 8
SHARE = 24
ROWS = NEAR * SHARE
BF = jnp.bfloat16
F32 = jnp.float32
VMEM = 12 * 1024 * 1024


def call(kernel, outs, scratch=()):
    return pl.pallas_call(
        kernel,
        out_shape=outs,
        scratch_shapes=scratch,
        compiler_params=pltpu.CompilerParams(vmem_limit_bytes=VMEM),
    )


def call_with_scalar(kernel, outs, count, scalars=1):
    return pl.pallas_call(
        kernel,
        out_shape=outs,
        in_specs=[pl.BlockSpec(memory_space=pltpu.SMEM)] * scalars + [pl.BlockSpec(memory_space=pltpu.VMEM)] * count,
        compiler_params=pltpu.CompilerParams(vmem_limit_bytes=VMEM),
    )


def pick(shape, axis):
    r = lax.broadcasted_iota(jnp.int32, shape, axis)
    u = lax.broadcasted_iota(jnp.int32, shape, 1 - axis)
    first = (r >= 1) & (r <= FEAT) & (u == r - 1)
    second = jnp.zeros(shape, jnp.bool_)
    base = 1 + FEAT
    for i in range(FEAT):
        width = FEAT - i
        inside = (r >= base) & (r < base + width)
        first = first | (inside & (u == i))
        second = second | (inside & (u == i + r - base))
        base += width
    return first.astype(F32).astype(BF), second.astype(F32).astype(BF)


def weights_of(shape, axis, twice):
    r = lax.broadcasted_iota(jnp.int32, shape, axis)
    scale = jnp.where(r == 0, 1.0, jnp.where(r <= FEAT, 0.5, 1.0 / (4.0 * math.sqrt(2.0))))
    if twice:
        base = 1 + FEAT
        square = jnp.zeros(shape, jnp.bool_)
        for i in range(FEAT):
            square = square | (r == base)
            base += FEAT - i
        scale = jnp.where((r > FEAT) & ~square, 2.0 * scale, scale)
    one_first = jnp.where(r == 0, 1.0, 0.0)
    one_second = jnp.where(r <= FEAT, 1.0, 0.0)
    return scale, one_first, one_second


NT = (((1,), (1,)), ((), ()))
NN = (((1,), (0,)), ((), ()))


def dot(a, b, dims=NN):
    return lax.dot_general(a, b, dims, preferred_element_type=F32)


def gather_products(flip, core_ref, x_ref, gain_ref, wf_ref, wv_ref, ww_ref):
    squares = feats = values = windowed = 0.0
    for y in range(4):
        at = pl.multiple_of((2 * y + (core_ref[0] + flip) % 2) * 256, 256)
        x = x_ref[y, :, :].astype(F32)
        squares = squares + x * x
        scaled = (x * gain_ref[0:1, pl.ds(at, 256)]).astype(BF)
        feats = feats + dot(scaled, wf_ref[:, pl.ds(at, 256)], NT)
        values = values + dot(scaled, wv_ref[pl.ds(at, 256), :])
        windowed = windowed + dot(scaled, ww_ref[pl.ds(at, 256), :])
    return jnp.sum(squares, axis=1, keepdims=True), feats, values, windowed


def copies_kernel(core_ref, ctx_ref, row_ref, x_ref, out_ref):
    for y in range(4):
        out_ref[y, :, :] = x_ref[...]


def begin_kernel(core_ref, x_ref, gain_ref, wf_ref, wv_ref, ww_ref, held_ref):
    squares, feats, values, windowed = gather_products(0, core_ref, x_ref, gain_ref, wf_ref, wv_ref, ww_ref)
    held_ref[:, :256] = values
    held_ref[:, 256:512] = windowed
    held_ref[:, 512:544] = feats
    held_ref[:, 544:] = jnp.broadcast_to(squares, (squares.shape[0], 96))


def project_kernel(core_ref, x_ref, gain_ref, wf_ref, wv_ref, ww_ref, held_ref, pack_ref, rim_ref, state_ref):
    count = x_ref.shape[1]
    squares, feats, values, windowed = gather_products(1, core_ref, x_ref, gain_ref, wf_ref, wv_ref, ww_ref)
    scale = lax.rsqrt((squares + held_ref[:, 544:545]) * (1.0 / 2048.0) + EPS)
    values = ((values + held_ref[:, :256]) * scale).astype(BF)
    windowed = ((windowed + held_ref[:, 256:512]) * scale).astype(BF)
    feats = ((feats + held_ref[:, 512:544]) * scale).astype(BF)
    rim_ref[:, :128] = windowed[:, 128:]
    rim_ref[:, 128:] = values[:, 128:]
    vlin = values[:, :128]
    pack_ref[:, :128] = windowed[:, :128]
    pack_ref[:, 128:256] = vlin
    pack_ref[:, 256:288] = feats
    pack_ref[:, 288:384] = jnp.zeros((count, 96), BF)
    pack_ref[:, 384:512] = windowed[:, 128:]
    pack_ref[:, 512:] = values[:, 128:]
    first, second = pick((ROWS, FEAT), 0)
    scale, add_first, add_second = weights_of((ROWS, 1), 0, False)
    k = feats[:, FEAT:]
    phi = (dot(first, k, NT) + add_first) * (dot(second, k, NT) + add_second) * scale
    state = dot(phi.astype(BF), vlin)
    for i in range(NEAR):
        state_ref[i, :, :] = state[SHARE * i : SHARE * (i + 1), :].astype(BF)


def inner_kernel(pack_ref, after_ref, num_ref):
    count = pack_ref.shape[0]
    tile = 256
    for t in range(count // tile):
        ql = pack_ref[t * tile : (t + 1) * tile, 256 : 256 + FEAT]
        kl = pack_ref[: (t + 1) * tile, 256 + FEAT : 256 + 2 * FEAT]
        inner = dot(ql, kl, NT)
        width = kl.shape[0]
        row = lax.broadcasted_iota(jnp.int32, (tile, width), 0) + t * tile
        col = lax.broadcasted_iota(jnp.int32, (tile, width), 1)
        series = 1.0 + inner * 0.25 + inner * inner * (1.0 / 32.0)
        weight = jnp.where(row >= col, series, 0.0).astype(BF)
        num_ref[t * tile : (t + 1) * tile, :] = dot(weight, pack_ref[: (t + 1) * tile, 128:256])


def attend_kernel(first_ref, pack_ref, prev_ref, win_ref):
    count = pack_ref.shape[0]
    tile = 256
    no_prev = first_ref[0] == 0
    for t in range(count // tile):
        q = pack_ref[t * tile : (t + 1) * tile, :128]
        old = prev_ref[t * tile :, :]
        new = pack_ref[: (t + 1) * tile, 384:]
        keys = jnp.concatenate([old[:, :128], new[:, :128]], axis=0)
        vals = jnp.concatenate([old[:, 128:], new[:, 128:]], axis=0)
        width = keys.shape[0]
        scores = dot(q, keys, NT) * (1.0 / math.sqrt(128.0))
        at = lax.broadcasted_iota(jnp.int32, (tile, width), 0) + count
        key = lax.broadcasted_iota(jnp.int32, (tile, width), 1)
        least = jnp.where(no_prev, count - t * tile, 0)
        allowed = (key <= at) & (key > at - count) & (key >= least)
        scores = jnp.where(allowed, scores, -1e30)
        lifted = jnp.exp(scores - jnp.max(scores, axis=1, keepdims=True))
        probs = (lifted / jnp.sum(lifted, axis=1, keepdims=True)).astype(BF)
        win_ref[t * tile : (t + 1) * tile, :] = dot(probs, vals).astype(BF)


def linear_kernel(pack_ref, num_ref, prefix_ref, win_ref, mix_ref):
    first, second = pick((FEAT, ROWS), 1)
    scale, add_first, add_second = weights_of((1, ROWS), 1, True)
    q = pack_ref[:, 256 : 256 + FEAT]
    phi = (dot(q, first) + add_first) * (dot(q, second) + add_second) * scale
    prefix = jnp.concatenate([prefix_ref[i, :, :].astype(F32) for i in range(NEAR)], axis=0).astype(BF)
    numerator = num_ref[...] + dot(phi.astype(BF), prefix)
    mean = jnp.mean(numerator * numerator, axis=1, keepdims=True)
    mix_ref[:, :128] = (numerator * lax.rsqrt(mean + EPS)).astype(BF)
    mix_ref[:, 128:] = win_ref[...]


def pick_kernel(core_ref, w_ref, after_ref, out_ref):
    for y in range(4):
        at = pl.multiple_of((2 * y + 1 - core_ref[0]) * 256, 256)
        out_ref[y, :, :] = w_ref[:, pl.ds(at, 256)]


def own_kernel(core_ref, mix_ref, w_ref, sum_ref):
    for y in range(4):
        at = pl.multiple_of((2 * y + core_ref[0]) * 256, 256)
        sum_ref[y, :, :] = dot(mix_ref[...], w_ref[:, pl.ds(at, 256)])


def output_kernel(mix_ref, w_ref, own_ref, sum_ref):
    for y in range(4):
        sum_ref[y, :, :] = (own_ref[y, :, :] + dot(mix_ref[...], w_ref[y, :, :])).astype(BF)


def total_kernel(got_ref, out_ref):
    total = got_ref[0, :, :].astype(F32)
    for i in range(1, NEAR):
        total = total + got_ref[i, :, :].astype(F32)
    total = total.astype(BF)
    for z in range(out_ref.shape[0]):
        out_ref[z, :, :] = total


def prefix_kernel(place_ref, got_ref, totals_ref, out_ref):
    state = jnp.zeros((SHARE, 128), F32)
    for z in range(totals_ref.shape[0] - 1):
        state = state + jnp.where(z < place_ref[0], totals_ref[z, :, :].astype(F32), 0.0)
    for i in range(NEAR):
        out_ref[i, :, :] = state.astype(BF)
        state = state + got_ref[i, :, :].astype(F32)


def shards(tokens, gain, w_feat, w_value, w_window, w_out):
    count = tokens.shape[0]
    head = lax.axis_index("head")
    ctx = lax.axis_index("ctx")
    core = (head % 2).astype(jnp.int32).reshape(1)
    along_y = [[2 * y + c for y in range(4)] for c in range(2)]

    def across(value):
        return lax.ppermute(value, "head", [(h, h ^ 1) for h in range(8)])

    def shape(dims, kind=BF):
        return jax.ShapeDtypeStruct(dims, kind)

    block = ctx.astype(jnp.int32).reshape(1)
    row = (ctx // NEAR).astype(jnp.int32).reshape(1)
    copies = call_with_scalar(copies_kernel, shape((4,) + tokens.shape), 1, 3)(core, block, row, tokens)
    spread = lax.all_to_all(copies, "head", 0, 0, tiled=True, axis_index_groups=along_y)
    other = across(spread)
    weights = (gain.reshape(1, -1), w_feat.T, w_value, w_window)
    held = call_with_scalar(begin_kernel, shape((count, 640), F32), 5)(core, spread, *weights)
    pack, rim, states = call_with_scalar(
        project_kernel, [shape((count, 640)), shape((count, 256)), shape((NEAR, SHARE, 128))], 6
    )(core, other, *weights, held)
    in_x = [[NEAR * z + x for x in range(NEAR)] for z in range(8)]
    in_z = [[NEAR * z + x for z in range(8)] for x in range(NEAR)]
    quarters = lax.all_to_all(states, "ctx", 0, 0, tiled=True, axis_index_groups=in_x)
    rim, quarters = lax.optimization_barrier((rim, quarters))
    totals = lax.all_to_all(
        call(total_kernel, shape((8, SHARE, 128)))(quarters), "ctx", 0, 0, tiled=True, axis_index_groups=in_z
    )
    prev = lax.ppermute(rim, "ctx", [(b, b + 1) for b in range(63)])
    numerator = call(inner_kernel, shape((count, 128), F32))(pack, quarters)
    w_other = across(call_with_scalar(pick_kernel, shape((4, 256, 256)), 2)(core, w_out, quarters))
    win_out = call_with_scalar(attend_kernel, shape((count, 128)), 2)(block, pack, prev)
    sums = call_with_scalar(prefix_kernel, shape((NEAR, SHARE, 128)), 2)(
        row, quarters, totals
    )
    sums, numerator = lax.optimization_barrier((sums, numerator))
    prefix = lax.all_to_all(sums, "ctx", 0, 0, tiled=True, axis_index_groups=in_x)
    mix = call(linear_kernel, shape((count, 256)))(pack, numerator, prefix, win_out)
    own = call_with_scalar(own_kernel, shape((4, count, 256), F32), 2)(core, mix, w_out)
    summed = call(output_kernel, shape((4, count, 256)))(across(mix), w_other, own)
    parts = lax.all_to_all(summed, "head", 0, 0, tiled=True, axis_index_groups=along_y)
    return jnp.sum(parts.astype(F32), axis=0).astype(BF)


def solution(mesh):
    placed = (P("ctx", "head"), P(), P(None, "head"), P(None, "head"), P(None, "head"), P("head", None))
    return jax.shard_map(shards, mesh=mesh, in_specs=placed, out_specs=P("ctx", "head"), check_vma=False)
```

```python
import functools
import math

import jax
import jax.numpy as jnp
from jax import lax
from jax.experimental import pallas as pl
from jax.experimental.pallas import tpu as pltpu
from jax.sharding import PartitionSpec as P

EPS = 1e-05
FEAT = 16
QUARTER = 40
ROWS = 4 * QUARTER
BF = jnp.bfloat16
F32 = jnp.float32
VMEM = 12 * 1024 * 1024


def call(kernel, outs, scratch=()):
    return pl.pallas_call(
        kernel,
        out_shape=outs,
        scratch_shapes=scratch,
        compiler_params=pltpu.CompilerParams(vmem_limit_bytes=VMEM),
    )


def call_with_scalar(kernel, outs, count, scalars=1):
    return pl.pallas_call(
        kernel,
        out_shape=outs,
        in_specs=[pl.BlockSpec(memory_space=pltpu.SMEM)] * scalars + [pl.BlockSpec(memory_space=pltpu.VMEM)] * count,
        compiler_params=pltpu.CompilerParams(vmem_limit_bytes=VMEM),
    )


def pick(shape, axis):
    r = lax.broadcasted_iota(jnp.int32, shape, axis)
    u = lax.broadcasted_iota(jnp.int32, shape, 1 - axis)
    first = (r >= 1) & (r <= FEAT) & (u == r - 1)
    second = jnp.zeros(shape, jnp.bool_)
    base = 1 + FEAT
    for i in range(FEAT):
        width = FEAT - i
        inside = (r >= base) & (r < base + width)
        first = first | (inside & (u == i))
        second = second | (inside & (u == i + r - base))
        base += width
    return first.astype(F32).astype(BF), second.astype(F32).astype(BF)


def weights_of(shape, axis, twice):
    r = lax.broadcasted_iota(jnp.int32, shape, axis)
    scale = jnp.where(r == 0, 1.0, jnp.where(r <= FEAT, 0.5, 1.0 / (4.0 * math.sqrt(2.0))))
    if twice:
        base = 1 + FEAT
        square = jnp.zeros(shape, jnp.bool_)
        for i in range(FEAT):
            square = square | (r == base)
            base += FEAT - i
        scale = jnp.where((r > FEAT) & ~square, 2.0 * scale, scale)
    one_first = jnp.where(r == 0, 1.0, 0.0)
    one_second = jnp.where(r <= FEAT, 1.0, 0.0)
    return scale, one_first, one_second


NT = (((1,), (1,)), ((), ()))
NN = (((1,), (0,)), ((), ()))


def dot(a, b, dims=NN):
    return lax.dot_general(a, b, dims, preferred_element_type=F32)


def gather_products(flip, core_ref, x_ref, gain_ref, wf_ref, wv_ref, ww_ref):
    squares = feats = values = windowed = 0.0
    for y in range(4):
        at = pl.multiple_of((2 * y + (core_ref[0] + flip) % 2) * 256, 256)
        x = x_ref[y, :, :].astype(F32)
        squares = squares + x * x
        scaled = (x * gain_ref[0:1, pl.ds(at, 256)]).astype(BF)
        feats = feats + dot(scaled, wf_ref[:, pl.ds(at, 256)], NT)
        values = values + dot(scaled, wv_ref[pl.ds(at, 256), :])
        windowed = windowed + dot(scaled, ww_ref[pl.ds(at, 256), :])
    return jnp.sum(squares, axis=1, keepdims=True), feats, values, windowed


def copies_kernel(core_ref, ctx_ref, row_ref, x_ref, out_ref):
    for y in range(4):
        out_ref[y, :, :] = x_ref[...]


def begin_kernel(core_ref, x_ref, gain_ref, wf_ref, wv_ref, ww_ref, held_ref):
    squares, feats, values, windowed = gather_products(0, core_ref, x_ref, gain_ref, wf_ref, wv_ref, ww_ref)
    held_ref[:, :256] = values
    held_ref[:, 256:512] = windowed
    held_ref[:, 512:544] = feats
    held_ref[:, 544:] = jnp.broadcast_to(squares, (squares.shape[0], 96))


def project_kernel(core_ref, x_ref, gain_ref, wf_ref, wv_ref, ww_ref, held_ref, pack_ref, rim_hbm, state_ref, rim_ref, sem):
    count = x_ref.shape[1]
    squares, feats, values, windowed = gather_products(1, core_ref, x_ref, gain_ref, wf_ref, wv_ref, ww_ref)
    scale = lax.rsqrt((squares + held_ref[:, 544:545]) * (1.0 / 2048.0) + EPS)
    values = ((values + held_ref[:, :256]) * scale).astype(BF)
    windowed = ((windowed + held_ref[:, 256:512]) * scale).astype(BF)
    feats = ((feats + held_ref[:, 512:544]) * scale).astype(BF)
    rim_ref[:, :128] = windowed[:, 128:]
    rim_ref[:, 128:] = values[:, 128:]
    store = pltpu.make_async_copy(rim_ref, rim_hbm, sem)
    store.start()
    vlin = values[:, :128]
    pack_ref[:, :128] = windowed[:, :128]
    pack_ref[:, 128:256] = vlin
    pack_ref[:, 256:288] = feats
    pack_ref[:, 288:384] = jnp.zeros((count, 96), BF)
    pack_ref[:, 384:512] = windowed[:, 128:]
    pack_ref[:, 512:] = values[:, 128:]
    first, second = pick((ROWS, FEAT), 0)
    scale, add_first, add_second = weights_of((ROWS, 1), 0, False)
    k = feats[:, FEAT:]
    phi = (dot(first, k, NT) + add_first) * (dot(second, k, NT) + add_second) * scale
    state = dot(phi.astype(BF), vlin)
    for i in range(4):
        state_ref[i, :, :] = state[QUARTER * i : QUARTER * (i + 1), :].astype(BF)
    store.wait()


def inner_kernel(pack_ref, after_ref, num_ref):
    count = pack_ref.shape[0]
    tile = 256
    for t in range(count // tile):
        ql = pack_ref[t * tile : (t + 1) * tile, 256 : 256 + FEAT]
        kl = pack_ref[: (t + 1) * tile, 256 + FEAT : 256 + 2 * FEAT]
        inner = dot(ql, kl, NT)
        width = kl.shape[0]
        row = lax.broadcasted_iota(jnp.int32, (tile, width), 0) + t * tile
        col = lax.broadcasted_iota(jnp.int32, (tile, width), 1)
        series = 1.0 + inner * 0.25 + inner * inner * (1.0 / 32.0)
        weight = jnp.where(row >= col, series, 0.0).astype(BF)
        num_ref[t * tile : (t + 1) * tile, :] = dot(weight, pack_ref[: (t + 1) * tile, 128:256])


def attend_kernel(first_ref, pack_ref, prev_ref, win_ref):
    count = pack_ref.shape[0]
    tile = 256
    no_prev = first_ref[0] == 0
    for t in range(count // tile):
        q = pack_ref[t * tile : (t + 1) * tile, :128]
        old = prev_ref[t * tile :, :]
        new = pack_ref[: (t + 1) * tile, 384:]
        keys = jnp.concatenate([old[:, :128], new[:, :128]], axis=0)
        vals = jnp.concatenate([old[:, 128:], new[:, 128:]], axis=0)
        width = keys.shape[0]
        scores = dot(q, keys, NT) * (1.0 / math.sqrt(128.0))
        at = lax.broadcasted_iota(jnp.int32, (tile, width), 0) + count
        key = lax.broadcasted_iota(jnp.int32, (tile, width), 1)
        least = jnp.where(no_prev, count - t * tile, 0)
        allowed = (key <= at) & (key > at - count) & (key >= least)
        scores = jnp.where(allowed, scores, -1e30)
        lifted = jnp.exp(scores - jnp.max(scores, axis=1, keepdims=True))
        probs = (lifted / jnp.sum(lifted, axis=1, keepdims=True)).astype(BF)
        win_ref[t * tile : (t + 1) * tile, :] = dot(probs, vals).astype(BF)


def linear_kernel(pack_ref, num_ref, prefix_ref, win_ref, mix_ref):
    first, second = pick((FEAT, ROWS), 1)
    scale, add_first, add_second = weights_of((1, ROWS), 1, True)
    q = pack_ref[:, 256 : 256 + FEAT]
    phi = (dot(q, first) + add_first) * (dot(q, second) + add_second) * scale
    prefix = jnp.concatenate([prefix_ref[i, :, :].astype(F32) for i in range(4)], axis=0).astype(BF)
    numerator = num_ref[...] + dot(phi.astype(BF), prefix)
    mean = jnp.mean(numerator * numerator, axis=1, keepdims=True)
    mix_ref[:, :128] = (numerator * lax.rsqrt(mean + EPS)).astype(BF)
    mix_ref[:, 128:] = win_ref[...]


def pick_kernel(core_ref, w_ref, after_ref, out_ref):
    for y in range(4):
        at = pl.multiple_of((2 * y + 1 - core_ref[0]) * 256, 256)
        out_ref[y, :, :] = w_ref[:, pl.ds(at, 256)]


def own_kernel(core_ref, mix_ref, w_ref, sum_ref):
    for y in range(4):
        at = pl.multiple_of((2 * y + core_ref[0]) * 256, 256)
        sum_ref[y, :, :] = dot(mix_ref[...], w_ref[:, pl.ds(at, 256)])


def output_kernel(mix_ref, w_ref, own_ref, sum_ref):
    for y in range(4):
        sum_ref[y, :, :] = (own_ref[y, :, :] + dot(mix_ref[...], w_ref[y, :, :])).astype(BF)


def sum_kernel(parts_ref, out_ref):
    total = parts_ref[0, :, :].astype(F32)
    for y in range(1, 4):
        total = total + parts_ref[y, :, :].astype(F32)
    out_ref[...] = total.astype(BF)


def total_kernel(got_ref, out_ref):
    total = got_ref[0, :, :].astype(F32)
    for i in range(1, 4):
        total = total + got_ref[i, :, :].astype(F32)
    total = total.astype(BF)
    for z in range(16):
        out_ref[z, :, :] = total


def prefix_kernel(place_ref, got_ref, totals_ref, out_ref):
    state = jnp.zeros((QUARTER, 128), F32)
    for z in range(15):
        state = state + jnp.where(z < place_ref[0], totals_ref[z, :, :].astype(F32), 0.0)
    for i in range(4):
        out_ref[i, :, :] = state.astype(BF)
        state = state + got_ref[i, :, :].astype(F32)


def shards(tokens, gain, w_feat, w_value, w_window, w_out):
    count = tokens.shape[0]
    head = lax.axis_index("head")
    ctx = lax.axis_index("ctx")
    core = (head % 2).astype(jnp.int32).reshape(1)
    along_y = [[2 * y + c for y in range(4)] for c in range(2)]

    def across(value):
        return lax.ppermute(value, "head", [(h, h ^ 1) for h in range(8)])

    def shape(dims, kind=BF):
        return jax.ShapeDtypeStruct(dims, kind)

    block = ctx.astype(jnp.int32).reshape(1)
    row = (ctx // 4).astype(jnp.int32).reshape(1)
    copies = call_with_scalar(copies_kernel, shape((4,) + tokens.shape), 1, 3)(core, block, row, tokens)
    spread = lax.all_to_all(copies, "head", 0, 0, tiled=True, axis_index_groups=along_y)
    other = across(spread)
    weights = (gain.reshape(1, -1), w_feat.T, w_value, w_window)
    held = call_with_scalar(begin_kernel, shape((count, 640), F32), 5)(core, spread, *weights)
    vmem, hbm = pl.BlockSpec(memory_space=pltpu.VMEM), pl.BlockSpec(memory_space=pltpu.HBM)
    pack, rim, states = pl.pallas_call(
        project_kernel,
        out_shape=[shape((count, 640)), shape((count, 256)), shape((4, QUARTER, 128))],
        in_specs=[pl.BlockSpec(memory_space=pltpu.SMEM)] + [vmem] * 6,
        out_specs=[vmem, hbm, vmem],
        scratch_shapes=[pltpu.VMEM((count, 256), BF), pltpu.SemaphoreType.DMA],
        compiler_params=pltpu.CompilerParams(vmem_limit_bytes=VMEM),
    )(core, other, *weights, held)
    in_x = [[4 * z + x for x in range(4)] for z in range(16)]
    in_z = [[4 * z + x for z in range(16)] for x in range(4)]
    quarters = lax.all_to_all(states, "ctx", 0, 0, tiled=True, axis_index_groups=in_x)
    rim, quarters = lax.optimization_barrier((rim, quarters))
    totals = lax.all_to_all(
        call(total_kernel, shape((16, QUARTER, 128)))(quarters), "ctx", 0, 0, tiled=True, axis_index_groups=in_z
    )
    prev = lax.ppermute(rim, "ctx", [(b, b + 1) for b in range(63)])
    numerator = call(inner_kernel, shape((count, 128), F32))(pack, quarters)
    w_other = across(call_with_scalar(pick_kernel, shape((4, 256, 256)), 2)(core, w_out, quarters))
    win_out = call_with_scalar(attend_kernel, shape((count, 128)), 2)(block, pack, prev)
    sums = call_with_scalar(prefix_kernel, shape((4, QUARTER, 128)), 2)(
        row, quarters, totals
    )
    sums, numerator = lax.optimization_barrier((sums, numerator))
    prefix = lax.all_to_all(sums, "ctx", 0, 0, tiled=True, axis_index_groups=in_x)
    mix = call(linear_kernel, shape((count, 256)))(pack, numerator, prefix, win_out)
    own = call_with_scalar(own_kernel, shape((4, count, 256), F32), 2)(core, mix, w_out)
    summed = call(output_kernel, shape((4, count, 256)))(across(mix), w_other, own)
    parts = lax.all_to_all(summed, "head", 0, 0, tiled=True, axis_index_groups=along_y)
    return call(sum_kernel, shape((count, 256)))(parts)


def solution(mesh):
    placed = (P("ctx", "head"), P(), P(None, "head"), P(None, "head"), P(None, "head"), P("head", None))
    return jax.shard_map(shards, mesh=mesh, in_specs=placed, out_specs=P("ctx", "head"), check_vma=False)
```

```python
import functools
import math

import jax
import jax.numpy as jnp
from jax import lax
from jax.experimental import pallas as pl
from jax.experimental.pallas import tpu as pltpu
from jax.sharding import PartitionSpec as P

EPS = 1e-05
FEAT = 16
QUARTER = 40
ROWS = 4 * QUARTER
BF = jnp.bfloat16
F32 = jnp.float32
VMEM = 12 * 1024 * 1024


def call(kernel, outs, scratch=()):
    return pl.pallas_call(
        kernel,
        out_shape=outs,
        scratch_shapes=scratch,
        compiler_params=pltpu.CompilerParams(vmem_limit_bytes=VMEM),
    )


def call_with_scalar(kernel, outs, count, scalars=1):
    return pl.pallas_call(
        kernel,
        out_shape=outs,
        in_specs=[pl.BlockSpec(memory_space=pltpu.SMEM)] * scalars + [pl.BlockSpec(memory_space=pltpu.VMEM)] * count,
        compiler_params=pltpu.CompilerParams(vmem_limit_bytes=VMEM),
    )


def pick(shape, axis):
    r = lax.broadcasted_iota(jnp.int32, shape, axis)
    u = lax.broadcasted_iota(jnp.int32, shape, 1 - axis)
    first = (r >= 1) & (r <= FEAT) & (u == r - 1)
    second = jnp.zeros(shape, jnp.bool_)
    base = 1 + FEAT
    for i in range(FEAT):
        width = FEAT - i
        inside = (r >= base) & (r < base + width)
        first = first | (inside & (u == i))
        second = second | (inside & (u == i + r - base))
        base += width
    return first.astype(F32).astype(BF), second.astype(F32).astype(BF)


def weights_of(shape, axis, twice):
    r = lax.broadcasted_iota(jnp.int32, shape, axis)
    scale = jnp.where(r == 0, 1.0, jnp.where(r <= FEAT, 0.5, 1.0 / (4.0 * math.sqrt(2.0))))
    if twice:
        base = 1 + FEAT
        square = jnp.zeros(shape, jnp.bool_)
        for i in range(FEAT):
            square = square | (r == base)
            base += FEAT - i
        scale = jnp.where((r > FEAT) & ~square, 2.0 * scale, scale)
    one_first = jnp.where(r == 0, 1.0, 0.0)
    one_second = jnp.where(r <= FEAT, 1.0, 0.0)
    return scale, one_first, one_second


NT = (((1,), (1,)), ((), ()))
NN = (((1,), (0,)), ((), ()))


def dot(a, b, dims=NN):
    return lax.dot_general(a, b, dims, preferred_element_type=F32)


def gather_products(flip, core_ref, x_ref, gain_ref, wf_ref, wv_ref, ww_ref):
    squares = feats = values = windowed = 0.0
    for y in range(4):
        at = pl.multiple_of((2 * y + (core_ref[0] + flip) % 2) * 256, 256)
        x = x_ref[y, :, :].astype(F32)
        squares = squares + x * x
        scaled = (x * gain_ref[0:1, pl.ds(at, 256)]).astype(BF)
        feats = feats + dot(scaled, wf_ref[:, pl.ds(at, 256)], NT)
        values = values + dot(scaled, wv_ref[pl.ds(at, 256), :])
        windowed = windowed + dot(scaled, ww_ref[pl.ds(at, 256), :])
    return jnp.sum(squares, axis=1, keepdims=True), feats, values, windowed


def copies_kernel(core_ref, ctx_ref, row_ref, x_ref, out_ref):
    for y in range(4):
        out_ref[y, :, :] = x_ref[...]


def begin_kernel(core_ref, x_ref, gain_ref, wf_ref, wv_ref, ww_ref, held_ref):
    squares, feats, values, windowed = gather_products(0, core_ref, x_ref, gain_ref, wf_ref, wv_ref, ww_ref)
    held_ref[:, :256] = values
    held_ref[:, 256:512] = windowed
    held_ref[:, 512:544] = feats
    held_ref[:, 544:] = jnp.broadcast_to(squares, (squares.shape[0], 96))


def project_kernel(core_ref, x_ref, gain_ref, wf_ref, wv_ref, ww_ref, held_ref, pack_ref, rim_ref, state_ref):
    count = x_ref.shape[1]
    squares, feats, values, windowed = gather_products(1, core_ref, x_ref, gain_ref, wf_ref, wv_ref, ww_ref)
    scale = lax.rsqrt((squares + held_ref[:, 544:545]) * (1.0 / 2048.0) + EPS)
    values = ((values + held_ref[:, :256]) * scale).astype(BF)
    windowed = ((windowed + held_ref[:, 256:512]) * scale).astype(BF)
    feats = ((feats + held_ref[:, 512:544]) * scale).astype(BF)
    rim_ref[:, :128] = windowed[:, 128:]
    rim_ref[:, 128:] = values[:, 128:]
    vlin = values[:, :128]
    pack_ref[:, :128] = windowed[:, :128]
    pack_ref[:, 128:256] = vlin
    pack_ref[:, 256:288] = feats
    pack_ref[:, 288:384] = jnp.zeros((count, 96), BF)
    pack_ref[:, 384:512] = windowed[:, 128:]
    pack_ref[:, 512:] = values[:, 128:]
    first, second = pick((ROWS, FEAT), 0)
    scale, add_first, add_second = weights_of((ROWS, 1), 0, False)
    k = feats[:, FEAT:]
    phi = (dot(first, k, NT) + add_first) * (dot(second, k, NT) + add_second) * scale
    state = dot(phi.astype(BF), vlin)
    for i in range(4):
        state_ref[i, :, :] = state[QUARTER * i : QUARTER * (i + 1), :].astype(BF)


def inner_kernel(pack_ref, after_ref, num_ref):
    count = pack_ref.shape[0]
    tile = 256
    for t in range(count // tile):
        ql = pack_ref[t * tile : (t + 1) * tile, 256 : 256 + FEAT]
        kl = pack_ref[: (t + 1) * tile, 256 + FEAT : 256 + 2 * FEAT]
        inner = dot(ql, kl, NT)
        width = kl.shape[0]
        row = lax.broadcasted_iota(jnp.int32, (tile, width), 0) + t * tile
        col = lax.broadcasted_iota(jnp.int32, (tile, width), 1)
        series = 1.0 + inner * 0.25 + inner * inner * (1.0 / 32.0)
        weight = jnp.where(row >= col, series, 0.0).astype(BF)
        num_ref[t * tile : (t + 1) * tile, :] = dot(weight, pack_ref[: (t + 1) * tile, 128:256])


def attend_kernel(first_ref, pack_ref, prev_ref, win_ref):
    count = pack_ref.shape[0]
    tile = 256
    no_prev = first_ref[0] == 0
    for t in range(count // tile):
        q = pack_ref[t * tile : (t + 1) * tile, :128]
        old = prev_ref[t * tile :, :]
        new = pack_ref[: (t + 1) * tile, 384:]
        keys = jnp.concatenate([old[:, :128], new[:, :128]], axis=0)
        vals = jnp.concatenate([old[:, 128:], new[:, 128:]], axis=0)
        width = keys.shape[0]
        scores = dot(q, keys, NT) * (1.0 / math.sqrt(128.0))
        at = lax.broadcasted_iota(jnp.int32, (tile, width), 0) + count
        key = lax.broadcasted_iota(jnp.int32, (tile, width), 1)
        least = jnp.where(no_prev, count - t * tile, 0)
        allowed = (key <= at) & (key > at - count) & (key >= least)
        scores = jnp.where(allowed, scores, -1e30)
        lifted = jnp.exp(scores - jnp.max(scores, axis=1, keepdims=True))
        probs = (lifted / jnp.sum(lifted, axis=1, keepdims=True)).astype(BF)
        win_ref[t * tile : (t + 1) * tile, :] = dot(probs, vals).astype(BF)


def linear_kernel(pack_ref, num_ref, prefix_ref, after_ref, lin_ref):
    first, second = pick((FEAT, ROWS), 1)
    scale, add_first, add_second = weights_of((1, ROWS), 1, True)
    q = pack_ref[:, 256 : 256 + FEAT]
    phi = (dot(q, first) + add_first) * (dot(q, second) + add_second) * scale
    prefix = jnp.concatenate([prefix_ref[i, :, :].astype(F32) for i in range(4)], axis=0).astype(BF)
    numerator = num_ref[...] + dot(phi.astype(BF), prefix)
    mean = jnp.mean(numerator * numerator, axis=1, keepdims=True)
    lin_ref[...] = (numerator * lax.rsqrt(mean + EPS)).astype(BF)


def pick_kernel(core_ref, w_ref, after_ref, out_ref):
    for y in range(4):
        at = pl.multiple_of((2 * y + 1 - core_ref[0]) * 256, 256)
        out_ref[y, :, :] = w_ref[:, pl.ds(at, 256)]


def own_kernel(core_ref, lin_ref, win_ref, w_ref, win2_ref, w2_ref, sum_ref):
    for y in range(4):
        columns = pl.ds(pl.multiple_of((2 * y + core_ref[0]) * 256, 256), 256)
        total = dot(lin_ref[...], w_ref[:128, columns]) + dot(win_ref[...], w_ref[128:, columns])
        sum_ref[y, :, :] = total + dot(win2_ref[...], w2_ref[y, 128:, :])


def output_kernel(lin_ref, w_ref, own_ref, sum_ref):
    for y in range(4):
        sum_ref[y, :, :] = (own_ref[y, :, :] + dot(lin_ref[...], w_ref[y, :128, :])).astype(BF)


def total_kernel(got_ref, out_ref):
    total = got_ref[0, :, :].astype(F32)
    for i in range(1, 4):
        total = total + got_ref[i, :, :].astype(F32)
    total = total.astype(BF)
    for z in range(16):
        out_ref[z, :, :] = total


def prefix_kernel(place_ref, got_ref, totals_ref, out_ref):
    state = jnp.zeros((QUARTER, 128), F32)
    for z in range(15):
        state = state + jnp.where(z < place_ref[0], totals_ref[z, :, :].astype(F32), 0.0)
    for i in range(4):
        out_ref[i, :, :] = state.astype(BF)
        state = state + got_ref[i, :, :].astype(F32)


def shards(tokens, gain, w_feat, w_value, w_window, w_out):
    count = tokens.shape[0]
    head = lax.axis_index("head")
    ctx = lax.axis_index("ctx")
    core = (head % 2).astype(jnp.int32).reshape(1)
    along_y = [[2 * y + c for y in range(4)] for c in range(2)]

    def across(value):
        return lax.ppermute(value, "head", [(h, h ^ 1) for h in range(8)])

    def shape(dims, kind=BF):
        return jax.ShapeDtypeStruct(dims, kind)

    block = ctx.astype(jnp.int32).reshape(1)
    row = (ctx // 4).astype(jnp.int32).reshape(1)
    copies = call_with_scalar(copies_kernel, shape((4,) + tokens.shape), 1, 3)(core, block, row, tokens)
    spread = lax.all_to_all(copies, "head", 0, 0, tiled=True, axis_index_groups=along_y)
    other = across(spread)
    weights = (gain.reshape(1, -1), w_feat.T, w_value, w_window)
    held = call_with_scalar(begin_kernel, shape((count, 640), F32), 5)(core, spread, *weights)
    pack, rim, states = call_with_scalar(
        project_kernel, [shape((count, 640)), shape((count, 256)), shape((4, QUARTER, 128))], 6
    )(core, other, *weights, held)
    in_x = [[4 * z + x for x in range(4)] for z in range(16)]
    in_z = [[4 * z + x for z in range(16)] for x in range(4)]
    quarters = lax.all_to_all(states, "ctx", 0, 0, tiled=True, axis_index_groups=in_x)
    rim, quarters = lax.optimization_barrier((rim, quarters))
    totals = lax.all_to_all(
        call(total_kernel, shape((16, QUARTER, 128)))(quarters), "ctx", 0, 0, tiled=True, axis_index_groups=in_z
    )
    prev = lax.ppermute(rim, "ctx", [(b, b + 1) for b in range(63)])
    numerator = call(inner_kernel, shape((count, 128), F32))(pack, quarters)
    w_other = across(call_with_scalar(pick_kernel, shape((4, 256, 256)), 2)(core, w_out, quarters))
    win_out = call_with_scalar(attend_kernel, shape((count, 128)), 2)(block, pack, prev)
    sums = call_with_scalar(prefix_kernel, shape((4, QUARTER, 128)), 2)(
        row, quarters, totals
    )
    sums, numerator = lax.optimization_barrier((sums, numerator))
    prefix = lax.all_to_all(sums, "ctx", 0, 0, tiled=True, axis_index_groups=in_x)
    win_other = across(win_out)
    lin = call(linear_kernel, shape((count, 128)))(pack, numerator, prefix, win_other)
    own = call_with_scalar(own_kernel, shape((4, count, 256), F32), 5)(core, lin, win_out, w_out, win_other, w_other)
    summed = call(output_kernel, shape((4, count, 256)))(across(lin), w_other, own)
    parts = lax.all_to_all(summed, "head", 0, 0, tiled=True, axis_index_groups=along_y)
    return jnp.sum(parts.astype(F32), axis=0).astype(BF)


def solution(mesh):
    placed = (P("ctx", "head"), P(), P(None, "head"), P(None, "head"), P(None, "head"), P("head", None))
    return jax.shard_map(shards, mesh=mesh, in_specs=placed, out_specs=P("ctx", "head"), check_vma=False)
```
